32 devices in a mesh: dp: 16 (over z, y, core), tensor: 2 (over x).
Axes of the slice: x: 2, y: 2, z: 4, core: 2. Of those that a mesh axis runs over, the one named last changes fastest.
Arguments:
- features: bfloat16 [32, 1024, 768], P(('dp', 'tensor')), may hold values from -6 to 6
- lengths: int32 [32], P(('dp', 'tensor')), may hold values from 512 to 1024, as said below
- span_starts: int32 [32, 8], P(('dp', 'tensor')), may hold values from 0 to 1014, as said below
- buckets: int32 [2047], replicated, may hold values from 0 to 319
- cotangent: bfloat16 [32, 1024, 768], P(('dp', 'tensor')), may hold values from -6 to 6
- qkv_w: float32 [3, 768, 768], P(None, 'dp'), may hold values from -0.21875 to 0.21875
- qkv_m: float32 [3, 768, 768], P(None, 'dp'), may hold values from -0.00061035156 to 0.00061035156
- qkv_v: float32 [3, 768, 768], P(None, 'dp'), may hold values from 1.409991e-09 to 2.2559856e-08
- out_w: float32 [768, 768], P('dp'), may hold values from -3 to 3
- out_m: float32 [768, 768], P('dp'), may hold values from -7.6293945e-05 to 7.6293945e-05
- out_v: float32 [768, 768], P('dp'), may hold values from 2.819982e-11 to 4.229973e-10
- ffn_in: float32 [769, 3072], P(None, ('dp', 'tensor')), may hold values from -0.21875 to 0.21875
- ffn_in_m: float32 [769, 3072], P(None, ('dp', 'tensor')), may hold values from -0.00061035156 to 0.00061035156
- ffn_in_v: float32 [769, 3072], P(None, ('dp', 'tensor')), may hold values from 1.409991e-09 to 2.2559856e-08
- ffn_out: float32 [3072, 768], P(('dp', 'tensor')), may hold values from -0.109375 to 0.109375
- ffn_out_m: float32 [3072, 768], P(('dp', 'tensor')), may hold values from -0.00061035156 to 0.00061035156
- ffn_out_v: float32 [3072, 768], P(('dp', 'tensor')), may hold values from 1.409991e-09 to 2.2559856e-08
- small_params: float32 [9, 768], replicated, may hold values from -4 to 4, as said below
- small_m: float32 [9, 768], replicated, may hold values from -0.0012207031 to 0.0012207031
- small_v: float32 [9, 768], replicated, may hold values from 5.639964e-09 to 9.0239425e-08
- pos_table: float32 [321, 12], replicated, may hold values from -4 to 4
- pos_m: float32 [321, 12], replicated, may hold values from -0.0012207031 to 0.0012207031
- pos_v: float32 [321, 12], replicated, may hold values from 5.639964e-09 to 9.0239425e-08
- gate_proj: float32 [65, 8], replicated, may hold values from -0.75 to 0.75
- gate_m: float32 [65, 8], replicated, may hold values from -0.0012207031 to 0.0012207031
- gate_v: float32 [65, 8], replicated, may hold values from 5.639964e-09 to 9.0239425e-08
- step_count: int32 [1], replicated, may hold values from 1 to 4
Outputs:
- layer_out: float32 [32, 1024, 768], P(('dp', 'tensor'))
- feature_grad: float32 [32, 1024, 768], P(('dp', 'tensor'))
- grad_norm: float32 [1], replicated
- qkv_new: float32 [3, 768, 768], P(None, 'dp')
- qkv_moment: float32 [3, 768, 768], P(None, 'dp')
- qkv_second: float32 [3, 768, 768], P(None, 'dp')
- qkv_copy: bfloat16 [3, 768, 768], P(None, 'dp')
- out_new: float32 [768, 768], P('dp')
- out_moment: float32 [768, 768], P('dp')
- out_second: float32 [768, 768], P('dp')
- out_copy: bfloat16 [768, 768], P('dp')
- ffn_in_new: float32 [769, 3072], P(None, ('dp', 'tensor'))
- ffn_in_moment: float32 [769, 3072], P(None, ('dp', 'tensor'))
- ffn_in_second: float32 [769, 3072], P(None, ('dp', 'tensor'))
- ffn_in_copy: bfloat16 [769, 3072], P(None, ('dp', 'tensor'))
- ffn_out_new: float32 [3072, 768], P(('dp', 'tensor'))
- ffn_out_moment: float32 [3072, 768], P(('dp', 'tensor'))
- ffn_out_second: float32 [3072, 768], P(('dp', 'tensor'))
- ffn_out_copy: bfloat16 [3072, 768], P(('dp', 'tensor'))
- small_grad: float32 [9, 768], replicated
- small_new: float32 [9, 768], replicated
- small_moment: float32 [9, 768], replicated
- small_second: float32 [9, 768], replicated
- pos_new: float32 [321, 12], replicated
- pos_moment: float32 [321, 12], replicated
- pos_second: float32 [321, 12], replicated
- gate_new: float32 [65, 8], replicated
- gate_moment: float32 [65, 8], replicated
- gate_second: float32 [65, 8], replicated
The draws below stay inside these ranges and needn't reach their ends.
Inputs may be any that keep to these rules, and one draw needn't show every extreme that they name: `lengths`: every length is at least half of 1024; the first utterance is full in every draw. `span_starts`: each start is at most its utterance's length minus 10; spans may intersect. buckets[o] is the bucket of relative offset o - 1023. `small_params`: gains (rows 3 and 5) lie between 0.7 and 1.3.
All inputs are finite; a program needn't handle non-finite values.
Results may differ from the reference program's by a relative error of at most 0.02.
Values may be sent and summed in bfloat16 or wider, within the bound.
No kernel may reach another device: no remote copies, remote signals or barrier semaphores. Data moves between devices by JAX's collectives and lax.ppermute only.
A program may use at most 320 MiB of HBM per device.

```python
import math
from functools import partial
import jax
import jax.numpy as jnp
from jax import lax

D = 768
H = 12
HD = 64
FF = 3072
NB = 320
L = 1024
SPAN = 10
NSPAN = 8
UTTS = 32
PARAMS = 7092244


def common_spans(key):
    base_key = jax.random.fold_in(key, 11)
    key_len, key_pos = jax.random.split(base_key)
    lengths = jax.random.randint(key_len, (UTTS,), L // 2, L + 1).at[0].set(L)
    fraction = jax.random.randint(key_pos, (UTTS, NSPAN), 0, 1048576)
    starts = fraction * (lengths[:, None] - SPAN + 1) // 1048576
    return (lengths.astype(jnp.int32), starts.astype(jnp.int32))


def draw_lengths(key, part):
    return common_spans(key)[0]


def draw_span_starts(key, part):
    return common_spans(key)[1]


def draw_small_params(key, part):
    key_a, key_b, key_c = jax.random.split(jax.random.fold_in(key, 5), 3)
    shifts = 0.1 * jax.random.truncated_normal(key_a, -4.0, 4.0, (9, D))
    gain_values = 1.0 + jax.random.uniform(key_b, (9, D), minval=-0.3, maxval=0.3)
    mask_values = jax.random.truncated_normal(key_c, -4.0, 4.0, (9, D))
    row_index = jnp.arange(9)[:, None]
    is_gain = (row_index == 3) | (row_index == 5)
    return jnp.where(is_gain, gain_values, jnp.where(row_index == 8, mask_values, shifts)).astype(jnp.float32)


def set_ends(values, key, least, top_value):
    longest = values.shape.index(max(values.shape))
    spots = []
    for shift in (0, 1):
        where = [jax.random.randint(jax.random.fold_in(key, axis), (), 0, length) for axis, length in enumerate(values.shape)]
        where[longest] = (where[longest] + shift) % values.shape[longest]
        spots.append(tuple(where))
    return values.at[spots[0]].set(least).at[spots[1]].set(top_value)


def block_levels(own_key, dims, shards, low, high):
    def one(axis_at, parts):
        draws = jax.random.uniform(jax.random.fold_in(jax.random.fold_in(own_key, 6), axis_at), (parts,), jnp.float32, low / len(shards), high / len(shards))
        return jnp.repeat(jnp.exp(draws), dims[axis_at] // parts).reshape((-1,) + (1,) * (len(dims) - axis_at - 1))

    level = one(*shards[0])
    for cut in shards[1:]:
        level = level * one(*cut)
    return level


def bell_draw(own_key, shape, scale, reach, cuts=(), kind=jnp.bfloat16):
    result = jax.random.normal(own_key, shape, jnp.float32) * scale
    if len(cuts) > 0:
        result = block_levels(own_key, shape, cuts, -0.22, 0.18) * result
    return jnp.clip(result, min=-reach, max=reach).astype(kind)


def setup_inputs(seed: int = 0) -> dict:
    splits = jax.random.split(jax.random.key(seed), 28)
    return {
        "features": bell_draw(splits[0], (UTTS, L, D), 1.0, 6.0, ((0, 32),)),
        "lengths": draw_lengths(jax.random.fold_in(splits[27], 71), 0),
        "span_starts": draw_span_starts(jax.random.fold_in(splits[27], 71), 0),
        "buckets": set_ends(jax.random.randint(splits[3], (2 * L - 1,), 0, NB), jax.random.fold_in(splits[3], 1), 0, NB - 1).astype(jnp.int32),
        "cotangent": bell_draw(splits[4], (UTTS, L, D), 1.0, 6.0, ((0, 32),)),
        "qkv_w": bell_draw(splits[5], (3, D, D), D ** -0.5, 0.21875, ((1, 16),), jnp.float32),
        "qkv_m": bell_draw(splits[6], (3, D, D), (0.11 * PARAMS ** -0.5), 0.00061035156, ((1, 16),), jnp.float32),
        "qkv_v": jnp.clip(jnp.exp(math.log(2.255985620536194e-08) - 2.7725887 * jax.random.uniform(splits[7], (3, D, D), jnp.float32) ** block_levels(splits[7], (3, D, D), ((1, 16),), -0.2, 0.2)), 1.4099910128351212e-09, 2.255985620536194e-08),
        "out_w": bell_draw(splits[8], (D, D), 4 ** -0.5, 3.0, ((0, 16),), jnp.float32),
        "out_m": bell_draw(splits[9], (D, D), (0.015 * PARAMS ** -0.5), 7.62939453125e-05, ((0, 16),), jnp.float32),
        "out_v": jnp.clip(jnp.exp(math.log(4.2299730385053635e-10) - 2.7080502 * jax.random.uniform(splits[10], (D, D), jnp.float32) ** block_levels(splits[10], (D, D), ((0, 16),), -0.2, 0.2)), 2.8199819215868338e-11, 4.2299730385053635e-10),
        "ffn_in": bell_draw(splits[11], (D + 1, FF), D ** -0.5, 0.21875, ((1, 32),), jnp.float32),
        "ffn_in_m": bell_draw(splits[12], (D + 1, FF), (0.11 * PARAMS ** -0.5), 0.00061035156, ((1, 32),), jnp.float32),
        "ffn_in_v": jnp.clip(jnp.exp(math.log(2.255985620536194e-08) - 2.7725887 * jax.random.uniform(splits[13], (D + 1, FF), jnp.float32) ** block_levels(splits[13], (D + 1, FF), ((1, 32),), -0.2, 0.2)), 1.4099910128351212e-09, 2.255985620536194e-08),
        "ffn_out": bell_draw(splits[14], (FF, D), FF ** -0.5, 0.109375, ((0, 32),), jnp.float32),
        "ffn_out_m": bell_draw(splits[15], (FF, D), (0.11 * PARAMS ** -0.5), 0.00061035156, ((0, 32),), jnp.float32),
        "ffn_out_v": jnp.clip(jnp.exp(math.log(2.255985620536194e-08) - 2.7725887 * jax.random.uniform(splits[16], (FF, D), jnp.float32) ** block_levels(splits[16], (FF, D), ((0, 32),), -0.2, 0.2)), 1.4099910128351212e-09, 2.255985620536194e-08),
        "small_params": draw_small_params(jax.random.fold_in(splits[27], 71), 0),
        "small_m": bell_draw(splits[18], (9, D), (0.22 * PARAMS ** -0.5), 0.0012207031, (), jnp.float32),
        "small_v": jnp.clip(jnp.exp(jax.random.uniform(splits[19], (9, D), jnp.float32, math.log(5.639964051340485e-09), math.log(9.023942482144776e-08))), 5.639964051340485e-09, 9.023942482144776e-08),
        "pos_table": bell_draw(splits[20], (NB + 1, H), 1.0, 4.0, (), jnp.float32),
        "pos_m": bell_draw(splits[21], (NB + 1, H), (0.22 * PARAMS ** -0.5), 0.0012207031, (), jnp.float32),
        "pos_v": jnp.clip(jnp.exp(jax.random.uniform(splits[22], (NB + 1, H), jnp.float32, math.log(5.639964051340485e-09), math.log(9.023942482144776e-08))), 5.639964051340485e-09, 9.023942482144776e-08),
        "gate_proj": bell_draw(splits[23], (HD + 1, 8), HD ** -0.5, 0.75, (), jnp.float32),
        "gate_m": bell_draw(splits[24], (HD + 1, 8), (0.22 * PARAMS ** -0.5), 0.0012207031, (), jnp.float32),
        "gate_v": jnp.clip(jnp.exp(jax.random.uniform(splits[25], (HD + 1, 8), jnp.float32, math.log(5.639964051340485e-09), math.log(9.023942482144776e-08))), 5.639964051340485e-09, 9.023942482144776e-08),
        "step_count": jax.random.randint(splits[26], (1,), 1, 5).astype(jnp.int32),
    }


PRECISE = lax.Precision.HIGHEST
CLIP_NORM = 1.0
BETA_ONE = 0.9
BETA_TWO = 0.98
ADAM_EPS = 1e-08
DECAY_RATE = 0.01
NORM_EPS = 1e-05
NEG_BIG = -1e+30

@jax.custom_vjp
def low(v):
    return lax.optimization_barrier(v.astype(jnp.bfloat16)).astype(jnp.float32)

@jax.custom_vjp
def low_back(v):
    return v

def low_keep(v):
    return (low(v), None)

def low_pass(kept, grad):
    return (grad,)

def back_keep(v):
    return (v, None)

def back_low(kept, grad):
    return (low(grad),)
low.defvjp(low_keep, low_pass)
low_back.defvjp(back_keep, back_low)

def round_both(value_in):
    return low(low_back(value_in))

def matmul(left, right):
    return jnp.dot(left, right, precision=PRECISE, preferred_element_type=jnp.float32)

def layer_norm(rows_in, gain_row, shift_row):
    row_mean = lax.optimization_barrier(jnp.mean(rows_in, axis=-1, keepdims=True))
    centred = rows_in - row_mean
    inv_std = lax.rsqrt(lax.optimization_barrier(jnp.mean(centred * centred, axis=-1, keepdims=True)) + NORM_EPS)
    return centred * inv_std * gain_row + shift_row

def gate_of(heads_in, gate_proj, gate_const):
    logits = jnp.einsum('lhd,de->lhe', heads_in, gate_proj[:-1], precision=PRECISE) + gate_proj[-1]
    gate_one = jax.nn.sigmoid(lax.optimization_barrier(jnp.sum(logits[..., :4], axis=-1)))
    gate_two = jax.nn.sigmoid(lax.optimization_barrier(jnp.sum(logits[..., 4:], axis=-1)))
    return gate_one * (gate_two * gate_const - 1.0) + 2.0

def layer_forward(frames_in, qkv_w, out_w, ffn_in, ffn_out, small_params, pos_table, gate_proj, length, starts, buckets):
    positions = jnp.arange(L, dtype=jnp.int32)
    inside = (positions[:, None] >= starts[None, :]) & (positions[:, None] < starts[None, :] + SPAN)
    masked = jnp.any(inside, axis=1)
    mixed_in = jnp.where(masked[:, None], small_params[8][None, :], frames_in)
    rounded = low(mixed_in)
    w_qkv = low(qkv_w)
    w_attn = low(out_w)
    w_first = low(ffn_in)
    w_second = low(ffn_out)
    query_scale = HD ** (-0.5)
    queries = round_both((matmul(rounded, w_qkv[0]) + small_params[0]) * query_scale).reshape(L, H, HD)
    keys_all = round_both(matmul(rounded, w_qkv[1])).reshape(L, H, HD)
    values_all = round_both(matmul(rounded, w_qkv[2]) + small_params[1]).reshape(L, H, HD)
    gate_vals = gate_of(rounded.reshape(L, H, HD), gate_proj, pos_table[NB])
    offsets = pos_table[:NB][buckets]
    offset_index = positions[None, :] - positions[:, None] + L - 1
    relative = jnp.transpose(offsets[offset_index], (2, 0, 1))
    scores = jnp.einsum('ihd,jhd->hij', queries, keys_all, precision=PRECISE) + jnp.transpose(gate_vals)[:, :, None] * relative
    scores = low_back(jnp.where((positions < length)[None, None, :], scores, NEG_BIG))
    prob_vals = jax.nn.softmax(scores, axis=-1)
    context = round_both(jnp.einsum('hij,jhd->ihd', low(prob_vals), values_all, precision=PRECISE).reshape(L, D))
    attention = low_back(matmul(context, w_attn) + small_params[2])
    first_out = layer_norm(mixed_in + attention, small_params[3], small_params[4])
    hidden = low_back(matmul(low(first_out), w_first[:D]) + w_first[D])
    branch = low_back(matmul(low(jax.nn.gelu(hidden, approximate=False)), w_second) + small_params[7])
    return layer_norm(first_out + branch, small_params[5], small_params[6])

def adam_step(weight, grad_in, moment, second, clip_factor, rate_in, count_in):
    scaled = grad_in * clip_factor
    new_moment = BETA_ONE * moment + (1.0 - BETA_ONE) * scaled
    new_second = BETA_TWO * second + (1.0 - BETA_TWO) * scaled * scaled
    first_fix = 1.0 - BETA_ONE ** count_in
    second_fix = 1.0 - BETA_TWO ** count_in
    update = new_moment / first_fix / (jnp.sqrt(new_second / second_fix) + ADAM_EPS)
    return (weight - rate_in * (update + DECAY_RATE * weight), new_moment, new_second)

def reference(features, lengths, span_starts, buckets, cotangent, qkv_w, qkv_m, qkv_v, out_w, out_m, out_v, ffn_in, ffn_in_m, ffn_in_v, ffn_out, ffn_out_m, ffn_out_v, small_params, small_m, small_v, pos_table, pos_m, pos_v, gate_proj, gate_m, gate_v, step_count):
    weights = (qkv_w, out_w, ffn_in, ffn_out, small_params, pos_table, gate_proj)
    positions = jnp.arange(L, dtype=jnp.int32)

    def one_utterance(summed, utterance_in):
        frames_in, length, starts, cot_in = utterance_in
        forward = partial(layer_forward, length=length, starts=starts, buckets=buckets)
        output, backward = jax.vjp(forward, frames_in.astype(jnp.float32), *weights)
        valid_rows = (positions < length).astype(jnp.float32)
        gradients = backward(cot_in.astype(jnp.float32) * valid_rows[:, None])
        summed = tuple((running + weight_grad for running, weight_grad in zip(summed, gradients[1:])))
        return (summed, (output, gradients[0]))
    zeros_init = tuple((jnp.zeros(weight.shape, jnp.float32) for weight in weights))
    summed, (layer_out, feature_grad) = lax.scan(one_utterance, zeros_init, (features, lengths, span_starts, cotangent))
    grad_norm = jnp.sqrt(sum((jnp.sum(weight_grad * weight_grad) for weight_grad in summed)))
    clip_factor = jnp.minimum(1.0, CLIP_NORM / (grad_norm + 1e-06))
    count_in = step_count[0].astype(jnp.float32)
    qkv_new, qkv_moment, qkv_second = adam_step(qkv_w, summed[0], qkv_m, qkv_v, clip_factor, 2.0 * D ** (-0.5), count_in)
    out_new, out_moment, out_second = adam_step(out_w, summed[1], out_m, out_v, clip_factor, 1.0, count_in)
    ffn_in_new, ffn_in_moment, ffn_in_second = adam_step(ffn_in, summed[2], ffn_in_m, ffn_in_v, clip_factor, 2.0 * D ** (-0.5), count_in)
    ffn_out_new, ffn_out_moment, ffn_out_second = adam_step(ffn_out, summed[3], ffn_out_m, ffn_out_v, clip_factor, 2.0 * FF ** (-0.5), count_in)
    small_new, small_moment, small_second = adam_step(small_params, summed[4], small_m, small_v, clip_factor, 0.5, count_in)
    pos_new, pos_moment, pos_second = adam_step(pos_table, summed[5], pos_m, pos_v, clip_factor, 1.0, count_in)
    gate_new, gate_moment, gate_second = adam_step(gate_proj, summed[6], gate_m, gate_v, clip_factor, 2.0 * HD ** (-0.5), count_in)
    return (layer_out, feature_grad, grad_norm.reshape(1), qkv_new, qkv_moment, qkv_second, qkv_new.astype(jnp.bfloat16), out_new, out_moment, out_second, out_new.astype(jnp.bfloat16), ffn_in_new, ffn_in_moment, ffn_in_second, ffn_in_new.astype(jnp.bfloat16), ffn_out_new, ffn_out_moment, ffn_out_second, ffn_out_new.astype(jnp.bfloat16), summed[4], small_new, small_moment, small_second, pos_new, pos_moment, pos_second, gate_new, gate_moment, gate_second)
```

```python
import functools

import jax
import jax.numpy as jnp
from jax import lax
from jax.experimental import pallas as pl
from jax.experimental.pallas import tpu as pltpu
from jax.sharding import PartitionSpec as P

D = 768
H = 12
HD = 64
FF = 3072
NB = 320
SPAN = 10
CLIP_NORM = 1.0
BETA_ONE = 0.9
BETA_TWO = 0.98
ADAM_EPS = 1e-08
DECAY_RATE = 0.01
NORM_EPS = 1e-05
NEG_BIG = -1e30


def adam_step(weight, grad_in, moment, second, clip_factor, rate_in, count_in):
    scaled = grad_in * clip_factor
    new_moment = BETA_ONE * moment + (1.0 - BETA_ONE) * scaled
    new_second = BETA_TWO * second + (1.0 - BETA_TWO) * scaled * scaled
    first_fix = 1.0 - BETA_ONE**count_in
    second_fix = 1.0 - BETA_TWO**count_in
    update = new_moment / first_fix / (jnp.sqrt(new_second / second_fix) + ADAM_EPS)
    return (weight - rate_in * (update + DECAY_RATE * weight), new_moment, new_second)


NT=(((1,),(1,)),((),()))
TN=(((0,),(0,)),((),()))
def dot(a,b,dims=(((1,),(0,)),((),()))):
    return lax.dot_general(a,b,dims,preferred_element_type=jnp.float32)

def toep_kernel(off_ref, out_ref):
    row=jnp.broadcast_to(off_ref[0], out_ref.shape[1:])
    out_ref[0]=pltpu.roll(row, 0, 1, stride=1, stride_axis=0)

def toep(offr):
    n,w=offr.shape[0],offr.shape[-1]
    return pl.pallas_call(toep_kernel, grid=(n,),
        in_specs=[pl.BlockSpec((1,1,w),lambda h:(h,0,0))],
        out_specs=pl.BlockSpec((1,128,w),lambda h:(h,0,0)),
        out_shape=jax.ShapeDtypeStruct((n,128,w),jnp.float32))(offr.reshape(n,1,w))

def fwd_kernel(len_ref, q_ref,k_ref,v_ref,t_ref,g_ref,p_ref,o_ref,rl_ref,s_ref, *, seq, ib):
    h=pl.program_id(0)
    par=lax.rem(h,2)
    lane=lax.broadcasted_iota(jnp.int32,(seq,128),1)
    rowi=lax.broadcasted_iota(jnp.int32,(seq,128),0)
    inh=(lane//64)==par
    flag=lane==(64*(1-par))
    one=jnp.bfloat16(1.0); zero=jnp.bfloat16(0.0)
    bias=jnp.where(rowi<len_ref[0],0.0,NEG_BIG).astype(jnp.bfloat16)
    qm=jnp.where(flag,one,jnp.where(inh,q_ref[0],zero))
    km=jnp.where(flag,bias,k_ref[0])
    vm=jnp.where(flag,one,v_ref[0])
    vt=vm.T
    nb=seq//128
    base=seq-128
    for i0 in range(0,seq,ib):
        gate=g_ref[0,:,i0:i0+ib]
        qb=qm[i0:i0+ib]
        m=None
        for jb in range(nb):
            j0=jb*128
            c0=i0-j0+base
            s=dot(km[j0:j0+128],qb,NT)+t_ref[0,:,c0:c0+ib]*gate
            s_ref[j0:j0+128,:]=s
            mm=jnp.max(s.reshape(16,8,ib),axis=0)
            m=mm if m is None else jnp.maximum(m,mm)
        m=jnp.max(m,axis=0,keepdims=True)
        for jb in range(nb):
            j0=jb*128
            e=jnp.exp(s_ref[j0:j0+128,:]-m).astype(jnp.bfloat16)
            p_ref[0,j0:j0+128,i0:i0+ib]=e
        ct=dot(vt,p_ref[0,:,i0:i0+ib])
        l=jnp.where(par==0,ct[64:65],ct[0:1])
        rl=1.0/l
        oc=(ct*rl).T
        rc=jnp.broadcast_to(rl,(128,ib)).T
        ih=inh[i0:i0+ib]
        o_ref[i0:i0+ib,:]=jnp.where(ih,oc.astype(jnp.bfloat16),o_ref[i0:i0+ib,:])
        rl_ref[i0:i0+ib,:]=jnp.where(ih,rc,rl_ref[i0:i0+ib,:])

def attn_fwd(length,qkv,t2,gates,ib=256):
    seq=qkv.shape[1]; w=t2.shape[-1]
    return pl.pallas_call(functools.partial(fwd_kernel,seq=seq,ib=ib),
        grid_spec=pltpu.PrefetchScalarGridSpec(num_scalar_prefetch=1,grid=(H,),
        in_specs=[pl.BlockSpec((1,seq,128),lambda h,l:(0,0,h//2)),
                  pl.BlockSpec((1,seq,128),lambda h,l:(1,0,h//2)),
                  pl.BlockSpec((1,seq,128),lambda h,l:(2,0,h//2)),
                  pl.BlockSpec((1,128,w),lambda h,l:(h,0,0)),
                  pl.BlockSpec((1,1,seq),lambda h,l:(h,0,0))],
        out_specs=[pl.BlockSpec((1,seq,seq),lambda h,l:(h,0,0)),
                   pl.BlockSpec((seq,128),lambda h,l:(0,h//2)),
                   pl.BlockSpec((seq,128),lambda h,l:(0,h//2))],
        scratch_shapes=[pltpu.VMEM((seq,ib),jnp.float32)]),
        out_shape=[jax.ShapeDtypeStruct((H,seq,seq),jnp.bfloat16),
                   jax.ShapeDtypeStruct((seq,D),jnp.bfloat16),
                   jax.ShapeDtypeStruct((seq,D),jnp.float32)],
        compiler_params=pltpu.CompilerParams(vmem_limit_bytes=50<<20),
        )(length,qkv,qkv,qkv,t2,gates)

def bwd_kernel(q_ref,k_ref,v_ref,dc_ref,c_ref,p_ref,t_ref,g_ref,dq_ref,dk_ref,dv_ref,dg_ref,do_ref,a_ref,ds_ref,*,seq,ib):
    h=pl.program_id(0)
    par=lax.rem(h,2)
    lane=lax.broadcasted_iota(jnp.int32,(seq,128),1)
    inh=(lane//64)==par
    f0=lane==(64*(1-par))
    f1=lane==(64*(1-par)+1)
    one=jnp.bfloat16(1.0)
    dc=dc_ref[...]
    dcf=jnp.where(inh,dc.astype(jnp.float32),0.0)
    delta=-jnp.sum(dcf*c_ref[...].astype(jnp.float32),axis=1,keepdims=True)
    hi=delta.astype(jnp.bfloat16).astype(jnp.float32)
    lo=delta-hi
    dca=jnp.where(f0,hi,jnp.where(f1,lo,dcf)).astype(jnp.bfloat16)
    va=jnp.where(f0|f1,one,v_ref[0])
    kt=k_ref[0].T
    q=q_ref[0]
    nb=seq//128
    base=seq-128
    a_ref[...]=jnp.zeros_like(a_ref)
    for i0 in range(0,seq,ib):
        gate=g_ref[0,:,i0:i0+ib]
        dcb=dca[i0:i0+ib]
        dg=jnp.zeros((8,ib),jnp.float32)
        for jb in range(nb):
            j0=jb*128
            c0=i0-j0+base
            ds=dot(va[j0:j0+128],dcb,NT)*p_ref[0,j0:j0+128,i0:i0+ib].astype(jnp.float32)
            ds_ref[j0:j0+128,i0:i0+ib]=ds.astype(jnp.bfloat16)
            dg=dg+jnp.sum((ds*t_ref[0,:,c0:c0+ib]).reshape(16,8,ib),axis=0)
            a_ref[:,c0:c0+ib]+=ds*gate
        dg_ref[0,:,i0:i0+ib]=jnp.sum(dg,axis=0,keepdims=True)
        dqt=dot(kt,ds_ref[:,i0:i0+ib])
        dq_ref[i0:i0+ib,:]=jnp.where(inh[i0:i0+ib],dqt.T.astype(jnp.bfloat16),dq_ref[i0:i0+ib,:])
    dk=dot(ds_ref[...],q)
    dk_ref[...]=jnp.where(inh,dk.astype(jnp.bfloat16),dk_ref[...])
    dv=dot(p_ref[0],dc)
    dv_ref[...]=jnp.where(inh,dv.astype(jnp.bfloat16),dv_ref[...])
    a=a_ref[...]
    w=a.shape[1]
    r=64
    while r>=8:
        a=a[:r]+pltpu.roll(a[r:],w-r,1)
        r//=2
    acc=a[0:1]
    for r in range(1,8):
        acc=acc+pltpu.roll(a[r:r+1],w-r,1)
    do_ref[0]=acc

def attn_bwd(qkv,dctx,ctx,p,t2,gates,ib=256):
    seq=qkv.shape[1]; w=t2.shape[-1]
    pairb=pl.BlockSpec((seq,128),lambda h:(0,h//2))
    return pl.pallas_call(functools.partial(bwd_kernel,seq=seq,ib=ib),
        grid=(H,),
        in_specs=[pl.BlockSpec((1,seq,128),lambda h:(0,0,h//2)),
                  pl.BlockSpec((1,seq,128),lambda h:(1,0,h//2)),
                  pl.BlockSpec((1,seq,128),lambda h:(2,0,h//2)),
                  pairb,pairb,
                  pl.BlockSpec((1,seq,seq),lambda h:(h,0,0)),
                  pl.BlockSpec((1,128,w),lambda h:(h,0,0)),
                  pl.BlockSpec((1,1,seq),lambda h:(h,0,0))],
        out_specs=[pairb,pairb,pairb,
                   pl.BlockSpec((1,1,seq),lambda h:(h,0,0)),
                   pl.BlockSpec((1,1,w),lambda h:(h,0,0))],
        scratch_shapes=[pltpu.VMEM((128,w),jnp.float32),pltpu.VMEM((seq,seq),jnp.bfloat16)],
        out_shape=[jax.ShapeDtypeStruct((seq,D),jnp.bfloat16)]*3+[
                   jax.ShapeDtypeStruct((H,1,seq),jnp.float32),
                   jax.ShapeDtypeStruct((H,1,w),jnp.float32)],
        compiler_params=pltpu.CompilerParams(vmem_limit_bytes=50<<20),
        )(qkv,qkv,qkv,dctx,ctx,p,t2,gates)


def gelu_both(x):
    half = 0.5 * (1.0 + lax.erf(x * 0.7071067811865476))
    dens = jnp.exp(-0.5 * x * x) * 0.3989422804014327
    return x * half, half + x * dens


def split3(x):
    hi = x.astype(jnp.bfloat16)
    rest = x - hi.astype(jnp.float32)
    mid = rest.astype(jnp.bfloat16)
    low = (rest - mid.astype(jnp.float32)).astype(jnp.bfloat16)
    return hi, mid, low


def tree_sum(parts):
    while len(parts) > 1:
        half = len(parts) // 2
        parts = [parts[i] + parts[i + half] for i in range(half)]
    return parts[0]


def norm_rows(r):
    mean = jnp.mean(r, axis=-1, keepdims=True)
    cen = r - mean
    inv = lax.rsqrt(jnp.mean(cen * cen, axis=-1, keepdims=True) + NORM_EPS)
    return cen * inv, inv


def norm_back(cot, n, inv, gain):
    e = cot * gain
    return inv * (
        e - jnp.mean(e, axis=-1, keepdims=True) - n * jnp.mean(e * n, axis=-1, keepdims=True)
    )


class Net:
    def __init__(self, dp_size, t_size):
        self.t = t_size
        self.sizes = {"z": dp_size // 4, "y": 2, "c": 2, "x": t_size}
        d = lax.axis_index("dp")
        self.at = {"z": d // 4, "y": d // 2 % 2, "c": d % 2, "x": lax.axis_index("tensor")}

    def shift(self, v, axis, k):
        pairs = []
        sz = self.sizes
        for z in range(sz["z"]):
            for y in range(2):
                for c in range(2):
                    for x in range(sz["x"]):
                        src = {"z": z, "y": y, "c": c, "x": x}
                        dst = dict(src)
                        dst[axis] = (src[axis] - k) % sz[axis]
                        flat = [((q["z"] * 2 + q["y"]) * 2 + q["c"]) * sz["x"] + q["x"] for q in (src, dst)]
                        pairs.append(tuple(flat))
        return lax.ppermute(v, ("dp", "tensor"), pairs)

    def gather(self, v, axis, dim):
        return jnp.concatenate([v] + [self.shift(v, axis, k) for k in range(1, self.sizes[axis])], axis=dim)

    def scatter(self, v, axis, dim):
        n = self.sizes[axis]
        total = lax.index_in_dim(v, 0, dim, False).astype(jnp.float32)
        for k in range(1, n):
            total += self.shift(lax.index_in_dim(v, k, dim, False), axis, n - k).astype(jnp.float32)
        return total.astype(jnp.bfloat16)

    def scatter_own(self, v, axis, dim):
        n = self.sizes[axis]
        at = self.at[axis]
        total = lax.dynamic_index_in_dim(v, at, dim, False).astype(jnp.float32)
        for k in range(1, n):
            part = lax.dynamic_index_in_dim(v, (at + k) % n, dim, False)
            total += self.shift(part, axis, n - k).astype(jnp.float32)
        return total.astype(jnp.bfloat16)

    def gather_own(self, v, axis, dim):
        n = self.sizes[axis]
        at = self.at[axis]
        out = jnp.zeros(v.shape[:dim] + (n,) + v.shape[dim:], v.dtype)
        for k in range(n):
            part = v if k == 0 else self.shift(v, axis, k)
            out = lax.dynamic_update_index_in_dim(out, part, (at + k) % n, dim)
        return out

    def total(self, v):
        for axis in ("c", "x", "y", "z"):
            v = tree_sum([v] + [self.shift(v, axis, k) for k in range(1, self.sizes[axis])])
        return v


def local(dp_size, t_size, features, lengths, span_starts, buckets, cotangent,
          qkv_w, qkv_m, qkv_v, out_w, out_m, out_v, ffn_in, ffn_in_m, ffn_in_v,
          ffn_out, ffn_out_m, ffn_out_v, small_params, small_m, small_v,
          pos_table, pos_m, pos_v, gate_proj, gate_m, gate_v, step_count):
    f32, b16 = jnp.float32, jnp.bfloat16
    net = Net(dp_size, t_size)
    zs = net.sizes["z"]
    seq = features.shape[1]
    own = ffn_out.shape[0]
    rows = qkv_w.shape[1]
    scale = HD**-0.5

    attn_own = jnp.concatenate([qkv_w, out_w[None]], axis=0).astype(b16)
    attn_z = net.gather_own(attn_own, "z", 0)
    attn_y = net.gather_own(attn_z, "y", 1)
    attn_c = net.gather_own(attn_y, "c", 2)
    attn_all = attn_c.transpose(3, 0, 1, 2, 4, 5).reshape(4, D, D)
    qkv_all, out_all = attn_all[:3], attn_all[3]

    w_in_own = ffn_in[:D].T.astype(b16)
    w_out_own = ffn_out.astype(b16)
    b_in_own = ffn_in[D:].astype(b16).astype(f32)
    w_in_half = net.gather(net.gather(net.gather(w_in_own[None, None, None], "z", 2), "y", 1), "x", 0)
    w_out_half = net.gather(net.gather(net.gather(w_out_own[None, None, None], "z", 2), "x", 0), "y", 1)
    b_in_half = net.gather(net.gather(net.gather(b_in_own[None, None], "z", 2), "y", 1), "x", 0)
    w_in = [w_in_half.reshape(-1, D), net.shift(w_in_half, "c", 1).reshape(-1, D)]
    w_out = [w_out_half.reshape(-1, D), net.shift(w_out_half, "c", 1).reshape(-1, D)]
    b_in = [b_in_half.reshape(-1), net.shift(b_in_half, "c", 1).reshape(-1)]

    positions = jnp.arange(seq, dtype=jnp.int32)
    starts = span_starts[0]
    masked = jnp.any((positions[:, None] >= starts[None, :]) & (positions[:, None] < starts[None, :] + SPAN), axis=1)[:, None]
    mixed = jnp.where(masked, small_params[8][None, :], features[0].astype(f32))
    rounded = mixed.astype(b16)

    ga = jnp.sum(gate_proj[:HD, :4], axis=1)
    gb = jnp.sum(gate_proj[:HD, 4:], axis=1)
    za = jnp.sum(gate_proj[HD, :4])
    zb = jnp.sum(gate_proj[HD, 4:])
    eye = jnp.eye(H, dtype=f32)[:, :, None]
    wg = jnp.concatenate([(eye * ga).reshape(H, D), (eye * gb).reshape(H, D)], axis=0)
    wg3 = split3(wg)
    z3 = dot(jnp.concatenate(wg3, axis=0), rounded, NT).reshape(3, 2 * H, seq)
    z_all = z3[0] + z3[1] + z3[2]
    gate_a = jax.nn.sigmoid(z_all[:H] + za)
    gate_b = jax.nn.sigmoid(z_all[H:] + zb)
    const = pos_table[NB][:, None]
    gates = (gate_a * (gate_b * const - 1.0) + 2.0).reshape(H, 1, seq)

    rev = jnp.flip(buckets)
    order = jnp.concatenate([rev[127:], jnp.full((1,), -1, jnp.int32), rev[:127]])
    onehot = (jnp.arange(NB, dtype=jnp.int32)[:, None] == order[None, :]).astype(b16)
    off3 = dot(jnp.concatenate(split3(pos_table[:NB].T), axis=0), onehot).reshape(3, H, 2 * seq)
    table = toep(off3[0] + off3[1] + off3[2])

    proj = jnp.einsum("fi,kio->kfo", rounded, qkv_all, preferred_element_type=f32)
    bias3 = jnp.stack([small_params[0], jnp.zeros((D,), f32), small_params[1]])[:, None, :]
    scale3 = jnp.array([scale, 1.0, 1.0], f32)[:, None, None]
    qkv = ((proj + bias3) * scale3).astype(b16)
    probs, context, inv_sum = attn_fwd(lengths, qkv, table, gates)
    attention = dot(context, out_all) + small_params[2]
    n1, inv1 = norm_rows(mixed + attention)
    first = n1 * small_params[3] + small_params[4]
    first_low = first.astype(b16)

    active, slope = [], []
    for half in range(2):
        hid = dot(first_low, w_in[half], NT) + b_in[half]
        act, slo = gelu_both(hid)
        active.append(act.astype(b16))
        slope.append(slo.astype(b16))
    branch = dot(active[0], w_out[0]) + dot(active[1], w_out[1]) + small_params[7]
    n2, inv2 = norm_rows(first + branch)
    layer_out = n2 * small_params[5] + small_params[6]

    cot = jnp.where((positions < lengths[0])[:, None], cotangent[0].astype(f32), 0.0)
    d_gain2 = jnp.sum(cot * n2, axis=0)
    d_shift2 = jnp.sum(cot, axis=0)
    d_res2 = norm_back(cot, n2, inv2, small_params[5])
    d_branch = d_res2.astype(b16)
    d_bias_out = jnp.sum(d_branch.astype(f32), axis=0)
    shape_rel = (t_size, 2, zs, own, D)
    g_outw_peer = dot(active[1], d_branch, TN).astype(b16)
    g_outw_mine = dot(active[0], d_branch, TN).astype(b16)
    g_outw = (g_outw_mine.astype(f32) + net.shift(g_outw_peer, "c", 1).astype(f32)).astype(b16).reshape(shape_rel)
    g_outw = net.scatter(net.scatter(net.scatter(g_outw, "y", 1), "x", 0), "z", 0).astype(f32)
    d_hidden = [(dot(d_branch, w_out[h], NT) * slope[h].astype(f32)).astype(b16) for h in range(2)]
    d_first = d_res2 + (dot(d_hidden[0], w_in[0]) + dot(d_hidden[1], w_in[1]))
    g_in_peer = dot(d_hidden[1], first_low, TN).astype(b16)
    g_in_mine = dot(d_hidden[0], first_low, TN).astype(b16)
    g_in = (g_in_mine.astype(f32) + net.shift(g_in_peer, "c", 1).astype(f32)).astype(b16).reshape(shape_rel)
    g_in = net.scatter(net.scatter(net.scatter(g_in, "x", 0), "y", 0), "z", 0).astype(f32)
    g_bias_in = jnp.stack([jnp.sum(d.astype(f32), axis=0) for d in d_hidden]).reshape(2, t_size, 2, zs, own)
    for dim, axis in enumerate(("c", "x", "y", "z")):
        g_bias_in = jnp.roll(g_bias_in, net.at[axis], dim)
    g_bias_in = g_bias_in.transpose(3, 2, 0, 1, 4).reshape(-1, own)

    d_gain1 = jnp.sum(d_first * n1, axis=0)
    d_shift1 = jnp.sum(d_first, axis=0)
    d_res1 = norm_back(d_first, n1, inv1, small_params[3])
    d_attention = d_res1.astype(b16)
    d_bias_attn = jnp.sum(d_attention.astype(f32), axis=0)
    g_out_local = dot(context, d_attention, TN).astype(b16)
    d_context = (dot(d_attention, out_all, NT) * inv_sum).astype(b16)

    dq, dk, dv, dgate, doff = attn_bwd(qkv, d_context, context, probs, table, gates)
    dq = dq * scale
    g_qkv_local = [dot(rounded, d, TN).astype(b16) for d in (dq, dk, dv)]
    dgate = dgate.reshape(H, seq)
    d_a = dgate * (gate_b * const - 1.0) * gate_a * (1.0 - gate_a)
    d_b = dgate * gate_a * const * gate_b * (1.0 - gate_b)
    d_const = jnp.sum(dgate * gate_a * gate_b, axis=1)
    dz = jnp.concatenate([d_a, d_b], axis=0)
    dz_hi = dz.astype(b16)
    dz_lo = (dz - dz_hi.astype(f32)).astype(b16)
    d_heads = dot(jnp.concatenate([dz_hi, dz_lo, dz_hi], axis=0),
                  jnp.concatenate([wg3[0], wg3[0], wg3[1]], axis=0), TN)
    d_mixed = (d_res1 + dot(dq, qkv_all[0], NT) + dot(dk, qkv_all[1], NT) + dot(dv, qkv_all[2], NT) + d_heads)
    feature_grad = jnp.where(masked, 0.0, d_mixed)
    d_mask = jnp.sum(jnp.where(masked, d_mixed, 0.0), axis=0)
    g_z2 = dot(jnp.concatenate([dz_hi, dz_lo], axis=0), rounded).reshape(2, 2, H, H, HD)
    g_z = jnp.sum((g_z2[0] + g_z2[1]) * eye, axis=(1, 2))
    g_zb = jnp.sum(dz.reshape(2, H * seq), axis=1)
    g_gate_local = jnp.repeat(jnp.concatenate([g_z, g_zb[:, None]], axis=1).T, 4, axis=1)
    pos3 = dot(onehot, jnp.concatenate(split3(doff.reshape(H, 2 * seq)), axis=0), NT).reshape(NB, 3, H)
    pos_local = jnp.concatenate([jnp.sum(pos3, axis=1), d_const[None, :]], axis=0)
    small_local = jnp.stack([
        jnp.sum(dq.astype(f32), axis=0), jnp.sum(dv.astype(f32), axis=0), d_bias_attn,
        d_gain1, d_shift1, d_gain2, d_shift2, d_bias_out, d_mask])

    g_attn = jnp.stack(g_qkv_local + [g_out_local])
    if t_size <= 4:
        g_attn = g_attn.reshape(t_size, 4 // t_size, zs, 2, 2, rows, D)
        g_attn = net.scatter_own(g_attn, "c", 4)
        g_attn = net.scatter_own(g_attn, "x", 0)
        g_attn = net.scatter_own(g_attn, "y", 2)
        g_attn = net.scatter_own(g_attn, "z", 1)
    else:
        g_attn = g_attn.reshape(4, zs, 2, 2, rows, D).transpose(1, 2, 3, 0, 4, 5)
        g_attn = g_attn.reshape(zs, 2, 2, t_size, -1, D)
        g_attn = net.scatter_own(g_attn, "c", 2)
        g_attn = net.scatter_own(g_attn, "x", 2)
        g_attn = net.scatter_own(g_attn, "y", 1)
        g_attn = net.scatter_own(g_attn, "z", 0)
    attn_sq = jnp.sum(jnp.square(g_attn.astype(f32)))
    g_attn = net.gather_own(g_attn, "x", 0).reshape(4, rows, D).astype(f32)
    g_qkv, g_out = g_attn[:3], g_attn[3]

    parts = [small_local, pos_local, g_gate_local, g_bias_in]
    counts = [p.size for p in parts]
    pad = -sum(counts) % 1024
    flat = jnp.concatenate([p.reshape(-1) for p in parts] + [jnp.zeros((pad,), f32)])
    flat = net.total(flat.reshape(-1, 128)).reshape(-1)
    pieces, at = [], 0
    for p, count in zip(parts, counts):
        pieces.append(flat[at : at + count].reshape(p.shape))
        at += count
    g_small, g_pos, g_gate, g_bias = pieces
    shared = sum(jnp.sum(jnp.square(p)) for p in pieces)
    own_sum = attn_sq + jnp.sum(jnp.square(g_in)) + jnp.sum(jnp.square(g_outw))
    own_sum = net.total(jnp.broadcast_to(own_sum, (8, 128)))[0, 0]
    grad_norm = jnp.sqrt(own_sum + shared)
    clip = jnp.minimum(1.0, CLIP_NORM / (grad_norm + 1e-06))
    count = step_count[0].astype(f32)
    me = lax.axis_index("dp") * t_size + lax.axis_index("tensor")
    g_ffn_in = jnp.concatenate([g_in.T, lax.dynamic_slice_in_dim(g_bias, me, 1, 0)], axis=0)

    qkv_new, qkv_moment, qkv_second = adam_step(qkv_w, g_qkv, qkv_m, qkv_v, clip, 2.0 * D**-0.5, count)
    out_new, out_moment, out_second = adam_step(out_w, g_out, out_m, out_v, clip, 1.0, count)
    in_new, in_moment, in_second = adam_step(ffn_in, g_ffn_in, ffn_in_m, ffn_in_v, clip, 2.0 * D**-0.5, count)
    fo_new, fo_moment, fo_second = adam_step(ffn_out, g_outw, ffn_out_m, ffn_out_v, clip, 2.0 * FF**-0.5, count)
    small_new, small_moment, small_second = adam_step(small_params, g_small, small_m, small_v, clip, 0.5, count)
    pos_new, pos_moment, pos_second = adam_step(pos_table, g_pos, pos_m, pos_v, clip, 1.0, count)
    gate_new, gate_moment, gate_second = adam_step(gate_proj, g_gate, gate_m, gate_v, clip, 2.0 * HD**-0.5, count)
    return (
        layer_out[None], feature_grad[None], grad_norm.reshape(1),
        qkv_new, qkv_moment, qkv_second, qkv_new.astype(b16),
        out_new, out_moment, out_second, out_new.astype(b16),
        in_new, in_moment, in_second, in_new.astype(b16),
        fo_new, fo_moment, fo_second, fo_new.astype(b16),
        g_small, small_new, small_moment, small_second,
        pos_new, pos_moment, pos_second, gate_new, gate_moment, gate_second,
    )


def solution(mesh):
    both = ("dp", "tensor")
    three = (P(None, "dp", None),)
    row = (P("dp", None),)
    col = (P(None, both),)
    rows2 = (P(both, None),)
    utt = P(both, None, None)
    in_specs = (
        (utt, P(both), P(both, None), P(), utt) + three * 3 + row * 3 + col * 3 + rows2 * 3 + (P(),) * 10
    )
    out_specs = (utt, utt, P()) + three * 4 + row * 4 + col * 4 + rows2 * 4 + (P(),) * 10
    fn = functools.partial(local, mesh.shape["dp"], mesh.shape["tensor"])
    return jax.shard_map(fn, mesh=mesh, in_specs=in_specs, out_specs=out_specs, check_vma=False)
```

```python
import functools

import jax
import jax.numpy as jnp
from jax import lax
from jax.experimental import pallas as pl
from jax.experimental.pallas import tpu as pltpu
from jax.sharding import PartitionSpec as P

D = 768
H = 12
HD = 64
FF = 3072
NB = 320
SPAN = 10
CLIP_NORM = 1.0
BETA_ONE = 0.9
BETA_TWO = 0.98
ADAM_EPS = 1e-08
DECAY_RATE = 0.01
NORM_EPS = 1e-05
NEG_BIG = -1e30
GROUPS = 3


def adam_step(weight, grad_in, moment, second, clip_factor, rate_in, count_in):
    scaled = grad_in * clip_factor
    new_moment = BETA_ONE * moment + (1.0 - BETA_ONE) * scaled
    new_second = BETA_TWO * second + (1.0 - BETA_TWO) * scaled * scaled
    first_fix = 1.0 - BETA_ONE**count_in
    second_fix = 1.0 - BETA_TWO**count_in
    update = new_moment / first_fix / (jnp.sqrt(new_second / second_fix) + ADAM_EPS)
    return (weight - rate_in * (update + DECAY_RATE * weight), new_moment, new_second)


VMEM = 60 << 20
NT = (((1,), (1,)), ((), ()))
TN = (((0,), (0,)), ((), ()))


def dot(a, b, dims=(((1,), (0,)), ((), ()))):
    return lax.dot_general(a, b, dims, preferred_element_type=jnp.float32)


def cost(us):
    return pl.CostEstimate(flops=0, bytes_accessed=int(us * 3.0e6), transcendentals=0)


def table_kernel(off_ref, out_ref):
    row = jnp.broadcast_to(off_ref[0], out_ref.shape[1:])
    out_ref[0] = pltpu.roll(row, 0, 1, stride=1, stride_axis=0)


def bias_tables(offr):
    n, w = offr.shape
    return pl.pallas_call(
        table_kernel,
        grid=(n,),
        in_specs=[pl.BlockSpec((1, 1, w), lambda h: (h, 0, 0))],
        out_specs=pl.BlockSpec((1, 128, w), lambda h: (h, 0, 0)),
        out_shape=jax.ShapeDtypeStruct((n, 128, w), jnp.float32),
        compiler_params=pltpu.CompilerParams(vmem_limit_bytes=VMEM),
        cost_estimate=cost(10),
    )(offr.reshape(n, 1, w))


def assemble_kernel(at_ref, mine_ref, peer_ref, out_ref, sem, *, zs, rows, cols):
    z0, y0, c0 = at_ref[0], at_ref[1], at_ref[2]
    copies = []
    for c, src in enumerate((mine_ref, peer_ref)):
        for y in range(2):
            for z in range(zs):
                block = (lax.rem(z0 + z, zs) * 2 + lax.rem(y0 + y, 2)) * 2 + lax.rem(c0 + c, 2)
                first = pl.multiple_of(block * rows, rows)
                for k in range(3):
                    there = out_ref.at[pl.ds(first, rows), pl.ds(k * cols, cols)]
                    copies.append(pltpu.make_async_copy(src.at[y, z, 3 + k], there, sem.at[len(copies)]))
    for copy in copies:
        copy.start()
    for copy in copies:
        copy.wait()


def assemble(at, mine, peer):
    _, zs, _, rows, cols = mine.shape
    hbm = pl.BlockSpec(memory_space=pl.ANY)
    return pl.pallas_call(
        functools.partial(assemble_kernel, zs=zs, rows=rows, cols=cols),
        in_specs=[pl.BlockSpec(memory_space=pltpu.SMEM), hbm, hbm],
        out_specs=pl.BlockSpec(memory_space=pltpu.VMEM),
        scratch_shapes=[pltpu.SemaphoreType.DMA((12 * zs,))],
        out_shape=jax.ShapeDtypeStruct((D, D), jnp.bfloat16),
        compiler_params=pltpu.CompilerParams(vmem_limit_bytes=VMEM),
        cost_estimate=cost(2),
    )(at, mine, peer)


def fwd_kernel(len_ref, at_ref, x_ref, mine_ref, peer_ref, bias_ref, t_ref, g_ref, *rest, seq, ib, zs, rows, kept):
    p_ref, o_ref, of_ref, rl_ref, qkv_ref, w_ref, s_ref, sem = rest[kept:]
    h = pl.program_id(0)

    @pl.when(h == 0)
    def _():
        z0, y0, c0 = at_ref[0], at_ref[1], at_ref[2]
        copies = []
        for c, src in enumerate((mine_ref, peer_ref)):
            for y in range(2):
                for z in range(zs):
                    block = (lax.rem(z0 + z, zs) * 2 + lax.rem(y0 + y, 2)) * 2 + lax.rem(c0 + c, 2)
                    first = pl.multiple_of(block * rows, rows)
                    there = w_ref.at[:, pl.ds(first, rows), :]
                    copies.append(pltpu.make_async_copy(src.at[y, z, pl.ds(0, 3)], there, sem.at[len(copies)]))
        for copy in copies:
            copy.start()
        for copy in copies:
            copy.wait()
        for k in range(3):
            r = dot(x_ref[...], w_ref[k]) + bias_ref[k]
            qkv_ref[k] = (r * HD**-0.5 if k == 0 else r).astype(jnp.bfloat16)

    par = lax.rem(h, 2)
    lane = lax.broadcasted_iota(jnp.int32, (seq, 128), 1)
    rowi = lax.broadcasted_iota(jnp.int32, (seq, 128), 0)
    inh = (lane // 64) == par
    flag = lane == (64 * (1 - par))
    one = jnp.bfloat16(1.0)
    zero = jnp.bfloat16(0.0)
    pair = pl.ds(pl.multiple_of(h // 2 * 128, 128), 128)
    bias = jnp.where(rowi < len_ref[0], 0.0, NEG_BIG).astype(jnp.bfloat16)
    qm = jnp.where(flag, one, jnp.where(inh, qkv_ref[0, :, pair], zero))
    km = jnp.where(flag, bias, qkv_ref[1, :, pair])
    vm = jnp.where(flag, one, qkv_ref[2, :, pair])
    vt = vm.T
    base = seq - 128
    for i0 in range(0, seq, ib):
        gate = g_ref[0, :, i0 : i0 + ib]
        qb = qm[i0 : i0 + ib]
        m = None
        for j0 in range(0, seq, 128):
            c0 = i0 - j0 + base
            s = dot(km[j0 : j0 + 128], qb, NT) + t_ref[0, :, c0 : c0 + ib] * gate
            s_ref[j0 : j0 + 128, :] = s
            mm = jnp.max(s.reshape(16, 8, ib), axis=0)
            m = mm if m is None else jnp.maximum(m, mm)
        m = jnp.max(m, axis=0, keepdims=True)
        for j0 in range(0, seq, 128):
            e = jnp.exp(s_ref[j0 : j0 + 128, :] - m).astype(jnp.bfloat16)
            p_ref[0, j0 : j0 + 128, i0 : i0 + ib] = e
        ct = dot(vt, p_ref[0, :, i0 : i0 + ib])
        total = jnp.where(par == 0, ct[64:65], ct[0:1])
        rl = 1.0 / total
        oc = (ct * rl).T
        rc = jnp.broadcast_to(rl, (128, ib)).T
        ih = inh[i0 : i0 + ib]
        o_ref[i0 : i0 + ib, :] = jnp.where(ih, oc.astype(jnp.bfloat16), o_ref[i0 : i0 + ib, :])
        of_ref[i0 : i0 + ib, :] = jnp.where(ih, oc, of_ref[i0 : i0 + ib, :])
        rl_ref[i0 : i0 + ib, :] = jnp.where(ih, rc, rl_ref[i0 : i0 + ib, :])


def attn_fwd(length, at, x, mine, peer, bias, table, gates, head0, heads, kept, ib=256):
    seq = x.shape[0]
    _, zs, _, rows, cols = mine.shape
    w = table.shape[-1]
    f32, b16 = jnp.float32, jnp.bfloat16
    out_pair = pl.BlockSpec((seq, 128), lambda h, n, a: (0, head0 // 2 + h // 2))
    hbm = pl.BlockSpec(memory_space=pl.ANY)
    return pl.pallas_call(
        functools.partial(fwd_kernel, seq=seq, ib=ib, zs=zs, rows=rows, kept=len(kept)),
        grid_spec=pltpu.PrefetchScalarGridSpec(
            num_scalar_prefetch=2,
            grid=(heads,),
            in_specs=[
                pl.BlockSpec((seq, D), lambda h, n, a: (0, 0)),
                hbm,
                hbm,
                pl.BlockSpec((3, 1, cols), lambda h, n, a: (0, 0, 0)),
                pl.BlockSpec((1, 128, w), lambda h, n, a: (head0 + h, 0, 0)),
                pl.BlockSpec((1, 1, seq), lambda h, n, a: (head0 + h, 0, 0)),
            ] + [hbm] * len(kept),
            out_specs=[pl.BlockSpec((1, seq, seq), lambda h, n, a: (h, 0, 0)), out_pair, out_pair, out_pair,
                       pl.BlockSpec((3, seq, cols), lambda h, n, a: (0, 0, 0)),
                       pl.BlockSpec((3, D, cols), lambda h, n, a: (0, 0, 0))],
            scratch_shapes=[pltpu.VMEM((seq, ib), f32), pltpu.SemaphoreType.DMA((4 * zs,))],
        ),
        out_shape=[jax.ShapeDtypeStruct((heads, seq, seq), b16), jax.ShapeDtypeStruct((seq, D), b16),
                   jax.ShapeDtypeStruct((seq, D), f32), jax.ShapeDtypeStruct((seq, D), f32),
                   jax.ShapeDtypeStruct((3, seq, cols), b16), jax.ShapeDtypeStruct((3, D, cols), b16)],
        input_output_aliases={8: 1, 9: 2, 10: 3} if kept else {},
        compiler_params=pltpu.CompilerParams(vmem_limit_bytes=VMEM),
        cost_estimate=cost(2.7 * heads + 4),
    )(length, at, x, mine, peer, bias, table, gates, *kept)


def bwd_kernel(q_ref, k_ref, v_ref, dc_ref, c_ref, p_ref, t_ref, g_ref, d_ref, dg_ref, do_ref, a_ref, ds_ref, *, seq, ib):
    par = lax.rem(pl.program_id(0), 2)
    lane = lax.broadcasted_iota(jnp.int32, (seq, 128), 1)
    inh = (lane // 64) == par
    f0 = lane == (64 * (1 - par))
    f1 = lane == (64 * (1 - par) + 1)
    one = jnp.bfloat16(1.0)
    dc = dc_ref[...]
    dcf = jnp.where(inh, dc.astype(jnp.float32), 0.0)
    delta = -jnp.sum(dcf * c_ref[...], axis=1, keepdims=True)
    hi = delta.astype(jnp.bfloat16).astype(jnp.float32)
    lo = delta - hi
    dca = jnp.where(f0, hi, jnp.where(f1, lo, dcf)).astype(jnp.bfloat16)
    va = jnp.where(f0 | f1, one, v_ref[0])
    kt = k_ref[0].T
    q = q_ref[0]
    base = seq - 128
    a_ref[...] = jnp.zeros_like(a_ref)
    for i0 in range(0, seq, ib):
        gate = g_ref[0, :, i0 : i0 + ib]
        dcb = dca[i0 : i0 + ib]
        dg = jnp.zeros((8, ib), jnp.float32)
        for j0 in range(0, seq, 128):
            c0 = i0 - j0 + base
            ds = dot(va[j0 : j0 + 128], dcb, NT) * p_ref[0, j0 : j0 + 128, i0 : i0 + ib].astype(jnp.float32)
            ds_ref[j0 : j0 + 128, i0 : i0 + ib] = ds.astype(jnp.bfloat16)
            dg = dg + jnp.sum((ds * t_ref[0, :, c0 : c0 + ib]).reshape(16, 8, ib), axis=0)
            a_ref[:, c0 : c0 + ib] += ds * gate
        dg_ref[0, :, i0 : i0 + ib] = jnp.sum(dg, axis=0, keepdims=True)
        dqt = dot(kt, ds_ref[:, i0 : i0 + ib]).T * HD**-0.5
        d_ref[0, i0 : i0 + ib, :] = jnp.where(inh[i0 : i0 + ib], dqt.astype(jnp.bfloat16), d_ref[0, i0 : i0 + ib, :])
    dk = dot(ds_ref[...], q)
    d_ref[1] = jnp.where(inh, dk.astype(jnp.bfloat16), d_ref[1])
    dv = dot(p_ref[0], dc)
    d_ref[2] = jnp.where(inh, dv.astype(jnp.bfloat16), d_ref[2])
    a = a_ref[...]
    w = a.shape[1]
    r = 64
    while r >= 8:
        a = a[:r] + pltpu.roll(a[r:], w - r, 1)
        r //= 2
    acc = a[0:1]
    for r in range(1, 8):
        acc = acc + pltpu.roll(a[r : r + 1], w - r, 1)
    do_ref[0] = acc


def attn_bwd(qkv, dctx, ctx, probs, table, gates, head0, heads, ib=256):
    seq = qkv.shape[1]
    w = table.shape[-1]

    def part(k):
        return pl.BlockSpec((1, seq, 128), lambda h: (k, 0, h // 2))

    pair = pl.BlockSpec((seq, 128), lambda h: (0, head0 // 2 + h // 2))
    return pl.pallas_call(
        functools.partial(bwd_kernel, seq=seq, ib=ib),
        grid=(heads,),
        in_specs=[
            part(0),
            part(1),
            part(2),
            pair,
            pair,
            pl.BlockSpec((1, seq, seq), lambda h: (h, 0, 0)),
            pl.BlockSpec((1, 128, w), lambda h: (head0 + h, 0, 0)),
            pl.BlockSpec((1, 1, seq), lambda h: (head0 + h, 0, 0)),
        ],
        out_specs=[
            pl.BlockSpec((3, seq, 128), lambda h: (0, 0, h // 2)),
            pl.BlockSpec((1, 1, seq), lambda h: (h, 0, 0)),
            pl.BlockSpec((1, 1, w), lambda h: (h, 0, 0)),
        ],
        scratch_shapes=[pltpu.VMEM((128, w), jnp.float32), pltpu.VMEM((seq, seq), jnp.bfloat16)],
        out_shape=[
            jax.ShapeDtypeStruct((3, seq, heads * HD), jnp.bfloat16),
            jax.ShapeDtypeStruct((heads, 1, seq), jnp.float32),
            jax.ShapeDtypeStruct((heads, 1, w), jnp.float32),
        ],
        compiler_params=pltpu.CompilerParams(vmem_limit_bytes=VMEM),
        cost_estimate=cost(3.0 * heads),
    )(qkv, qkv, qkv, dctx, ctx, probs, table, gates)


def wgrad_kernel(xt_ref, d_ref, a_ref, b_ref, g_ref, *, pair):
    xt = xt_ref[...]
    for k in range(3):
        g_ref[:, k * 256 : k * 256 + 256] = dot(xt, d_ref[k]).astype(jnp.bfloat16)
    if pair:
        g_ref[:, 768:1536] = dot(a_ref[...], b_ref[...], TN).astype(jnp.bfloat16)
    else:
        for k in range(3):
            g_ref[:, 768 + k * 256 : 1024 + k * 256] = dot(xt, a_ref[k]).astype(jnp.bfloat16)


def weight_grads(xt, d3, a, b, block=256):
    seq = xt.shape[1]
    pair = a.ndim == 2
    kinds = pl.BlockSpec((3, seq, 256), lambda i: (0, 0, 0))
    a_spec = pl.BlockSpec((seq, block), lambda i: (0, i)) if pair else kinds
    b_spec = pl.BlockSpec((seq, D), lambda i: (0, 0)) if pair else pl.BlockSpec((8, 128), lambda i: (0, 0))
    return pl.pallas_call(
        functools.partial(wgrad_kernel, pair=pair),
        grid=(D // block,),
        in_specs=[pl.BlockSpec((block, seq), lambda i: (i, 0)), kinds, a_spec, b_spec],
        out_specs=pl.BlockSpec((block, 2 * D), lambda i: (i, 0)),
        out_shape=jax.ShapeDtypeStruct((D, 2 * D), jnp.bfloat16),
        compiler_params=pltpu.CompilerParams(vmem_limit_bytes=VMEM),
        cost_estimate=cost(5),
    )(xt, d3, a, b)


def core_split_kernel(at_ref, d_ref, x_ref, keep_ref, send_ref, *, wide, places):
    g = dot(d_ref[...], x_ref[...], TN).astype(jnp.bfloat16)
    first = at_ref[2] == 0
    for k in range(places):
        low = g[2 * k * wide : (2 * k + 1) * wide]
        high = g[(2 * k + 1) * wide : (2 * k + 2) * wide]
        keep_ref[k] = jnp.where(first, low, high)
        send_ref[k] = jnp.where(first, high, low)


def core_split_grads(at, d, x, wide):
    seq, units = d.shape
    places = max(1, 384 // (2 * wide))
    cols = places * 2 * wide
    out = pl.BlockSpec((places, wide, D), lambda i: (i, 0, 0))
    shape = jax.ShapeDtypeStruct((units // (2 * wide), wide, D), jnp.bfloat16)
    return pl.pallas_call(
        functools.partial(core_split_kernel, wide=wide, places=places),
        grid=(units // cols,),
        in_specs=[pl.BlockSpec(memory_space=pltpu.SMEM), pl.BlockSpec((seq, cols), lambda i: (0, i)),
                  pl.BlockSpec((seq, D), lambda i: (0, 0))],
        out_specs=[out, out],
        out_shape=[shape, shape],
        compiler_params=pltpu.CompilerParams(vmem_limit_bytes=VMEM),
        cost_estimate=cost(8),
    )(at, d, x)


def row_norm(r):
    mean = jnp.mean(r, axis=-1, keepdims=True)
    cen = r - mean
    inv = lax.rsqrt(jnp.mean(cen * cen, axis=-1, keepdims=True) + NORM_EPS)
    return cen * inv, inv


def row_norm_back(cot, n, inv, gain):
    e = cot * gain
    return inv * (e - jnp.mean(e, axis=-1, keepdims=True) - n * jnp.mean(e * n, axis=-1, keepdims=True))


def mix_kernel(c_ref, w_ref, x_ref, mask_ref, small_ref, r_ref, low_ref):
    att = dot(c_ref[...], w_ref[...])
    mixed = jnp.where(mask_ref[...] > 0.5, small_ref[8:9], x_ref[...].astype(jnp.float32))
    r = mixed + att + small_ref[2:3]
    n, _ = row_norm(r)
    r_ref[...] = r
    low_ref[...] = (n * small_ref[3:4] + small_ref[4:5]).astype(jnp.bfloat16)


def mix_out(ctx, w_attn, rounded, mask, small, block=256):
    seq = rounded.shape[0]
    wide = pl.BlockSpec((block, D), lambda i: (i, 0))
    return pl.pallas_call(
        mix_kernel,
        grid=(seq // block,),
        in_specs=[wide, pl.BlockSpec((D, D), lambda i: (0, 0)), wide,
                  pl.BlockSpec((block, 1), lambda i: (i, 0)), pl.BlockSpec((9, D), lambda i: (0, 0))],
        out_specs=[wide, wide],
        out_shape=[jax.ShapeDtypeStruct((seq, D), jnp.float32), jax.ShapeDtypeStruct((seq, D), jnp.bfloat16)],
        compiler_params=pltpu.CompilerParams(vmem_limit_bytes=VMEM),
        cost_estimate=cost(4),
    )(ctx, w_attn, rounded, mask, small)


def gelu_both(x):
    cdf = 0.5 * (1.0 + lax.erf(x * 0.7071067811865476))
    dens = jnp.exp(-0.5 * x * x) * 0.3989422804014327
    return x * cdf, cdf + x * dens


def weight_copies(w_ref, wi_ref, wo_ref, sem):
    owners, own, _ = wi_ref.shape
    per = 768 // own
    copies = []
    for c in range(owners // per):
        here = pl.ds(c * per, per)
        copies.append((
            pltpu.make_async_copy(w_ref.at[here, pl.ds(0, own), :], wi_ref.at[here], sem.at[0, c]),
            pltpu.make_async_copy(w_ref.at[here, pl.ds(own, own), :], wo_ref.at[here], sem.at[1, c]),
        ))
    return per, copies


def by_step(w_ref, wi_ref, wo_ref, sem, body):
    per, copies = weight_copies(w_ref, wi_ref, wo_ref, sem)
    i = pl.program_id(0)

    @pl.when(i == 0)
    def _():
        for pair in copies:
            for copy in pair:
                copy.start()

        def wait(c):
            for copy in copies[c]:
                copy.wait()

        body(per, len(copies), wait)

    @pl.when(i > 0)
    def _():
        body(per, len(copies), lambda c: None)


def ffn_kernel(len_ref, low_ref, w_ref, b_ref, r_ref, cot_ref, small_ref,
               act_ref, slope_ref, out_ref, dres_ref, dlow_ref, red_ref, wi_ref, wo_ref, sem, *, block):
    i = pl.program_id(0)

    @pl.when(i == 0)
    def _():
        red_ref[...] = jnp.zeros_like(red_ref)

    def body(per, chunks, wait):
        low = low_ref[...]
        acc = None
        for c in range(chunks):
            wait(c)
            cols = slice(c * 768, c * 768 + 768)
            hid = dot(low, wi_ref[c * per : c * per + per].reshape(-1, D), NT) + b_ref[:, cols]
            act, slo = gelu_both(hid)
            act = act.astype(jnp.bfloat16)
            act_ref[:, cols] = act
            slope_ref[:, cols] = slo.astype(jnp.bfloat16)
            part = dot(act, wo_ref[c * per : c * per + per].reshape(-1, D))
            acc = part if acc is None else acc + part
        n1, _ = row_norm(r_ref[...])
        first = n1 * small_ref[3:4] + small_ref[4:5]
        n, inv = row_norm(first + (acc + small_ref[7:8]))
        out_ref[...] = n * small_ref[5:6] + small_ref[6:7]
        at = lax.broadcasted_iota(jnp.int32, (block, D), 0) + i * block
        cot = jnp.where(at < len_ref[0], cot_ref[...].astype(jnp.float32), 0.0)
        dres = row_norm_back(cot, n, inv, small_ref[5:6])
        dlow = dres.astype(jnp.bfloat16)
        dres_ref[...] = dres
        dlow_ref[...] = dlow
        for k, v in enumerate((cot * n, cot, dlow.astype(jnp.float32))):
            red_ref[k : k + 1] += jnp.sum(v, axis=0, keepdims=True)

    by_step(w_ref, wi_ref, wo_ref, sem, body)


def ffn_scratch(w_all):
    owners, rows, _ = w_all.shape
    own = (rows - 8) // 2
    return [
        pltpu.VMEM((owners, own, D), jnp.bfloat16),
        pltpu.VMEM((owners, own, D), jnp.bfloat16),
        pltpu.SemaphoreType.DMA((2, owners * own // 768)),
    ]


def ffn_forward(length, low, w_all, bias, r1, cot, small, block=256):
    seq = low.shape[0]
    wide = pl.BlockSpec((block, D), lambda i, n: (i, 0))
    hidden = pl.BlockSpec((block, FF), lambda i, n: (i, 0))
    f32, b16 = jnp.float32, jnp.bfloat16
    return pl.pallas_call(
        functools.partial(ffn_kernel, block=block),
        grid_spec=pltpu.PrefetchScalarGridSpec(
            num_scalar_prefetch=1,
            grid=(seq // block,),
            in_specs=[wide, pl.BlockSpec(memory_space=pl.ANY), pl.BlockSpec((1, FF), lambda i, n: (0, 0)), wide, wide,
                      pl.BlockSpec((9, D), lambda i, n: (0, 0))],
            out_specs=[hidden, hidden, wide, wide, wide, pl.BlockSpec((8, D), lambda i, n: (0, 0))],
            scratch_shapes=ffn_scratch(w_all),
        ),
        out_shape=[jax.ShapeDtypeStruct((seq, FF), b16), jax.ShapeDtypeStruct((seq, FF), b16),
                   jax.ShapeDtypeStruct((seq, D), f32), jax.ShapeDtypeStruct((seq, D), f32),
                   jax.ShapeDtypeStruct((seq, D), b16), jax.ShapeDtypeStruct((8, D), f32)],
        compiler_params=pltpu.CompilerParams(vmem_limit_bytes=VMEM),
        cost_estimate=cost(18),
    )(length, low, w_all, bias, r1, cot, small)


def ffn_back_kernel(dlow_ref, w_ref, slope_ref, dres_ref, r_ref, wa_ref, rl_ref, small_ref,
                    dh_ref, gb_ref, dr1_ref, da_ref, dc_ref, red_ref, wi_ref, wo_ref, sem):
    @pl.when(pl.program_id(0) == 0)
    def _():
        red_ref[...] = jnp.zeros_like(red_ref)
        gb_ref[...] = jnp.zeros_like(gb_ref)

    def body(per, chunks, wait):
        dlow = dlow_ref[...]
        acc = None
        for c in range(chunks):
            wait(c)
            cols = slice(c * 768, c * 768 + 768)
            dh = dot(dlow, wo_ref[c * per : c * per + per].reshape(-1, D), NT) * slope_ref[:, cols].astype(jnp.float32)
            dh = dh.astype(jnp.bfloat16)
            dh_ref[:, cols] = dh
            gb_ref[:, cols] += jnp.sum(dh.astype(jnp.float32), axis=0, keepdims=True)
            part = dot(dh, wi_ref[c * per : c * per + per].reshape(-1, D))
            acc = part if acc is None else acc + part
        n, inv = row_norm(r_ref[...])
        dfirst = dres_ref[...] + acc
        dr1 = row_norm_back(dfirst, n, inv, small_ref[3:4])
        low = dr1.astype(jnp.bfloat16)
        dr1_ref[...] = dr1
        da_ref[...] = low
        dc_ref[...] = (dot(low, wa_ref[...], NT) * rl_ref[...]).astype(jnp.bfloat16)
        for k, v in enumerate((low.astype(jnp.float32), dfirst * n, dfirst)):
            red_ref[k : k + 1] += jnp.sum(v, axis=0, keepdims=True)

    by_step(w_ref, wi_ref, wo_ref, sem, body)


def ffn_backward(dlow, w_all, slope, dres, r1, w_attn, rl, small, block=256):
    seq = dlow.shape[0]
    wide = pl.BlockSpec((block, D), lambda i: (i, 0))
    hidden = pl.BlockSpec((block, FF), lambda i: (i, 0))
    f32, b16 = jnp.float32, jnp.bfloat16
    return pl.pallas_call(
        ffn_back_kernel,
        grid=(seq // block,),
        in_specs=[wide, pl.BlockSpec(memory_space=pl.ANY), hidden, wide, wide,
                  pl.BlockSpec((D, D), lambda i: (0, 0)), wide, pl.BlockSpec((9, D), lambda i: (0, 0))],
        out_specs=[hidden, pl.BlockSpec((1, FF), lambda i: (0, 0)),
                   wide, wide, wide, pl.BlockSpec((8, D), lambda i: (0, 0))],
        out_shape=[jax.ShapeDtypeStruct((seq, FF), b16), jax.ShapeDtypeStruct((1, FF), f32),
                   jax.ShapeDtypeStruct((seq, D), f32), jax.ShapeDtypeStruct((seq, D), b16),
                   jax.ShapeDtypeStruct((seq, D), b16), jax.ShapeDtypeStruct((8, D), f32)],
        scratch_shapes=ffn_scratch(w_all),
        compiler_params=pltpu.CompilerParams(vmem_limit_bytes=VMEM),
        cost_estimate=cost(18),
    )(dlow, w_all, slope, dres, r1, w_attn, rl, small)


def input_kernel(dr_ref, d0_ref, d1_ref, d2_ref, w0_ref, w1_ref, w2_ref, z_ref, wg_ref, mask_ref,
                 fg_ref, red_ref):
    i = pl.program_id(0)
    acc = dr_ref[...] + dot(z_ref[...], wg_ref[...], TN)
    qs, vs = [], []
    for d_ref, w_ref in ((d0_ref, w0_ref), (d1_ref, w1_ref), (d2_ref, w2_ref)):
        for k in range(3):
            acc += dot(d_ref[k], w_ref[k], NT)
        qs.append(jnp.sum(d_ref[0].astype(jnp.float32), axis=0, keepdims=True))
        vs.append(jnp.sum(d_ref[2].astype(jnp.float32), axis=0, keepdims=True))
    masked = mask_ref[...] > 0.5
    fg_ref[...] = jnp.where(masked, 0.0, acc)
    dm = jnp.sum(jnp.where(masked, acc, 0.0), axis=0, keepdims=True)
    red = jnp.concatenate(
        [jnp.concatenate(qs, axis=1), jnp.concatenate(vs, axis=1), dm, jnp.zeros((5, D), jnp.float32)], axis=0
    )

    @pl.when(i == 0)
    def _():
        red_ref[...] = red

    @pl.when(i > 0)
    def _():
        red_ref[...] += red


def input_grad(dr1, ds, ws, dz, wg, mask, block=256):
    seq = dr1.shape[0]
    wide = pl.BlockSpec((block, D), lambda i: (i, 0))
    part = pl.BlockSpec((3, block, 256), lambda i: (0, i, 0))
    wpart = pl.BlockSpec((3, D, 256), lambda i: (0, 0, 0))
    return pl.pallas_call(
        input_kernel,
        grid=(seq // block,),
        in_specs=[wide, part, part, part, wpart, wpart, wpart,
                  pl.BlockSpec((dz.shape[0], block), lambda i: (0, i)),
                  pl.BlockSpec(wg.shape, lambda i: (0, 0)),
                  pl.BlockSpec((block, 1), lambda i: (i, 0))],
        out_specs=[wide, pl.BlockSpec((8, D), lambda i: (0, 0))],
        out_shape=[jax.ShapeDtypeStruct((seq, D), jnp.float32), jax.ShapeDtypeStruct((8, D), jnp.float32)],
        compiler_params=pltpu.CompilerParams(vmem_limit_bytes=VMEM),
        cost_estimate=cost(8),
    )(dr1, *ds, *ws, dz, wg, mask)


def split3(x):
    hi = x.astype(jnp.bfloat16)
    rest = x - hi.astype(jnp.float32)
    mid = rest.astype(jnp.bfloat16)
    low = (rest - mid.astype(jnp.float32)).astype(jnp.bfloat16)
    return hi, mid, low


def tree_sum(parts):
    while len(parts) > 1:
        half = len(parts) // 2
        parts = [parts[i] + parts[i + half] for i in range(half)]
    return parts[0]


def added(parts):
    return sum(p.astype(jnp.float32) for p in parts)


class Net:
    def __init__(self, dp_size, t_size):
        self.t = t_size
        self.sizes = {"z": dp_size // 4, "y": 2, "c": 2, "x": t_size}
        d = lax.axis_index("dp")
        self.at = {"z": d // 4, "y": d // 2 % 2, "c": d % 2, "x": lax.axis_index("tensor")}

    def shift(self, v, axis, k):
        pairs = []
        sz = self.sizes
        for z in range(sz["z"]):
            for y in range(2):
                for c in range(2):
                    for x in range(sz["x"]):
                        src = {"z": z, "y": y, "c": c, "x": x}
                        dst = dict(src)
                        dst[axis] = (src[axis] - k) % sz[axis]
                        flat = [((q["z"] * 2 + q["y"]) * 2 + q["c"]) * sz["x"] + q["x"] for q in (src, dst)]
                        pairs.append(tuple(flat))
        return lax.ppermute(v, ("dp", "tensor"), pairs)

    def gather(self, v, axis, dim):
        return jnp.concatenate([v] + [self.shift(v, axis, k) for k in range(1, self.sizes[axis])], axis=dim)

    def scatter(self, parts, axis, dim):
        n = self.sizes[axis]
        at = self.at[axis]

        def slot(i):
            return [lax.dynamic_index_in_dim(p, i, dim, False) for p in parts]

        arrived = []
        for k in range(1, n):
            send = added(slot((at + k) % n)).astype(jnp.bfloat16)
            arrived.append(self.shift(send, axis, n - k))
        return slot(at), arrived

    def gather_own(self, v, axis, dim):
        n = self.sizes[axis]
        at = self.at[axis]
        out = jnp.zeros(v.shape[:dim] + (n,) + v.shape[dim:], v.dtype)
        for k in range(n):
            part = v if k == 0 else self.shift(v, axis, k)
            out = lax.dynamic_update_index_in_dim(out, part, (at + k) % n, dim)
        return out

    def total(self, v, axes=("c", "x", "y", "z")):
        for axis in axes:
            v = tree_sum([v] + [self.shift(v, axis, k) for k in range(1, self.sizes[axis])])
        return v


def rolled(net, v, dims, sign):
    for dim, axis in dims:
        v = jnp.roll(v, sign * net.at[axis], dim)
    return v


def natural(net, places, mine, peer):
    if mine.shape[3] % 16 == 0:
        return assemble(places, mine, peer)
    v = rolled(net, jnp.stack([mine, peer])[:, :, :, 3:], ((0, "c"), (1, "y"), (2, "z")), 1)
    return v.transpose(2, 1, 0, 4, 3, 5).reshape(D, D)


def wide_rows(net, places, mine, peer):
    if mine.shape[3] % 16 == 0:
        return places, mine, peer
    zs, kinds, cols = net.sizes["z"], mine.shape[2], mine.shape[4]
    v = rolled(net, jnp.stack([mine, peer]), ((0, "c"), (1, "y"), (2, "z")), 1)
    v = v.transpose(2, 1, 0, 4, 3, 5)
    v = v.reshape(1, 2, 2, -1, kinds, cols).transpose(2, 1, 0, 4, 3, 5)
    return places * 0, v[0], v[1]


def local(dp_size, t_size, features, lengths, span_starts, buckets, cotangent,
          qkv_w, qkv_m, qkv_v, out_w, out_m, out_v, ffn_in, ffn_in_m, ffn_in_v,
          ffn_out, ffn_out_m, ffn_out_v, small_params, small_m, small_v,
          pos_table, pos_m, pos_v, gate_proj, gate_m, gate_v, step_count):
    f32, b16 = jnp.float32, jnp.bfloat16
    net = Net(dp_size, t_size)
    zs = net.sizes["z"]
    seq = features.shape[1]
    own = ffn_out.shape[0]
    rows = qkv_w.shape[1]
    scale = HD**-0.5

    bar = lax.optimization_barrier
    places = jnp.stack([net.at["z"], net.at["y"], net.at["c"], net.at["x"]]).astype(jnp.int32)
    cols = D // GROUPS
    group_heads = H // GROUPS
    both = ("dp", "tensor")

    bias_row = jnp.pad(ffn_in[D:].astype(b16), ((0, 7), (0, D - own)))
    ffn_own = jnp.concatenate([ffn_in[:D].T.astype(b16), ffn_out.astype(b16), bias_row])

    qkv_low = qkv_w.astype(b16)[None, None]
    u0, u1, u2 = [qkv_low[..., g * cols : (g + 1) * cols] for g in range(3)]
    out_parts = out_w.astype(b16).reshape(rows, 3, cols).transpose(1, 0, 2)[None, None]
    u2 = jnp.concatenate([u2, out_parts], axis=2)
    positions = jnp.arange(seq, dtype=jnp.int32)
    starts = span_starts[0]
    masked = jnp.any((positions[:, None] >= starts[None, :]) & (positions[:, None] < starts[None, :] + SPAN), axis=1)[:, None]
    mask = masked.astype(f32)
    rounded = jnp.where(masked, small_params[8][None, :].astype(b16), features[0])
    z0 = net.gather(u0, "z", 1)
    z0, u1, u2, rounded, mask, buckets = bar((z0, u1, u2, rounded, mask, buckets))

    y0 = net.gather(z0, "y", 0)
    z1 = net.gather(u1, "z", 1)
    rev = jnp.flip(buckets)
    order = jnp.concatenate([rev[127:], jnp.full((1,), -1, jnp.int32), rev[:127]])
    onehot = (jnp.arange(NB, dtype=jnp.int32)[:, None] == order[None, :]).astype(b16)
    off3 = dot(jnp.concatenate(split3(pos_table[:NB].T), axis=0), onehot).reshape(3, H, 2 * seq)
    table = bias_tables(off3[0] + off3[1] + off3[2])
    y0, z1, u2, table, rounded, ffn_own = bar((y0, z1, u2, table, rounded, ffn_own))

    w_all = lax.all_gather(ffn_own, both, axis=0)
    w_all_k = w_all
    if own % 16:
        w_all_k = jnp.concatenate(
            [w_all[:, k * own : (k + 1) * own].reshape(4, -1, D) for k in range(2)] + [jnp.zeros((4, 8, D), b16)], axis=1)

    p0 = net.shift(y0, "c", 1)
    ga = jnp.sum(gate_proj[:HD, :4], axis=1)
    gb = jnp.sum(gate_proj[:HD, 4:], axis=1)
    za = jnp.sum(gate_proj[HD, :4])
    zb = jnp.sum(gate_proj[HD, 4:])
    eye = jnp.eye(H, dtype=f32)[:, :, None]
    wg = jnp.concatenate([(eye * ga).reshape(H, D), (eye * gb).reshape(H, D)], axis=0)
    wg3 = split3(wg)
    z3 = dot(jnp.concatenate(wg3, axis=0), rounded, NT).reshape(3, 2 * H, seq)
    z_all = z3[0] + z3[1] + z3[2]
    gate_a = jax.nn.sigmoid(z_all[:H] + za)
    gate_b = jax.nn.sigmoid(z_all[H:] + zb)
    const = pos_table[NB][:, None]
    gates = (gate_a * (gate_b * const - 1.0) + 2.0).reshape(H, 1, seq)
    rounded_t = rounded.T
    bias3 = jnp.stack([small_params[0], jnp.zeros((D,), f32), small_params[1]])[:, None, :]

    def attend(g, mine, peer, kept):
        at, mine, peer = wide_rows(net, places, mine, peer)
        bias = bias3[:, :, g * cols : (g + 1) * cols]
        return attn_fwd(lengths, at, rounded, mine, peer, bias, table, gates, g * group_heads, group_heads, kept)

    p0, z1, u2, gates, rounded_t = bar((p0, z1, u2, gates, rounded_t))
    y1 = net.gather(z1, "y", 0)
    z2 = net.gather(u2, "z", 1)
    probs0, *kept, q0, w0 = attend(0, y0, p0, ())
    y1, z2, probs0, q0, w0, *kept = bar((y1, z2, probs0, q0, w0, *kept))
    p1 = net.shift(y1, "c", 1)
    y2 = net.gather(z2, "y", 0)
    probs1, *kept, q1, w1 = attend(1, y1, p1, kept)
    y2, probs1, q1, w1, *kept = bar((y2, probs1, q1, w1, *kept))
    p2 = net.shift(y2, "c", 1)
    w_attn = natural(net, places, y2, p2)
    probs2, context, context_f, inv_sum, q2, w2 = attend(2, y2, p2, kept)
    qkv, w_qkv, probs = (q0, q1, q2), (w0, w1, w2), (probs0, probs1, probs2)
    r1, low = mix_out(context, w_attn, rounded, mask, small_params)

    bias_in = w_all[:, 2 * own, :own].reshape(1, -1).astype(f32)
    act, slope, layer_out, d_res2, d_branch, red2 = ffn_forward(
        lengths, low, w_all_k, bias_in, r1, cotangent[0], small_params)
    g_outw = dot(act, d_branch, TN).astype(b16)
    g_outw, d_branch = bar((g_outw, d_branch))
    g_outw = lax.psum_scatter(g_outw, both, scatter_dimension=0, tiled=True)
    d_hidden, g_bias_in, d_res1, d_attention, d_context, red1 = ffn_backward(
        d_branch, w_all_k, slope, d_res2, r1, w_attn, inv_sum, small_params)

    def attend_back(g):
        return attn_bwd(qkv[g], d_context, context_f, probs[g], table, gates, g * group_heads, group_heads)

    def by_owner(v):
        return v.reshape(zs, 2, 2, rows, v.shape[-1])

    g_keep, g_send = core_split_grads(places, d_hidden, low, t_size * own)
    g_got = net.shift(g_send, "c", 1)
    d0, dg0, do0 = attend_back(0)
    g_keep, g_got, d0, dg0, do0, d_context = bar((g_keep, g_got, d0, dg0, do0, d_context))
    gi = [v.reshape(zs, 2, t_size, own, D) for v in (g_keep, g_got)]
    part_a = [v[..., : own // 2, :] for v in gi]
    part_b = [v[..., own // 2 :, :] for v in gi]
    stay_a, got_a = net.scatter(part_a, "y", 1)
    stay_b, got_b = net.scatter(part_b, "x", 2)
    m1 = by_owner(weight_grads(rounded_t, d0, context, d_attention))
    stay_1, got_1 = net.scatter([m1], "c", 2)
    d1, dg1, do1 = attend_back(1)
    got_a, got_b, got_1, d1, dg1, do1, d_context = bar((got_a, got_b, got_1, d1, dg1, do1, d_context))
    stay_a, got_a = net.scatter(stay_a + got_a, "x", 1)
    stay_b, got_b = net.scatter(stay_b + got_b, "y", 1)
    stay_1, got_1 = net.scatter(stay_1 + got_1, "y", 1)
    d2, dg2, do2 = attend_back(2)
    got_a, got_b, got_1, d2, dg2, do2, g_outw = bar((got_a, got_b, got_1, d2, dg2, do2, g_outw))
    gi = jnp.concatenate([added(stay_a + got_a), added(stay_b + got_b)], axis=1).astype(b16)
    stay_i, got_i = net.scatter([gi], "z", 0)
    stay_1, got_1 = net.scatter(stay_1 + got_1, "z", 0)
    m2 = by_owner(weight_grads(rounded_t, d1, d2, jnp.zeros((8, 128), f32)))
    stay_2, got_2 = net.scatter([m2], "c", 2)

    dgate = jnp.concatenate([dg0, dg1, dg2], axis=0).reshape(H, seq)
    doff = jnp.concatenate([do0, do1, do2], axis=0).reshape(H, 2 * seq)
    d_a = dgate * (gate_b * const - 1.0) * gate_a * (1.0 - gate_a)
    d_b = dgate * gate_a * const * gate_b * (1.0 - gate_b)
    d_const = jnp.sum(dgate * gate_a * gate_b, axis=1)
    dz = jnp.concatenate([d_a, d_b], axis=0)
    dz_hi = dz.astype(b16)
    dz_lo = (dz - dz_hi.astype(f32)).astype(b16)
    feature_grad, red0 = input_grad(
        d_res1, (d0, d1, d2), w_qkv, jnp.concatenate([dz_hi, dz_lo, dz_hi], axis=0),
        jnp.concatenate([wg3[0], wg3[0], wg3[1]], axis=0), mask)
    g_z2 = dot(jnp.concatenate([dz_hi, dz_lo], axis=0), rounded).reshape(2, 2, H, H, HD)
    g_z = jnp.sum((g_z2[0] + g_z2[1]) * eye, axis=(1, 2))
    g_zb = jnp.sum(dz.reshape(2, H * seq), axis=1)
    g_gate_local = jnp.repeat(jnp.concatenate([g_z, g_zb[:, None]], axis=1).T, 4, axis=1)
    pos3 = dot(onehot, jnp.concatenate(split3(doff), axis=0), NT).reshape(NB, 3, H)
    pos_local = jnp.concatenate([jnp.sum(pos3, axis=1), d_const[None, :]], axis=0)
    small_local = jnp.concatenate([red0[:2], red1[:3], red2[:3], red0[2:3]], axis=0)

    got_i, got_1, got_2, feature_grad, small_local, pos_local, g_gate_local = bar(
        (got_i, got_1, got_2, feature_grad, small_local, pos_local, g_gate_local))
    g_in = added(stay_i + got_i)
    g_outw = g_outw.astype(f32)
    stay_2, got_2 = net.scatter(stay_2 + got_2, "y", 1)
    own_ffn = jnp.sum(jnp.square(g_in)) + jnp.sum(jnp.square(g_outw))
    m1 = added(stay_1 + got_1)
    got_2, own_ffn, m1 = bar((got_2, own_ffn, m1))
    stay_2, got_2 = net.scatter(stay_2 + got_2, "z", 0)
    m = jnp.stack([m1, added(stay_2 + got_2)]).astype(b16)
    m = tree_sum([m.astype(f32)] + [net.shift(m, "x", k).astype(f32) for k in range(1, t_size)])
    own_sum = jnp.sum(jnp.square(m)) * (1.0 / t_size) + own_ffn
    parts = [small_local, pos_local, g_gate_local, g_bias_in]
    counts = [p.size for p in parts]
    pad = -(sum(counts) + 1) % 1024
    flat = jnp.concatenate(
        [p.reshape(-1) for p in parts] + [own_sum.reshape(1), jnp.zeros((pad,), f32)]).reshape(-1, 128)
    flat = net.total(flat).reshape(-1)
    own_sum = flat[sum(counts)]
    m = m.reshape(2, rows, 2, 3, cols)
    g_qkv = jnp.stack([m[0, :, 0], m[1, :, 0], m[1, :, 1]], axis=2).transpose(1, 0, 2, 3).reshape(3, rows, D)
    g_out = m[0, :, 1].reshape(rows, D)
    pieces, at = [], 0
    for p, count in zip(parts, counts):
        pieces.append(flat[at : at + count].reshape(p.shape))
        at += count
    g_small, g_pos, g_gate, g_bias = pieces
    shared = sum(jnp.sum(jnp.square(p)) for p in pieces)
    grad_norm = jnp.sqrt(own_sum + shared)
    clip = jnp.minimum(1.0, CLIP_NORM / (grad_norm + 1e-06))
    count = step_count[0].astype(f32)
    me = lax.axis_index("dp") * t_size + lax.axis_index("tensor")
    g_bias = lax.dynamic_slice_in_dim(g_bias.reshape(-1, own), me, 1, 0)
    g_ffn_in = jnp.concatenate([g_in.T, g_bias], axis=0)

    qkv_new, qkv_moment, qkv_second = adam_step(qkv_w, g_qkv, qkv_m, qkv_v, clip, 2.0 * D**-0.5, count)
    out_new, out_moment, out_second = adam_step(out_w, g_out, out_m, out_v, clip, 1.0, count)
    in_new, in_moment, in_second = adam_step(ffn_in, g_ffn_in, ffn_in_m, ffn_in_v, clip, 2.0 * D**-0.5, count)
    fo_new, fo_moment, fo_second = adam_step(ffn_out, g_outw, ffn_out_m, ffn_out_v, clip, 2.0 * FF**-0.5, count)
    small_new, small_moment, small_second = adam_step(small_params, g_small, small_m, small_v, clip, 0.5, count)
    pos_new, pos_moment, pos_second = adam_step(pos_table, g_pos, pos_m, pos_v, clip, 1.0, count)
    gate_new, gate_moment, gate_second = adam_step(gate_proj, g_gate, gate_m, gate_v, clip, 2.0 * HD**-0.5, count)
    return (
        layer_out[None], feature_grad[None], grad_norm.reshape(1),
        qkv_new, qkv_moment, qkv_second, qkv_new.astype(b16),
        out_new, out_moment, out_second, out_new.astype(b16),
        in_new, in_moment, in_second, in_new.astype(b16),
        fo_new, fo_moment, fo_second, fo_new.astype(b16),
        g_small, small_new, small_moment, small_second,
        pos_new, pos_moment, pos_second, gate_new, gate_moment, gate_second,
    )


def solution(mesh):
    both = ("dp", "tensor")
    three = (P(None, "dp", None),)
    row = (P("dp", None),)
    col = (P(None, both),)
    rows2 = (P(both, None),)
    utt = P(both, None, None)
    in_specs = (
        (utt, P(both), P(both, None), P(), utt) + three * 3 + row * 3 + col * 3 + rows2 * 3 + (P(),) * 10
    )
    out_specs = (utt, utt, P()) + three * 4 + row * 4 + col * 4 + rows2 * 4 + (P(),) * 10
    fn = functools.partial(local, mesh.shape["dp"], mesh.shape["tensor"])
    return jax.shard_map(fn, mesh=mesh, in_specs=in_specs, out_specs=out_specs, check_vma=False)
```

```python
import functools

import jax
import jax.numpy as jnp
from jax import lax
from jax.experimental import pallas as pl
from jax.experimental.pallas import tpu as pltpu
from jax.sharding import PartitionSpec as P

D = 768
H = 12
HD = 64
FF = 3072
NB = 320
SPAN = 10
CLIP_NORM = 1.0
BETA_ONE = 0.9
BETA_TWO = 0.98
ADAM_EPS = 1e-08
DECAY_RATE = 0.01
NORM_EPS = 1e-05
NEG_BIG = -1e30
GROUPS = 3


def adam_step(weight, grad_in, moment, second, clip_factor, rate_in, count_in):
    scaled = grad_in * clip_factor
    new_moment = BETA_ONE * moment + (1.0 - BETA_ONE) * scaled
    new_second = BETA_TWO * second + (1.0 - BETA_TWO) * scaled * scaled
    first_fix = 1.0 - BETA_ONE**count_in
    second_fix = 1.0 - BETA_TWO**count_in
    update = new_moment / first_fix / (jnp.sqrt(new_second / second_fix) + ADAM_EPS)
    return (weight - rate_in * (update + DECAY_RATE * weight), new_moment, new_second)


VMEM = 60 << 20
NT = (((1,), (1,)), ((), ()))
TN = (((0,), (0,)), ((), ()))


def dot(a, b, dims=(((1,), (0,)), ((), ()))):
    return lax.dot_general(a, b, dims, preferred_element_type=jnp.float32)


def cost(us):
    return pl.CostEstimate(flops=0, bytes_accessed=int(us * 3.0e6), transcendentals=0)


def table_kernel(off_ref, out_ref):
    heads, _, w = out_ref.shape
    for h in range(heads):
        row = jnp.broadcast_to(off_ref[h], (8, w))
        eight = pltpu.roll(row, 0, 1, stride=1, stride_axis=0)
        for r in range(0, 128, 8):
            out_ref[h, r : r + 8] = pltpu.roll(eight, r, 1) if r else eight


def bias_tables(offr, heads=4):
    n, w = offr.shape
    return pl.pallas_call(
        table_kernel,
        grid=(n // heads,),
        in_specs=[pl.BlockSpec((heads, 1, w), lambda h: (h, 0, 0))],
        out_specs=pl.BlockSpec((heads, 128, w), lambda h: (h, 0, 0)),
        out_shape=jax.ShapeDtypeStruct((n, 128, w), jnp.float32),
        compiler_params=pltpu.CompilerParams(vmem_limit_bytes=VMEM),
        cost_estimate=cost(8),
    )(offr.reshape(n, 1, w))


def assemble_kernel(at_ref, mine_ref, peer_ref, out_ref, sem, *, zs, rows, cols):
    z0, y0, c0 = at_ref[0], at_ref[1], at_ref[2]
    copies = []
    for c, src in enumerate((mine_ref, peer_ref)):
        for y in range(2):
            for z in range(zs):
                block = (lax.rem(z0 + z, zs) * 2 + lax.rem(y0 + y, 2)) * 2 + lax.rem(c0 + c, 2)
                first = pl.multiple_of(block * rows, rows)
                for k in range(3):
                    there = out_ref.at[pl.ds(first, rows), pl.ds(k * cols, cols)]
                    copies.append(pltpu.make_async_copy(src.at[y, z, 3 + k], there, sem.at[len(copies)]))
    for copy in copies:
        copy.start()
    for copy in copies:
        copy.wait()


def assemble(at, mine, peer):
    _, zs, _, rows, cols = mine.shape
    hbm = pl.BlockSpec(memory_space=pl.ANY)
    return pl.pallas_call(
        functools.partial(assemble_kernel, zs=zs, rows=rows, cols=cols),
        in_specs=[pl.BlockSpec(memory_space=pltpu.SMEM), hbm, hbm],
        out_specs=pl.BlockSpec(memory_space=pltpu.VMEM),
        scratch_shapes=[pltpu.SemaphoreType.DMA((12 * zs,))],
        out_shape=jax.ShapeDtypeStruct((D, D), jnp.bfloat16),
        compiler_params=pltpu.CompilerParams(vmem_limit_bytes=VMEM),
        cost_estimate=cost(2),
    )(at, mine, peer)


def fwd_kernel(len_ref, at_ref, x_ref, mine_ref, peer_ref, bias_ref, t_ref, g_ref, *rest, seq, ib, zs, rows, kept):
    p_ref, o_ref, of_ref, rl_ref, qkv_ref, w_ref, s_ref, sem = rest[kept:]
    h = pl.program_id(0)

    @pl.when(h == 0)
    def _():
        z0, y0, c0 = at_ref[0], at_ref[1], at_ref[2]
        copies = []
        for c, src in enumerate((mine_ref, peer_ref)):
            for y in range(2):
                for z in range(zs):
                    block = (lax.rem(z0 + z, zs) * 2 + lax.rem(y0 + y, 2)) * 2 + lax.rem(c0 + c, 2)
                    first = pl.multiple_of(block * rows, rows)
                    there = w_ref.at[:, pl.ds(first, rows), :]
                    copies.append(pltpu.make_async_copy(src.at[y, z, pl.ds(0, 3)], there, sem.at[len(copies)]))
        for copy in copies:
            copy.start()
        for copy in copies:
            copy.wait()
        for k in range(3):
            r = dot(x_ref[...], w_ref[k]) + bias_ref[k]
            qkv_ref[k] = (r * HD**-0.5 if k == 0 else r).astype(jnp.bfloat16)

    par = lax.rem(h, 2)
    lane = lax.broadcasted_iota(jnp.int32, (seq, 128), 1)
    rowi = lax.broadcasted_iota(jnp.int32, (seq, 128), 0)
    inh = (lane // 64) == par
    flag = lane == (64 * (1 - par))
    one = jnp.bfloat16(1.0)
    zero = jnp.bfloat16(0.0)
    pair = pl.ds(pl.multiple_of(h // 2 * 128, 128), 128)
    bias = jnp.where(rowi < len_ref[0], 0.0, NEG_BIG).astype(jnp.bfloat16)
    qm = jnp.where(flag, one, jnp.where(inh, qkv_ref[0, :, pair], zero))
    km = jnp.where(flag, bias, qkv_ref[1, :, pair])
    vm = jnp.where(flag, one, qkv_ref[2, :, pair])
    vt = vm.T
    base = seq - 128
    def scores(i0):
        gate = g_ref[0, :, i0 : i0 + ib]
        qb = qm[i0 : i0 + ib]
        m = None
        for j0 in range(0, seq, 128):
            c0 = i0 - j0 + base
            s = dot(km[j0 : j0 + 128], qb, NT) + t_ref[0, :, c0 : c0 + ib] * gate
            s_ref[i0 // ib % 2, j0 : j0 + 128, :] = s
            mm = jnp.max(s.reshape(16, 8, ib), axis=0)
            m = mm if m is None else jnp.maximum(m, mm)
        return jnp.max(m, axis=0, keepdims=True)

    m = scores(0)
    for i0 in range(0, seq, ib):
        m_next = scores(i0 + ib) if i0 + ib < seq else None
        for j0 in range(0, seq, 128):
            e = jnp.exp(s_ref[i0 // ib % 2, j0 : j0 + 128, :] - m).astype(jnp.bfloat16)
            p_ref[0, j0 : j0 + 128, i0 : i0 + ib] = e
        m = m_next
        ct = dot(vt, p_ref[0, :, i0 : i0 + ib])
        total = jnp.where(par == 0, ct[64:65], ct[0:1])
        rl = 1.0 / total
        oc = (ct * rl).T
        rc = jnp.broadcast_to(rl, (128, ib)).T
        ih = inh[i0 : i0 + ib]
        o_ref[i0 : i0 + ib, :] = jnp.where(ih, oc.astype(jnp.bfloat16), o_ref[i0 : i0 + ib, :])
        of_ref[i0 : i0 + ib, :] = jnp.where(ih, oc, of_ref[i0 : i0 + ib, :])
        rl_ref[i0 : i0 + ib, :] = jnp.where(ih, rc, rl_ref[i0 : i0 + ib, :])


def attn_fwd(length, at, x, mine, peer, bias, table, gates, head0, heads, kept, ib=256):
    seq = x.shape[0]
    _, zs, _, rows, cols = mine.shape
    w = table.shape[-1]
    f32, b16 = jnp.float32, jnp.bfloat16
    out_pair = pl.BlockSpec((seq, 128), lambda h, n, a: (0, head0 // 2 + h // 2))
    hbm = pl.BlockSpec(memory_space=pl.ANY)
    return pl.pallas_call(
        functools.partial(fwd_kernel, seq=seq, ib=ib, zs=zs, rows=rows, kept=len(kept)),
        grid_spec=pltpu.PrefetchScalarGridSpec(
            num_scalar_prefetch=2,
            grid=(heads,),
            in_specs=[
                pl.BlockSpec((seq, D), lambda h, n, a: (0, 0)),
                hbm,
                hbm,
                pl.BlockSpec((3, 1, cols), lambda h, n, a: (0, 0, 0)),
                pl.BlockSpec((1, 128, w), lambda h, n, a: (head0 + h, 0, 0)),
                pl.BlockSpec((1, 1, seq), lambda h, n, a: (head0 + h, 0, 0)),
            ] + [hbm] * len(kept),
            out_specs=[pl.BlockSpec((1, seq, seq), lambda h, n, a: (h, 0, 0)), out_pair, out_pair, out_pair,
                       pl.BlockSpec((3, seq, cols), lambda h, n, a: (0, 0, 0)),
                       pl.BlockSpec((3, D, cols), lambda h, n, a: (0, 0, 0))],
            scratch_shapes=[pltpu.VMEM((2, seq, ib), f32), pltpu.SemaphoreType.DMA((4 * zs,))],
        ),
        out_shape=[jax.ShapeDtypeStruct((heads, seq, seq), b16), jax.ShapeDtypeStruct((seq, D), b16),
                   jax.ShapeDtypeStruct((seq, D), f32), jax.ShapeDtypeStruct((seq, D), f32),
                   jax.ShapeDtypeStruct((3, seq, cols), b16), jax.ShapeDtypeStruct((3, D, cols), b16)],
        input_output_aliases={8: 1, 9: 2, 10: 3} if kept else {},
        compiler_params=pltpu.CompilerParams(vmem_limit_bytes=VMEM),
        cost_estimate=cost(2.7 * heads + 4),
    )(length, at, x, mine, peer, bias, table, gates, *kept)


def bwd_kernel(q_ref, k_ref, v_ref, dc_ref, c_ref, p_ref, t_ref, g_ref, d_ref, dg_ref, do_ref, a_ref, ds_ref, *, seq, ib):
    par = lax.rem(pl.program_id(0), 2)
    lane = lax.broadcasted_iota(jnp.int32, (seq, 128), 1)
    inh = (lane // 64) == par
    f0 = lane == (64 * (1 - par))
    f1 = lane == (64 * (1 - par) + 1)
    one = jnp.bfloat16(1.0)
    dc = dc_ref[...]
    dcf = jnp.where(inh, dc.astype(jnp.float32), 0.0)
    delta = -jnp.sum(dcf * c_ref[...], axis=1, keepdims=True)
    hi = delta.astype(jnp.bfloat16).astype(jnp.float32)
    lo = delta - hi
    dca = jnp.where(f0, hi, jnp.where(f1, lo, dcf)).astype(jnp.bfloat16)
    va = jnp.where(f0 | f1, one, v_ref[0])
    kt = k_ref[0].T
    q = q_ref[0]
    base = seq - 128
    a_ref[...] = jnp.zeros_like(a_ref)
    for i0 in range(0, seq, ib):
        gate = g_ref[0, :, i0 : i0 + ib]
        dcb = dca[i0 : i0 + ib]
        dg = jnp.zeros((8, ib), jnp.float32)
        for j0 in range(0, seq, 128):
            c0 = i0 - j0 + base
            ds = dot(va[j0 : j0 + 128], dcb, NT) * p_ref[0, j0 : j0 + 128, i0 : i0 + ib].astype(jnp.float32)
            ds_ref[j0 : j0 + 128, i0 : i0 + ib] = ds.astype(jnp.bfloat16)
            dg = dg + jnp.sum((ds * t_ref[0, :, c0 : c0 + ib]).reshape(16, 8, ib), axis=0)
            a_ref[:, c0 : c0 + ib] += ds * gate
        dg_ref[0, :, i0 : i0 + ib] = jnp.sum(dg, axis=0, keepdims=True)
        dqt = dot(kt, ds_ref[:, i0 : i0 + ib]).T * HD**-0.5
        d_ref[0, i0 : i0 + ib, :] = jnp.where(inh[i0 : i0 + ib], dqt.astype(jnp.bfloat16), d_ref[0, i0 : i0 + ib, :])
    dk = dot(ds_ref[...], q)
    d_ref[1] = jnp.where(inh, dk.astype(jnp.bfloat16), d_ref[1])
    dv = dot(p_ref[0], dc)
    d_ref[2] = jnp.where(inh, dv.astype(jnp.bfloat16), d_ref[2])
    a = a_ref[...]
    w = a.shape[1]
    r = 64
    while r >= 8:
        a = a[:r] + pltpu.roll(a[r:], w - r, 1)
        r //= 2
    acc = a[0:1]
    for r in range(1, 8):
        acc = acc + pltpu.roll(a[r : r + 1], w - r, 1)
    do_ref[0] = acc


def attn_bwd(qkv, dctx, ctx, probs, table, gates, head0, heads, ib=256):
    seq = qkv.shape[1]
    w = table.shape[-1]

    def part(k):
        return pl.BlockSpec((1, seq, 128), lambda h: (k, 0, h // 2))

    pair = pl.BlockSpec((seq, 128), lambda h: (0, head0 // 2 + h // 2))
    return pl.pallas_call(
        functools.partial(bwd_kernel, seq=seq, ib=ib),
        grid=(heads,),
        in_specs=[
            part(0),
            part(1),
            part(2),
            pair,
            pair,
            pl.BlockSpec((1, seq, seq), lambda h: (h, 0, 0)),
            pl.BlockSpec((1, 128, w), lambda h: (head0 + h, 0, 0)),
            pl.BlockSpec((1, 1, seq), lambda h: (head0 + h, 0, 0)),
        ],
        out_specs=[
            pl.BlockSpec((3, seq, 128), lambda h: (0, 0, h // 2)),
            pl.BlockSpec((1, 1, seq), lambda h: (h, 0, 0)),
            pl.BlockSpec((1, 1, w), lambda h: (h, 0, 0)),
        ],
        scratch_shapes=[pltpu.VMEM((128, w), jnp.float32), pltpu.VMEM((seq, seq), jnp.bfloat16)],
        out_shape=[
            jax.ShapeDtypeStruct((3, seq, heads * HD), jnp.bfloat16),
            jax.ShapeDtypeStruct((heads, 1, seq), jnp.float32),
            jax.ShapeDtypeStruct((heads, 1, w), jnp.float32),
        ],
        compiler_params=pltpu.CompilerParams(vmem_limit_bytes=VMEM),
        cost_estimate=cost(3.0 * heads),
    )(qkv, qkv, qkv, dctx, ctx, probs, table, gates)


def wgrad_kernel(xt_ref, d_ref, a_ref, b_ref, g_ref, *, pair):
    xt = xt_ref[...]
    for k in range(3):
        g_ref[:, k * 256 : k * 256 + 256] = dot(xt, d_ref[k]).astype(jnp.bfloat16)
    if pair:
        g_ref[:, 768:1536] = dot(a_ref[...], b_ref[...], TN).astype(jnp.bfloat16)
    else:
        for k in range(3):
            g_ref[:, 768 + k * 256 : 1024 + k * 256] = dot(xt, a_ref[k]).astype(jnp.bfloat16)


def weight_grads(xt, d3, a, b, block=256):
    seq = xt.shape[1]
    pair = a.ndim == 2
    kinds = pl.BlockSpec((3, seq, 256), lambda i: (0, 0, 0))
    a_spec = pl.BlockSpec((seq, block), lambda i: (0, i)) if pair else kinds
    b_spec = pl.BlockSpec((seq, D), lambda i: (0, 0)) if pair else pl.BlockSpec((8, 128), lambda i: (0, 0))
    return pl.pallas_call(
        functools.partial(wgrad_kernel, pair=pair),
        grid=(D // block,),
        in_specs=[pl.BlockSpec((block, seq), lambda i: (i, 0)), kinds, a_spec, b_spec],
        out_specs=pl.BlockSpec((block, 2 * D), lambda i: (i, 0)),
        out_shape=jax.ShapeDtypeStruct((D, 2 * D), jnp.bfloat16),
        compiler_params=pltpu.CompilerParams(vmem_limit_bytes=VMEM),
        cost_estimate=cost(5),
    )(xt, d3, a, b)


def ffn_grad_kernel(dh_ref, act_ref, low_ref, dlow_ref, g_ref):
    per, two, _ = g_ref.shape
    own = two // 2
    g_ref[:, :own] = dot(dh_ref[...], low_ref[...], TN).astype(jnp.bfloat16).reshape(per, own, D)
    g_ref[:, own:] = dot(act_ref[...], dlow_ref[...], TN).astype(jnp.bfloat16).reshape(per, own, D)


def ffn_grads(dh, act, low, dlow, own, cols=768):
    seq = dh.shape[0]
    if own % 16:
        parts = [dot(a, b, TN).astype(jnp.bfloat16).reshape(-1, own, D) for a, b in ((dh, low), (act, dlow))]
        return jnp.concatenate(parts, axis=1)
    hidden = pl.BlockSpec((seq, cols), lambda i: (0, i))
    wide = pl.BlockSpec((seq, D), lambda i: (0, 0))
    return pl.pallas_call(
        ffn_grad_kernel,
        grid=(FF // cols,),
        in_specs=[hidden, hidden, wide, wide],
        out_specs=pl.BlockSpec((cols // own, 2 * own, D), lambda i: (i, 0, 0)),
        out_shape=jax.ShapeDtypeStruct((FF // own, 2 * own, D), jnp.bfloat16),
        compiler_params=pltpu.CompilerParams(vmem_limit_bytes=VMEM),
        cost_estimate=cost(16),
    )(dh, act, low, dlow)


def row_norm(r):
    mean = jnp.mean(r, axis=-1, keepdims=True)
    cen = r - mean
    inv = lax.rsqrt(jnp.mean(cen * cen, axis=-1, keepdims=True) + NORM_EPS)
    return cen * inv, inv


def row_norm_back(cot, n, inv, gain):
    e = cot * gain
    return inv * (e - jnp.mean(e, axis=-1, keepdims=True) - n * jnp.mean(e * n, axis=-1, keepdims=True))


def gelu_both(x):
    cdf = 0.5 * (1.0 + lax.erf(x * 0.7071067811865476))
    dens = jnp.exp(-0.5 * x * x) * 0.3989422804014327
    return x * cdf, cdf + x * dens


def weight_copies(w_ref, wi_ref, wo_ref, sem):
    owners, own, _ = wi_ref.shape
    per = 768 // own
    copies = []
    for c in range(owners // per):
        here = pl.ds(c * per, per)
        copies.append((
            pltpu.make_async_copy(w_ref.at[here, pl.ds(0, own), :], wi_ref.at[here], sem.at[0, c]),
            pltpu.make_async_copy(w_ref.at[here, pl.ds(own, own), :], wo_ref.at[here], sem.at[1, c]),
        ))
    return per, copies


def by_step(w_ref, wi_ref, wo_ref, sem, body):
    per, copies = weight_copies(w_ref, wi_ref, wo_ref, sem)
    i = pl.program_id(0)

    @pl.when(i == 0)
    def _():
        for pair in copies:
            for copy in pair:
                copy.start()

        def wait(c):
            for copy in copies[c]:
                copy.wait()

        body(per, len(copies), wait)

    @pl.when(i > 0)
    def _():
        body(per, len(copies), lambda c: None)


def ffn_scratch(w_all, block):
    owners, rows, _ = w_all.shape
    own = (rows - 8) // 2
    return [
        pltpu.VMEM((owners, own, D), jnp.bfloat16),
        pltpu.VMEM((owners, own, D), jnp.bfloat16),
        pltpu.VMEM((block, FF), jnp.bfloat16),
        pltpu.SemaphoreType.DMA((2, owners * own // 768)),
    ]


def middle_kernel(len_ref, c_ref, wa_ref, x_ref, mask_ref, w_ref, b_ref, cot_ref, rl_ref, small_ref,
                  low_ref, act_ref, dh_ref, dlow_ref, out_ref, dr1_ref, da_ref, dc_ref, gb_ref, red_ref,
                  wi_ref, wo_ref, slope_ref, sem, *, block):
    i = pl.program_id(0)
    f32, b16 = jnp.float32, jnp.bfloat16

    @pl.when(i == 0)
    def _():
        red_ref[...] = jnp.zeros_like(red_ref)
        gb_ref[...] = jnp.zeros_like(gb_ref)

    def body(per, chunks, wait):
        def weights(ref, c):
            return ref[c * per : c * per + per].reshape(-1, D)

        mixed = jnp.where(mask_ref[...] > 0.5, small_ref[8:9], x_ref[...].astype(f32))
        n1, inv1 = row_norm(mixed + dot(c_ref[...], wa_ref[...]) + small_ref[2:3])
        first = n1 * small_ref[3:4] + small_ref[4:5]
        low = first.astype(b16)
        low_ref[...] = low
        acc = None
        for c in range(chunks):
            wait(c)
            cols = slice(c * 768, c * 768 + 768)
            act, slo = gelu_both(dot(low, weights(wi_ref, c), NT) + b_ref[:, cols])
            act = act.astype(b16)
            act_ref[:, cols] = act
            slope_ref[:, cols] = slo.astype(b16)
            part = dot(act, weights(wo_ref, c))
            acc = part if acc is None else acc + part
        n2, inv2 = row_norm(first + (acc + small_ref[7:8]))
        out_ref[...] = n2 * small_ref[5:6] + small_ref[6:7]
        at = lax.broadcasted_iota(jnp.int32, (block, D), 0) + i * block
        cot = jnp.where(at < len_ref[0], cot_ref[...].astype(f32), 0.0)
        dres = row_norm_back(cot, n2, inv2, small_ref[5:6])
        dlow = dres.astype(b16)
        dlow_ref[...] = dlow
        for k, v in enumerate((cot * n2, cot, dlow.astype(f32))):
            red_ref[3 + k : 4 + k] += jnp.sum(v, axis=0, keepdims=True)
        acc = dres
        for c in range(chunks):
            cols = slice(c * 768, c * 768 + 768)
            dh = (dot(dlow, weights(wo_ref, c), NT) * slope_ref[:, cols].astype(f32)).astype(b16)
            dh_ref[:, cols] = dh
            gb_ref[:, cols] += jnp.sum(dh.astype(f32), axis=0, keepdims=True)
            acc = acc + dot(dh, weights(wi_ref, c))
        dr1 = row_norm_back(acc, n1, inv1, small_ref[3:4])
        da = dr1.astype(b16)
        dr1_ref[...] = dr1
        da_ref[...] = da
        dc_ref[...] = (dot(da, wa_ref[...], NT) * rl_ref[...]).astype(b16)
        for k, v in enumerate((da.astype(f32), acc * n1, acc)):
            red_ref[k : k + 1] += jnp.sum(v, axis=0, keepdims=True)

    by_step(w_ref, wi_ref, wo_ref, sem, body)


def middle(length, ctx, w_attn, rounded, mask, w_all, bias, cot, rl, small, block=256):
    seq = ctx.shape[0]
    wide = pl.BlockSpec((block, D), lambda i, n: (i, 0))
    hidden = pl.BlockSpec((block, FF), lambda i, n: (i, 0))
    one = pl.BlockSpec((1, FF), lambda i, n: (0, 0))
    f32, b16 = jnp.float32, jnp.bfloat16

    def shape(cols, kind, rows=seq):
        return jax.ShapeDtypeStruct((rows, cols), kind)

    return pl.pallas_call(
        functools.partial(middle_kernel, block=block),
        grid_spec=pltpu.PrefetchScalarGridSpec(
            num_scalar_prefetch=1,
            grid=(seq // block,),
            in_specs=[wide, pl.BlockSpec((D, D), lambda i, n: (0, 0)), wide, pl.BlockSpec((block, 1), lambda i, n: (i, 0)),
                      pl.BlockSpec(memory_space=pl.ANY), one, wide, wide, pl.BlockSpec((9, D), lambda i, n: (0, 0))],
            out_specs=[wide, hidden, hidden, wide, wide, wide, wide, wide, one, pl.BlockSpec((8, D), lambda i, n: (0, 0))],
            scratch_shapes=ffn_scratch(w_all, block),
        ),
        out_shape=[shape(D, b16), shape(FF, b16), shape(FF, b16), shape(D, b16), shape(D, f32), shape(D, f32),
                   shape(D, b16), shape(D, b16), shape(FF, f32, 1), shape(D, f32, 8)],
        compiler_params=pltpu.CompilerParams(vmem_limit_bytes=VMEM),
        cost_estimate=cost(40),
    )(length, ctx, w_attn, rounded, mask, w_all, bias, cot, rl, small)


def input_kernel(dr_ref, d0_ref, d1_ref, d2_ref, w0_ref, w1_ref, w2_ref, z_ref, wg_ref, mask_ref,
                 fg_ref, red_ref):
    i = pl.program_id(0)
    acc = dr_ref[...] + dot(z_ref[...], wg_ref[...], TN)
    qs, vs = [], []
    for d_ref, w_ref in ((d0_ref, w0_ref), (d1_ref, w1_ref), (d2_ref, w2_ref)):
        for k in range(3):
            acc += dot(d_ref[k], w_ref[k], NT)
        qs.append(jnp.sum(d_ref[0].astype(jnp.float32), axis=0, keepdims=True))
        vs.append(jnp.sum(d_ref[2].astype(jnp.float32), axis=0, keepdims=True))
    masked = mask_ref[...] > 0.5
    fg_ref[...] = jnp.where(masked, 0.0, acc)
    dm = jnp.sum(jnp.where(masked, acc, 0.0), axis=0, keepdims=True)
    red = jnp.concatenate(
        [jnp.concatenate(qs, axis=1), jnp.concatenate(vs, axis=1), dm, jnp.zeros((5, D), jnp.float32)], axis=0
    )

    @pl.when(i == 0)
    def _():
        red_ref[...] = red

    @pl.when(i > 0)
    def _():
        red_ref[...] += red


def input_grad(dr1, ds, ws, dz, wg, mask, block=256):
    seq = dr1.shape[0]
    wide = pl.BlockSpec((block, D), lambda i: (i, 0))
    part = pl.BlockSpec((3, block, 256), lambda i: (0, i, 0))
    wpart = pl.BlockSpec((3, D, 256), lambda i: (0, 0, 0))
    return pl.pallas_call(
        input_kernel,
        grid=(seq // block,),
        in_specs=[wide, part, part, part, wpart, wpart, wpart,
                  pl.BlockSpec((dz.shape[0], block), lambda i: (0, i)),
                  pl.BlockSpec(wg.shape, lambda i: (0, 0)),
                  pl.BlockSpec((block, 1), lambda i: (i, 0))],
        out_specs=[wide, pl.BlockSpec((8, D), lambda i: (0, 0))],
        out_shape=[jax.ShapeDtypeStruct((seq, D), jnp.float32), jax.ShapeDtypeStruct((8, D), jnp.float32)],
        compiler_params=pltpu.CompilerParams(vmem_limit_bytes=VMEM),
        cost_estimate=cost(8),
    )(dr1, *ds, *ws, dz, wg, mask)


def split3(x):
    hi = x.astype(jnp.bfloat16)
    rest = x - hi.astype(jnp.float32)
    mid = rest.astype(jnp.bfloat16)
    low = (rest - mid.astype(jnp.float32)).astype(jnp.bfloat16)
    return hi, mid, low


def tree_sum(parts):
    while len(parts) > 1:
        half = len(parts) // 2
        parts = [parts[i] + parts[i + half] for i in range(half)]
    return parts[0]


def added(parts):
    return sum(p.astype(jnp.float32) for p in parts)


class Net:
    def __init__(self, dp_size, t_size):
        self.t = t_size
        self.sizes = {"z": dp_size // 4, "y": 2, "c": 2, "x": t_size}
        d = lax.axis_index("dp")
        self.at = {"z": d // 4, "y": d // 2 % 2, "c": d % 2, "x": lax.axis_index("tensor")}

    def shift(self, v, axis, k, swap=False):
        pairs = []
        sz = self.sizes
        for z in range(sz["z"]):
            for y in range(2):
                for c in range(2):
                    for x in range(sz["x"]):
                        src = {"z": z, "y": y, "c": c, "x": x}
                        dst = dict(src)
                        dst[axis] = src[axis] ^ k if swap else (src[axis] - k) % sz[axis]
                        flat = [((q["z"] * 2 + q["y"]) * 2 + q["c"]) * sz["x"] + q["x"] for q in (src, dst)]
                        pairs.append(tuple(flat))
        return lax.ppermute(v, ("dp", "tensor"), pairs)

    def gather(self, v, axis, dim):
        return jnp.concatenate([v] + [self.shift(v, axis, k) for k in range(1, self.sizes[axis])], axis=dim)

    def scatter(self, parts, axis, dim):
        n = self.sizes[axis]
        at = self.at[axis]

        def slot(i):
            return [lax.dynamic_index_in_dim(p, i, dim, False) for p in parts]

        arrived = []
        for k in range(1, n):
            send = added(slot((at + k) % n)).astype(jnp.bfloat16)
            arrived.append(self.shift(send, axis, n - k))
        return slot(at), arrived

    def gather_own(self, v, axis, dim):
        n = self.sizes[axis]
        at = self.at[axis]
        out = jnp.zeros(v.shape[:dim] + (n,) + v.shape[dim:], v.dtype)
        for k in range(n):
            part = v if k == 0 else self.shift(v, axis, k)
            out = lax.dynamic_update_index_in_dim(out, part, (at + k) % n, dim)
        return out

    def total(self, v, axes=("c", "x", "y", "z")):
        for axis in axes:
            bit = 1
            while bit < self.sizes[axis]:
                v = v + self.shift(v, axis, bit, True)
                bit *= 2
        return v


def rolled(net, v, dims, sign):
    for dim, axis in dims:
        v = jnp.roll(v, sign * net.at[axis], dim)
    return v


def natural(net, places, mine, peer):
    if mine.shape[3] % 16 == 0:
        return assemble(places, mine, peer)
    v = rolled(net, jnp.stack([mine, peer])[:, :, :, 3:], ((0, "c"), (1, "y"), (2, "z")), 1)
    return v.transpose(2, 1, 0, 4, 3, 5).reshape(D, D)


def wide_rows(net, places, mine, peer):
    if mine.shape[3] % 16 == 0:
        return places, mine, peer
    zs, kinds, cols = net.sizes["z"], mine.shape[2], mine.shape[4]
    v = rolled(net, jnp.stack([mine, peer]), ((0, "c"), (1, "y"), (2, "z")), 1)
    v = v.transpose(2, 1, 0, 4, 3, 5)
    v = v.reshape(1, 2, 2, -1, kinds, cols).transpose(2, 1, 0, 4, 3, 5)
    return places * 0, v[0], v[1]


def local(dp_size, t_size, features, lengths, span_starts, buckets, cotangent,
          qkv_w, qkv_m, qkv_v, out_w, out_m, out_v, ffn_in, ffn_in_m, ffn_in_v,
          ffn_out, ffn_out_m, ffn_out_v, small_params, small_m, small_v,
          pos_table, pos_m, pos_v, gate_proj, gate_m, gate_v, step_count):
    f32, b16 = jnp.float32, jnp.bfloat16
    net = Net(dp_size, t_size)
    zs = net.sizes["z"]
    seq = features.shape[1]
    own = ffn_out.shape[0]
    rows = qkv_w.shape[1]
    scale = HD**-0.5

    bar = lax.optimization_barrier
    places = jnp.stack([net.at["z"], net.at["y"], net.at["c"], net.at["x"]]).astype(jnp.int32)
    cols = D // GROUPS
    group_heads = H // GROUPS
    both = ("dp", "tensor")

    qkv_low = qkv_w[None, None]
    u0, u1, u2 = [qkv_low[..., g * cols : (g + 1) * cols].astype(b16) for g in range(3)]
    z0 = net.gather(u0, "z", 1)
    rev = jnp.flip(buckets)
    order = jnp.concatenate([rev[127:], jnp.full((1,), -1, jnp.int32), rev[:127]])
    onehot = (jnp.arange(NB, dtype=jnp.int32)[:, None] == order[None, :]).astype(b16)
    off3 = dot(jnp.concatenate(split3(pos_table[:NB].T), axis=0), onehot).reshape(3, H, 2 * seq)
    table = bias_tables(off3[0] + off3[1] + off3[2])
    bias_row = jnp.pad(ffn_in[D:].astype(b16), ((0, 7), (0, D - own)))
    ffn_own = jnp.concatenate([ffn_in[:D].T.astype(b16), ffn_out.astype(b16), bias_row])
    z0, u1, table, features, ffn_own, out_w, gate_proj = bar((z0, u1, table, features, ffn_own, out_w, gate_proj))

    w_all = lax.all_gather(ffn_own, both, axis=0)
    w_all_k = w_all
    if own % 16:
        w_all_k = jnp.concatenate(
            [w_all[:, k * own : (k + 1) * own].reshape(4, -1, D) for k in range(2)] + [jnp.zeros((4, 8, D), b16)], axis=1)

    y0 = net.gather(z0, "y", 0)
    z1 = net.gather(u1, "z", 1)
    positions = jnp.arange(seq, dtype=jnp.int32)
    starts = span_starts[0]
    masked = jnp.any((positions[:, None] >= starts[None, :]) & (positions[:, None] < starts[None, :] + SPAN), axis=1)[:, None]
    mask = masked.astype(f32)
    rounded = jnp.where(masked, small_params[8][None, :].astype(b16), features[0])
    ga = jnp.sum(gate_proj[:HD, :4], axis=1)
    gb = jnp.sum(gate_proj[:HD, 4:], axis=1)
    za = jnp.sum(gate_proj[HD, :4])
    zb = jnp.sum(gate_proj[HD, 4:])
    eye = jnp.eye(H, dtype=f32)[:, :, None]
    wg = jnp.concatenate([(eye * ga).reshape(H, D), (eye * gb).reshape(H, D)], axis=0)
    wg3 = split3(wg)
    z3 = dot(jnp.concatenate(wg3, axis=0), rounded, NT).reshape(3, 2 * H, seq)
    z_all = z3[0] + z3[1] + z3[2]
    gate_a = jax.nn.sigmoid(z_all[:H] + za)
    gate_b = jax.nn.sigmoid(z_all[H:] + zb)
    const = pos_table[NB][:, None]
    gates = (gate_a * (gate_b * const - 1.0) + 2.0).reshape(H, 1, seq)
    rounded_t = rounded.T
    bias3 = jnp.stack([small_params[0], jnp.zeros((D,), f32), small_params[1]])[:, None, :]
    out_parts = out_w.astype(b16).reshape(rows, 3, cols).transpose(1, 0, 2)[None, None]
    u2 = jnp.concatenate([u2, out_parts], axis=2)
    y0, z1, u2, rounded, gates, rounded_t = bar((y0, z1, u2, rounded, gates, rounded_t))

    p0 = net.shift(y0, "c", 1)

    def attend(g, mine, peer, kept):
        at, mine, peer = wide_rows(net, places, mine, peer)
        bias = bias3[:, :, g * cols : (g + 1) * cols]
        return attn_fwd(lengths, at, rounded, mine, peer, bias, table, gates, g * group_heads, group_heads, kept)

    p0, z1, u2 = bar((p0, z1, u2))
    y1 = net.gather(z1, "y", 0)
    z2 = net.gather(u2, "z", 1)
    probs0, *kept, q0, w0 = attend(0, y0, p0, ())
    y1, z2, probs0, q0, w0, *kept = bar((y1, z2, probs0, q0, w0, *kept))
    p1 = net.shift(y1, "c", 1)
    y2 = net.gather(z2, "y", 0)
    probs1, *kept, q1, w1 = attend(1, y1, p1, kept)
    y2, probs1, q1, w1, *kept = bar((y2, probs1, q1, w1, *kept))
    p2 = net.shift(y2, "c", 1)
    w_attn = natural(net, places, y2, p2)
    probs2, context, context_f, inv_sum, q2, w2 = attend(2, y2, p2, kept)
    qkv, w_qkv, probs = (q0, q1, q2), (w0, w1, w2), (probs0, probs1, probs2)

    bias_in = w_all[:, 2 * own, :own].reshape(1, -1).astype(f32)
    low, act, d_hidden, d_branch, layer_out, d_res1, d_attention, d_context, g_bias_in, red = middle(
        lengths, context, w_attn, rounded, mask, w_all_k, bias_in, cotangent[0], inv_sum, small_params)

    def attend_back(g):
        return attn_bwd(qkv[g], d_context, context_f, probs[g], table, gates, g * group_heads, group_heads)

    def by_owner(v):
        return v.reshape(zs, 2, 2, rows, v.shape[-1])

    g_ffn = ffn_grads(d_hidden, act, low, d_branch, own)
    g_ffn, d_context = bar((g_ffn, d_context))
    g_ffn = lax.psum_scatter(g_ffn.reshape(dp_size, t_size, 2 * own, D), "dp", scatter_dimension=0, tiled=False)
    d0, dg0, do0 = attend_back(0)
    m1 = by_owner(weight_grads(rounded_t, d0, context, d_attention))
    m1, d0, dg0, do0, d_context = bar((m1, d0, dg0, do0, d_context))
    stay_1, got_1 = net.scatter([m1], "c", 2)
    d1, dg1, do1 = attend_back(1)
    got_1, d1, dg1, do1, d_context = bar((got_1, d1, dg1, do1, d_context))
    stay_1, got_1 = net.scatter(stay_1 + got_1, "y", 1)
    d2, dg2, do2 = attend_back(2)
    got_1, d2, dg2, do2 = bar((got_1, d2, dg2, do2))
    m2 = by_owner(weight_grads(rounded_t, d1, d2, jnp.zeros((8, 128), f32)))
    stay_2, got_2 = net.scatter([m2], "c", 2)

    dgate = jnp.concatenate([dg0, dg1, dg2], axis=0).reshape(H, seq)
    doff = jnp.concatenate([do0, do1, do2], axis=0).reshape(H, 2 * seq)
    d_a = dgate * (gate_b * const - 1.0) * gate_a * (1.0 - gate_a)
    d_b = dgate * gate_a * const * gate_b * (1.0 - gate_b)
    d_const = jnp.sum(dgate * gate_a * gate_b, axis=1)
    dz = jnp.concatenate([d_a, d_b], axis=0)
    dz_hi = dz.astype(b16)
    dz_lo = (dz - dz_hi.astype(f32)).astype(b16)
    g_z2 = dot(jnp.concatenate([dz_hi, dz_lo], axis=0), rounded).reshape(2, 2, H, H, HD)
    g_z = jnp.sum((g_z2[0] + g_z2[1]) * eye, axis=(1, 2))
    g_zb = jnp.sum(dz.reshape(2, H * seq), axis=1)
    g_gate_local = jnp.repeat(jnp.concatenate([g_z, g_zb[:, None]], axis=1).T, 4, axis=1)
    pos3 = dot(onehot, jnp.concatenate(split3(doff), axis=0), NT).reshape(NB, 3, H)
    pos_local = jnp.concatenate([jnp.sum(pos3, axis=1), d_const[None, :]], axis=0)
    got_2, got_1, dz_hi, dz_lo, pos_local, g_gate_local, d_res1 = bar(
        (got_2, got_1, dz_hi, dz_lo, pos_local, g_gate_local, d_res1))
    stay_2, got_2 = net.scatter(stay_2 + got_2, "y", 1)
    stay_1, got_1 = net.scatter(stay_1 + got_1, "z", 0)
    feature_grad, red0 = input_grad(
        d_res1, (d0, d1, d2), w_qkv, jnp.concatenate([dz_hi, dz_lo, dz_hi], axis=0),
        jnp.concatenate([wg3[0], wg3[0], wg3[1]], axis=0), mask)
    small_local = jnp.concatenate([red0[:2], red[:6], red0[2:3]], axis=0)

    parts = [small_local, pos_local, g_gate_local, g_bias_in]
    counts = [p.size for p in parts]
    pad = -(sum(counts) + 1) % 1024
    packed = jnp.concatenate([p.reshape(-1) for p in parts])
    got_2, got_1, feature_grad, packed = bar((got_2, got_1, feature_grad, packed))
    stay_2, got_2 = net.scatter(stay_2 + got_2, "z", 0)
    m1 = added(stay_1 + got_1).astype(b16)
    m1 = tree_sum([m1.astype(f32)] + [net.shift(m1, "x", k).astype(f32) for k in range(1, t_size)])
    got_2, m1, g_ffn = bar((got_2, m1, g_ffn))
    m2 = added(stay_2 + got_2).astype(b16)
    m2 = tree_sum([m2.astype(f32)] + [net.shift(m2, "x", k).astype(f32) for k in range(1, t_size)])
    stay_f, got_f = net.scatter([g_ffn], "x", 0)
    g_ffn = added(stay_f + got_f)
    own_ffn = jnp.sum(jnp.square(g_ffn)) + jnp.sum(jnp.square(m1)) * (1.0 / t_size)
    g_in_t = g_ffn[:own].T
    g_outw = g_ffn[own:]
    own_sum = jnp.sum(jnp.square(m2)) * (1.0 / t_size) + own_ffn
    flat = jnp.concatenate([packed, own_sum.reshape(1), jnp.zeros((pad,), f32)]).reshape(-1, 128)
    flat = net.total(flat).reshape(-1)
    own_sum = flat[sum(counts)]
    shared = jnp.sum(jnp.where(jnp.arange(flat.size) < sum(counts), flat * flat, 0.0))
    m1 = m1.reshape(rows, 2, 3, cols)
    m2 = m2.reshape(rows, 2, 3, cols)
    g_qkv = jnp.stack([m1[:, 0], m2[:, 0], m2[:, 1]], axis=2).transpose(1, 0, 2, 3).reshape(3, rows, D)
    g_out = m1[:, 1].reshape(rows, D)
    pieces, at = [], 0
    for p, count in zip(parts, counts):
        pieces.append(flat[at : at + count].reshape(p.shape))
        at += count
    g_small, g_pos, g_gate, g_bias = pieces
    grad_norm = jnp.sqrt(own_sum + shared)
    clip = jnp.minimum(1.0, CLIP_NORM / (grad_norm + 1e-06))
    count = step_count[0].astype(f32)
    me = lax.axis_index("dp") * t_size + lax.axis_index("tensor")
    g_bias = lax.dynamic_slice_in_dim(g_bias.reshape(-1, own), me, 1, 0)
    g_ffn_in = jnp.concatenate([g_in_t, g_bias], axis=0)

    qkv_new, qkv_moment, qkv_second = adam_step(qkv_w, g_qkv, qkv_m, qkv_v, clip, 2.0 * D**-0.5, count)
    out_new, out_moment, out_second = adam_step(out_w, g_out, out_m, out_v, clip, 1.0, count)
    in_new, in_moment, in_second = adam_step(ffn_in, g_ffn_in, ffn_in_m, ffn_in_v, clip, 2.0 * D**-0.5, count)
    fo_new, fo_moment, fo_second = adam_step(ffn_out, g_outw, ffn_out_m, ffn_out_v, clip, 2.0 * FF**-0.5, count)
    small_new, small_moment, small_second = adam_step(small_params, g_small, small_m, small_v, clip, 0.5, count)
    pos_new, pos_moment, pos_second = adam_step(pos_table, g_pos, pos_m, pos_v, clip, 1.0, count)
    gate_new, gate_moment, gate_second = adam_step(gate_proj, g_gate, gate_m, gate_v, clip, 2.0 * HD**-0.5, count)
    return (
        layer_out[None], feature_grad[None], grad_norm.reshape(1),
        qkv_new, qkv_moment, qkv_second, qkv_new.astype(b16),
        out_new, out_moment, out_second, out_new.astype(b16),
        in_new, in_moment, in_second, in_new.astype(b16),
        fo_new, fo_moment, fo_second, fo_new.astype(b16),
        g_small, small_new, small_moment, small_second,
        pos_new, pos_moment, pos_second, gate_new, gate_moment, gate_second,
    )


def solution(mesh):
    both = ("dp", "tensor")
    three = (P(None, "dp", None),)
    row = (P("dp", None),)
    col = (P(None, both),)
    rows2 = (P(both, None),)
    utt = P(both, None, None)
    in_specs = (
        (utt, P(both), P(both, None), P(), utt) + three * 3 + row * 3 + col * 3 + rows2 * 3 + (P(),) * 10
    )
    out_specs = (utt, utt, P()) + three * 4 + row * 4 + col * 4 + rows2 * 4 + (P(),) * 10
    fn = functools.partial(local, mesh.shape["dp"], mesh.shape["tensor"])
    return jax.shard_map(fn, mesh=mesh, in_specs=in_specs, out_specs=out_specs, check_vma=False)
```

```python
import functools

import jax
import jax.numpy as jnp
from jax import lax
from jax.experimental import pallas as pl
from jax.experimental.pallas import tpu as pltpu
from jax.sharding import PartitionSpec as P

D = 768
H = 12
HD = 64
FF = 3072
NB = 320
SPAN = 10
CLIP_NORM = 1.0
BETA_ONE = 0.9
BETA_TWO = 0.98
ADAM_EPS = 1e-08
DECAY_RATE = 0.01
NORM_EPS = 1e-05
NEG_BIG = -1e30
GROUPS = 3


def adam_step(weight, grad_in, moment, second, clip_factor, rate_in, count_in):
    scaled = grad_in * clip_factor
    new_moment = BETA_ONE * moment + (1.0 - BETA_ONE) * scaled
    new_second = BETA_TWO * second + (1.0 - BETA_TWO) * scaled * scaled
    first_fix = 1.0 - BETA_ONE**count_in
    second_fix = 1.0 - BETA_TWO**count_in
    update = new_moment / first_fix / (jnp.sqrt(new_second / second_fix) + ADAM_EPS)
    return (weight - rate_in * (update + DECAY_RATE * weight), new_moment, new_second)


VMEM = 60 << 20
NT = (((1,), (1,)), ((), ()))
TN = (((0,), (0,)), ((), ()))


def dot(a, b, dims=(((1,), (0,)), ((), ()))):
    return lax.dot_general(a, b, dims, preferred_element_type=jnp.float32)


def cost(us):
    return pl.CostEstimate(flops=0, bytes_accessed=int(us * 3.0e6), transcendentals=0)


def table_kernel(off_ref, out_ref):
    heads, _, w = out_ref.shape
    for h in range(heads):
        row = jnp.broadcast_to(off_ref[h], (8, w))
        eight = pltpu.roll(row, 0, 1, stride=1, stride_axis=0)
        for r in range(0, 128, 8):
            out_ref[h, r : r + 8] = pltpu.roll(eight, r, 1) if r else eight


def bias_tables(offr, heads=4):
    n, w = offr.shape
    return pl.pallas_call(
        table_kernel,
        grid=(n // heads,),
        in_specs=[pl.BlockSpec((heads, 1, w), lambda h: (h, 0, 0))],
        out_specs=pl.BlockSpec((heads, 128, w), lambda h: (h, 0, 0)),
        out_shape=jax.ShapeDtypeStruct((n, 128, w), jnp.float32),
        compiler_params=pltpu.CompilerParams(vmem_limit_bytes=VMEM),
        cost_estimate=cost(8),
    )(offr.reshape(n, 1, w))


def fwd_kernel(len_ref, at_ref, x_ref, mine_ref, peer_ref, bias_ref, t_ref, g_ref, *rest, seq, ib, zs, rows, kept):
    p_ref, o_ref, of_ref, rl_ref, qkv_ref, w_ref, s_ref, sem = rest[kept:]
    h = pl.program_id(0)

    @pl.when(h == 0)
    def _():
        z0, y0, c0 = at_ref[0], at_ref[1], at_ref[2]
        copies = []
        for c, src in enumerate((mine_ref, peer_ref)):
            for y in range(2):
                for z in range(zs):
                    block = (lax.rem(z0 + z, zs) * 2 + lax.rem(y0 + y, 2)) * 2 + lax.rem(c0 + c, 2)
                    first = pl.multiple_of(block * rows, rows)
                    there = w_ref.at[:, pl.ds(first, rows), :]
                    copies.append(pltpu.make_async_copy(src.at[y, z, pl.ds(0, 3)], there, sem.at[len(copies)]))
        for copy in copies:
            copy.start()
        for copy in copies:
            copy.wait()
        for k in range(3):
            r = dot(x_ref[...], w_ref[k]) + bias_ref[k]
            qkv_ref[k] = (r * HD**-0.5 if k == 0 else r).astype(jnp.bfloat16)

    par = lax.rem(h, 2)
    lane = lax.broadcasted_iota(jnp.int32, (seq, 128), 1)
    rowi = lax.broadcasted_iota(jnp.int32, (seq, 128), 0)
    inh = (lane // 64) == par
    flag = lane == (64 * (1 - par))
    one = jnp.bfloat16(1.0)
    zero = jnp.bfloat16(0.0)
    pair = pl.ds(pl.multiple_of(h // 2 * 128, 128), 128)
    bias = jnp.where(rowi < len_ref[0], 0.0, NEG_BIG).astype(jnp.bfloat16)
    qm = jnp.where(flag, one, jnp.where(inh, qkv_ref[0, :, pair], zero))
    km = jnp.where(flag, bias, qkv_ref[1, :, pair])
    vm = jnp.where(flag, one, qkv_ref[2, :, pair])
    vt = vm.T
    base = seq - 128
    def scores(i0):
        gate = g_ref[0, :, i0 : i0 + ib]
        qb = qm[i0 : i0 + ib]
        m = None
        for j0 in range(0, seq, 128):
            c0 = i0 - j0 + base
            s = dot(km[j0 : j0 + 128], qb, NT) + t_ref[0, :, c0 : c0 + ib] * gate
            s_ref[i0 // ib % 2, j0 : j0 + 128, :] = s
            mm = jnp.max(s.reshape(16, 8, ib), axis=0)
            m = mm if m is None else jnp.maximum(m, mm)
        return jnp.max(m, axis=0, keepdims=True)

    m = scores(0)
    for i0 in range(0, seq, ib):
        m_next = scores(i0 + ib) if i0 + ib < seq else None
        for j0 in range(0, seq, 128):
            e = jnp.exp(s_ref[i0 // ib % 2, j0 : j0 + 128, :] - m).astype(jnp.bfloat16)
            p_ref[0, j0 : j0 + 128, i0 : i0 + ib] = e
        m = m_next
        ct = dot(vt, p_ref[0, :, i0 : i0 + ib])
        total = jnp.where(par == 0, ct[64:65], ct[0:1])
        rl = 1.0 / total
        oc = (ct * rl).T
        rc = jnp.broadcast_to(rl, (128, ib)).T
        ih = inh[i0 : i0 + ib]
        o_ref[i0 : i0 + ib, :] = jnp.where(ih, oc.astype(jnp.bfloat16), o_ref[i0 : i0 + ib, :])
        of_ref[i0 : i0 + ib, :] = jnp.where(ih, oc, of_ref[i0 : i0 + ib, :])
        rl_ref[i0 : i0 + ib, :] = jnp.where(ih, rc, rl_ref[i0 : i0 + ib, :])


def attn_fwd(length, at, x, mine, peer, bias, table, gates, head0, heads, kept, ib=256):
    seq = x.shape[0]
    _, zs, _, rows, cols = mine.shape
    w = table.shape[-1]
    f32, b16 = jnp.float32, jnp.bfloat16
    out_pair = pl.BlockSpec((seq, 128), lambda h, n, a: (0, head0 // 2 + h // 2))
    hbm = pl.BlockSpec(memory_space=pl.ANY)
    return pl.pallas_call(
        functools.partial(fwd_kernel, seq=seq, ib=ib, zs=zs, rows=rows, kept=len(kept)),
        grid_spec=pltpu.PrefetchScalarGridSpec(
            num_scalar_prefetch=2,
            grid=(heads,),
            in_specs=[
                pl.BlockSpec((seq, D), lambda h, n, a: (0, 0)),
                hbm,
                hbm,
                pl.BlockSpec((3, 1, cols), lambda h, n, a: (0, 0, 0)),
                pl.BlockSpec((1, 128, w), lambda h, n, a: (head0 + h, 0, 0)),
                pl.BlockSpec((1, 1, seq), lambda h, n, a: (head0 + h, 0, 0)),
            ] + [hbm] * len(kept),
            out_specs=[pl.BlockSpec((1, seq, seq), lambda h, n, a: (h, 0, 0)), out_pair, out_pair, out_pair,
                       pl.BlockSpec((3, seq, cols), lambda h, n, a: (0, 0, 0)),
                       pl.BlockSpec((3, D, cols), lambda h, n, a: (0, 0, 0))],
            scratch_shapes=[pltpu.VMEM((2, seq, ib), f32), pltpu.SemaphoreType.DMA((4 * zs,))],
        ),
        out_shape=[jax.ShapeDtypeStruct((heads, seq, seq), b16), jax.ShapeDtypeStruct((seq, D), b16),
                   jax.ShapeDtypeStruct((seq, D), f32), jax.ShapeDtypeStruct((seq, D), f32),
                   jax.ShapeDtypeStruct((3, seq, cols), b16), jax.ShapeDtypeStruct((3, D, cols), b16)],
        input_output_aliases={8: 1, 9: 2, 10: 3} if kept else {},
        compiler_params=pltpu.CompilerParams(vmem_limit_bytes=VMEM),
        cost_estimate=cost(2.7 * heads + 4),
    )(length, at, x, mine, peer, bias, table, gates, *kept)


def bwd_kernel(q_ref, k_ref, v_ref, dc_ref, c_ref, p_ref, t_ref, g_ref, d_ref, dg_ref, do_ref, a_ref, ds_ref, *, seq, ib):
    par = lax.rem(pl.program_id(0), 2)
    lane = lax.broadcasted_iota(jnp.int32, (seq, 128), 1)
    inh = (lane // 64) == par
    f0 = lane == (64 * (1 - par))
    f1 = lane == (64 * (1 - par) + 1)
    one = jnp.bfloat16(1.0)
    dc = dc_ref[...]
    dcf = jnp.where(inh, dc.astype(jnp.float32), 0.0)
    delta = -jnp.sum(dcf * c_ref[...], axis=1, keepdims=True)
    hi = delta.astype(jnp.bfloat16).astype(jnp.float32)
    lo = delta - hi
    dca = jnp.where(f0, hi, jnp.where(f1, lo, dcf)).astype(jnp.bfloat16)
    va = jnp.where(f0 | f1, one, v_ref[0])
    kt = k_ref[0].T
    q = q_ref[0]
    base = seq - 128
    a_ref[...] = jnp.zeros_like(a_ref)
    dv = dot(p_ref[0], dc)
    d_ref[2] = jnp.where(inh, dv.astype(jnp.bfloat16), d_ref[2])
    for i0 in range(0, seq, ib):
        gate = g_ref[0, :, i0 : i0 + ib]
        dcb = dca[i0 : i0 + ib]
        dg = jnp.zeros((8, ib), jnp.float32)
        for j0 in range(0, seq, 128):
            c0 = i0 - j0 + base
            ds = dot(va[j0 : j0 + 128], dcb, NT) * p_ref[0, j0 : j0 + 128, i0 : i0 + ib].astype(jnp.float32)
            ds_ref[j0 : j0 + 128, i0 : i0 + ib] = ds.astype(jnp.bfloat16)
            dg = dg + jnp.sum((ds * t_ref[0, :, c0 : c0 + ib]).reshape(16, 8, ib), axis=0)
            a_ref[:, c0 : c0 + ib] += ds * gate
        dg_ref[0, :, i0 : i0 + ib] = jnp.sum(dg, axis=0, keepdims=True)
        dqt = dot(kt, ds_ref[:, i0 : i0 + ib]).T * HD**-0.5
        d_ref[0, i0 : i0 + ib, :] = jnp.where(inh[i0 : i0 + ib], dqt.astype(jnp.bfloat16), d_ref[0, i0 : i0 + ib, :])
    dk = dot(ds_ref[...], q)
    d_ref[1] = jnp.where(inh, dk.astype(jnp.bfloat16), d_ref[1])
    a = a_ref[...]
    w = a.shape[1]
    r = 64
    while r >= 8:
        a = a[:r] + pltpu.roll(a[r:], w - r, 1)
        r //= 2
    acc = a[0:1]
    for r in range(1, 8):
        acc = acc + pltpu.roll(a[r : r + 1], w - r, 1)
    do_ref[0] = acc


def attn_bwd(qkv, dctx, ctx, probs, table, gates, head0, heads, ib=256):
    seq = qkv.shape[1]
    w = table.shape[-1]

    def part(k):
        return pl.BlockSpec((1, seq, 128), lambda h: (k, 0, h // 2))

    pair = pl.BlockSpec((seq, 128), lambda h: (0, head0 // 2 + h // 2))
    return pl.pallas_call(
        functools.partial(bwd_kernel, seq=seq, ib=ib),
        grid=(heads,),
        in_specs=[
            part(0),
            part(1),
            part(2),
            pair,
            pair,
            pl.BlockSpec((1, seq, seq), lambda h: (h, 0, 0)),
            pl.BlockSpec((1, 128, w), lambda h: (head0 + h, 0, 0)),
            pl.BlockSpec((1, 1, seq), lambda h: (head0 + h, 0, 0)),
        ],
        out_specs=[
            pl.BlockSpec((3, seq, 128), lambda h: (0, 0, h // 2)),
            pl.BlockSpec((1, 1, seq), lambda h: (h, 0, 0)),
            pl.BlockSpec((1, 1, w), lambda h: (h, 0, 0)),
        ],
        scratch_shapes=[pltpu.VMEM((128, w), jnp.float32), pltpu.VMEM((seq, seq), jnp.bfloat16)],
        out_shape=[
            jax.ShapeDtypeStruct((3, seq, heads * HD), jnp.bfloat16),
            jax.ShapeDtypeStruct((heads, 1, seq), jnp.float32),
            jax.ShapeDtypeStruct((heads, 1, w), jnp.float32),
        ],
        compiler_params=pltpu.CompilerParams(vmem_limit_bytes=VMEM),
        cost_estimate=cost(3.0 * heads),
    )(qkv, qkv, qkv, dctx, ctx, probs, table, gates)


def wgrad_kernel(xt_ref, d_ref, a_ref, b_ref, g_ref, *, pair):
    xt = xt_ref[...]
    for k in range(3):
        g_ref[:, k * 256 : k * 256 + 256] = dot(xt, d_ref[k]).astype(jnp.bfloat16)
    if pair:
        g_ref[:, 768:1536] = dot(a_ref[...], b_ref[...], TN).astype(jnp.bfloat16)
    else:
        for k in range(3):
            g_ref[:, 768 + k * 256 : 1024 + k * 256] = dot(xt, a_ref[k]).astype(jnp.bfloat16)


def weight_grads(xt, d3, a, b, block=256):
    seq = xt.shape[1]
    pair = a.ndim == 2
    kinds = pl.BlockSpec((3, seq, 256), lambda i: (0, 0, 0))
    a_spec = pl.BlockSpec((seq, block), lambda i: (0, i)) if pair else kinds
    b_spec = pl.BlockSpec((seq, D), lambda i: (0, 0)) if pair else pl.BlockSpec((8, 128), lambda i: (0, 0))
    return pl.pallas_call(
        functools.partial(wgrad_kernel, pair=pair),
        grid=(D // block,),
        in_specs=[pl.BlockSpec((block, seq), lambda i: (i, 0)), kinds, a_spec, b_spec],
        out_specs=pl.BlockSpec((block, 2 * D), lambda i: (i, 0)),
        out_shape=jax.ShapeDtypeStruct((D, 2 * D), jnp.bfloat16),
        compiler_params=pltpu.CompilerParams(vmem_limit_bytes=VMEM),
        cost_estimate=cost(5),
    )(xt, d3, a, b)


def ffn_grad_kernel(dh_ref, act_ref, low_ref, dlow_ref, g_ref):
    per, two, _ = g_ref.shape
    own = two // 2
    g_ref[:, :own] = dot(dh_ref[...], low_ref[...], TN).astype(jnp.bfloat16).reshape(per, own, D)
    g_ref[:, own:] = dot(act_ref[...], dlow_ref[...], TN).astype(jnp.bfloat16).reshape(per, own, D)


def ffn_grads(dh, act, low, dlow, own, cols=768):
    seq = dh.shape[0]
    if own % 16:
        parts = [dot(a, b, TN).astype(jnp.bfloat16).reshape(-1, own, D) for a, b in ((dh, low), (act, dlow))]
        return jnp.concatenate(parts, axis=1)
    hidden = pl.BlockSpec((seq, cols), lambda i: (0, i))
    wide = pl.BlockSpec((seq, D), lambda i: (0, 0))
    return pl.pallas_call(
        ffn_grad_kernel,
        grid=(FF // cols,),
        in_specs=[hidden, hidden, wide, wide],
        out_specs=pl.BlockSpec((cols // own, 2 * own, D), lambda i: (i, 0, 0)),
        out_shape=jax.ShapeDtypeStruct((FF // own, 2 * own, D), jnp.bfloat16),
        compiler_params=pltpu.CompilerParams(vmem_limit_bytes=VMEM),
        cost_estimate=cost(16),
    )(dh, act, low, dlow)


def row_norm(r):
    mean = jnp.mean(r, axis=-1, keepdims=True)
    cen = r - mean
    inv = lax.rsqrt(jnp.mean(cen * cen, axis=-1, keepdims=True) + NORM_EPS)
    return cen * inv, inv


def row_norm_back(cot, n, inv, gain):
    e = cot * gain
    return inv * (e - jnp.mean(e, axis=-1, keepdims=True) - n * jnp.mean(e * n, axis=-1, keepdims=True))


def gelu_both(x):
    cdf = 0.5 * (1.0 + lax.erf(x * 0.7071067811865476))
    dens = jnp.exp(-0.5 * x * x) * 0.3989422804014327
    return x * cdf, cdf + x * dens


def weight_copies(w_ref, wi_ref, wo_ref, sem):
    owners, own, _ = wi_ref.shape
    per = 768 // own
    copies = []
    for c in range(owners // per):
        here = pl.ds(c * per, per)
        copies.append((
            pltpu.make_async_copy(w_ref.at[here, pl.ds(0, own), :], wi_ref.at[here], sem.at[0, c]),
            pltpu.make_async_copy(w_ref.at[here, pl.ds(own, own), :], wo_ref.at[here], sem.at[1, c]),
        ))
    return per, copies


def by_step(w_ref, wi_ref, wo_ref, sem, body):
    per, copies = weight_copies(w_ref, wi_ref, wo_ref, sem)
    i = pl.program_id(0)

    @pl.when(i == 0)
    def _():
        for pair in copies:
            for copy in pair:
                copy.start()

        def wait(c):
            for copy in copies[c]:
                copy.wait()

        body(per, len(copies), wait)

    @pl.when(i > 0)
    def _():
        body(per, len(copies), lambda c: None)


def ffn_scratch(w_all, block):
    owners, rows, _ = w_all.shape
    own = (rows - 8) // 2
    return [
        pltpu.VMEM((owners, own, D), jnp.bfloat16),
        pltpu.VMEM((owners, own, D), jnp.bfloat16),
        pltpu.VMEM((block, FF), jnp.bfloat16),
        pltpu.SemaphoreType.DMA((2, owners * own // 768)),
    ]


def middle_kernel(len_ref, at_ref, c_ref, mine_ref, peer_ref, x_ref, mask_ref, w_ref, b_ref, cot_ref, rl_ref, small_ref,
                  low_ref, act_ref, dh_ref, dlow_ref, out_ref, dr1_ref, da_ref, dc_ref, gb_ref, red_ref,
                  wi_ref, wo_ref, slope_ref, sem, wa_ref, wa_sem, *, block):
    i = pl.program_id(0)
    f32, b16 = jnp.float32, jnp.bfloat16

    _, zs, _, rows, cols = mine_ref.shape

    def projection_copies():
        z0, y0, c0 = at_ref[0], at_ref[1], at_ref[2]
        copies = []
        for c, src in enumerate((mine_ref, peer_ref)):
            for y in range(2):
                for z in range(zs):
                    owner = (lax.rem(z0 + z, zs) * 2 + lax.rem(y0 + y, 2)) * 2 + lax.rem(c0 + c, 2)
                    first = pl.multiple_of(owner * rows, rows)
                    for k in range(3):
                        there = wa_ref.at[pl.ds(first, rows), pl.ds(k * cols, cols)]
                        copies.append(pltpu.make_async_copy(src.at[y, z, 3 + k], there, wa_sem.at[len(copies)]))
        return copies

    @pl.when(i == 0)
    def _():
        copies = projection_copies()
        for copy in copies:
            copy.start()
        red_ref[...] = jnp.zeros_like(red_ref)
        gb_ref[...] = jnp.zeros_like(gb_ref)
        for copy in copies:
            copy.wait()

    def body(per, chunks, wait):
        def weights(ref, c):
            return ref[c * per : c * per + per].reshape(-1, D)

        mixed = jnp.where(mask_ref[...] > 0.5, small_ref[8:9], x_ref[...].astype(f32))
        n1, inv1 = row_norm(mixed + dot(c_ref[...], wa_ref[...]) + small_ref[2:3])
        first = n1 * small_ref[3:4] + small_ref[4:5]
        low = first.astype(b16)
        low_ref[...] = low
        acc = None
        for c in range(chunks):
            wait(c)
            cols = slice(c * 768, c * 768 + 768)
            act, slo = gelu_both(dot(low, weights(wi_ref, c), NT) + b_ref[:, cols])
            act = act.astype(b16)
            act_ref[:, cols] = act
            slope_ref[:, cols] = slo.astype(b16)
            part = dot(act, weights(wo_ref, c))
            acc = part if acc is None else acc + part
        n2, inv2 = row_norm(first + (acc + small_ref[7:8]))
        out_ref[...] = n2 * small_ref[5:6] + small_ref[6:7]
        at = lax.broadcasted_iota(jnp.int32, (block, D), 0) + i * block
        cot = jnp.where(at < len_ref[0], cot_ref[...].astype(f32), 0.0)
        dres = row_norm_back(cot, n2, inv2, small_ref[5:6])
        dlow = dres.astype(b16)
        dlow_ref[...] = dlow
        for k, v in enumerate((cot * n2, cot, dlow.astype(f32))):
            red_ref[3 + k : 4 + k] += jnp.sum(v, axis=0, keepdims=True)
        acc = dres
        for c in range(chunks):
            cols = slice(c * 768, c * 768 + 768)
            dh = (dot(dlow, weights(wo_ref, c), NT) * slope_ref[:, cols].astype(f32)).astype(b16)
            dh_ref[:, cols] = dh
            gb_ref[:, cols] += jnp.sum(dh.astype(f32), axis=0, keepdims=True)
            acc = acc + dot(dh, weights(wi_ref, c))
        dr1 = row_norm_back(acc, n1, inv1, small_ref[3:4])
        da = dr1.astype(b16)
        dr1_ref[...] = dr1
        da_ref[...] = da
        dc_ref[...] = (dot(da, wa_ref[...], NT) * rl_ref[...]).astype(b16)
        for k, v in enumerate((da.astype(f32), acc * n1, acc)):
            red_ref[k : k + 1] += jnp.sum(v, axis=0, keepdims=True)

    by_step(w_ref, wi_ref, wo_ref, sem, body)


def middle(length, at, ctx, mine, peer, rounded, mask, w_all, bias, cot, rl, small, block=256):
    seq = ctx.shape[0]
    wide = pl.BlockSpec((block, D), lambda i, n, a: (i, 0))
    hidden = pl.BlockSpec((block, FF), lambda i, n, a: (i, 0))
    one = pl.BlockSpec((1, FF), lambda i, n, a: (0, 0))
    hbm = pl.BlockSpec(memory_space=pl.ANY)
    zs = mine.shape[1]
    f32, b16 = jnp.float32, jnp.bfloat16

    def shape(cols, kind, rows=seq):
        return jax.ShapeDtypeStruct((rows, cols), kind)

    return pl.pallas_call(
        functools.partial(middle_kernel, block=block),
        grid_spec=pltpu.PrefetchScalarGridSpec(
            num_scalar_prefetch=2,
            grid=(seq // block,),
            in_specs=[wide, hbm, hbm, wide, pl.BlockSpec((block, 1), lambda i, n, a: (i, 0)),
                      pl.BlockSpec(memory_space=pl.ANY), one, wide, wide, pl.BlockSpec((9, D), lambda i, n, a: (0, 0))],
            out_specs=[wide, hidden, hidden, wide, wide, wide, wide, wide, one, pl.BlockSpec((8, D), lambda i, n, a: (0, 0))],
            scratch_shapes=ffn_scratch(w_all, block)
            + [pltpu.VMEM((D, D), b16), pltpu.SemaphoreType.DMA((12 * zs,))],
        ),
        out_shape=[shape(D, b16), shape(FF, b16), shape(FF, b16), shape(D, b16), shape(D, f32), shape(D, f32),
                   shape(D, b16), shape(D, b16), shape(FF, f32, 1), shape(D, f32, 8)],
        compiler_params=pltpu.CompilerParams(vmem_limit_bytes=VMEM),
        cost_estimate=cost(40),
    )(length, at, ctx, mine, peer, rounded, mask, w_all, bias, cot, rl, small)


def input_kernel(dr_ref, d0_ref, d1_ref, d2_ref, w0_ref, w1_ref, w2_ref, z_ref, wg_ref, mask_ref,
                 fg_ref, red_ref):
    i = pl.program_id(0)
    acc = dr_ref[...] + dot(z_ref[...], wg_ref[...], TN)
    qs, vs = [], []
    for d_ref, w_ref in ((d0_ref, w0_ref), (d1_ref, w1_ref), (d2_ref, w2_ref)):
        for k in range(3):
            acc += dot(d_ref[k], w_ref[k], NT)
        qs.append(jnp.sum(d_ref[0].astype(jnp.float32), axis=0, keepdims=True))
        vs.append(jnp.sum(d_ref[2].astype(jnp.float32), axis=0, keepdims=True))
    masked = mask_ref[...] > 0.5
    fg_ref[...] = jnp.where(masked, 0.0, acc)
    dm = jnp.sum(jnp.where(masked, acc, 0.0), axis=0, keepdims=True)
    red = jnp.concatenate(
        [jnp.concatenate(qs, axis=1), jnp.concatenate(vs, axis=1), dm, jnp.zeros((5, D), jnp.float32)], axis=0
    )

    @pl.when(i == 0)
    def _():
        red_ref[...] = red

    @pl.when(i > 0)
    def _():
        red_ref[...] += red


def input_grad(dr1, ds, ws, dz, wg, mask, block=256):
    seq = dr1.shape[0]
    wide = pl.BlockSpec((block, D), lambda i: (i, 0))
    part = pl.BlockSpec((3, block, 256), lambda i: (0, i, 0))
    wpart = pl.BlockSpec((3, D, 256), lambda i: (0, 0, 0))
    return pl.pallas_call(
        input_kernel,
        grid=(seq // block,),
        in_specs=[wide, part, part, part, wpart, wpart, wpart,
                  pl.BlockSpec((dz.shape[0], block), lambda i: (0, i)),
                  pl.BlockSpec(wg.shape, lambda i: (0, 0)),
                  pl.BlockSpec((block, 1), lambda i: (i, 0))],
        out_specs=[wide, pl.BlockSpec((8, D), lambda i: (0, 0))],
        out_shape=[jax.ShapeDtypeStruct((seq, D), jnp.float32), jax.ShapeDtypeStruct((8, D), jnp.float32)],
        compiler_params=pltpu.CompilerParams(vmem_limit_bytes=VMEM),
        cost_estimate=cost(8),
    )(dr1, *ds, *ws, dz, wg, mask)


def split3(x):
    hi = x.astype(jnp.bfloat16)
    rest = x - hi.astype(jnp.float32)
    mid = rest.astype(jnp.bfloat16)
    low = (rest - mid.astype(jnp.float32)).astype(jnp.bfloat16)
    return hi, mid, low


def tree_sum(parts):
    while len(parts) > 1:
        half = len(parts) // 2
        parts = [parts[i] + parts[i + half] for i in range(half)]
    return parts[0]


def added(parts):
    return sum(p.astype(jnp.float32) for p in parts)


class Net:
    def __init__(self, dp_size, t_size):
        self.t = t_size
        self.sizes = {"z": dp_size // 4, "y": 2, "c": 2, "x": t_size}
        d = lax.axis_index("dp")
        self.at = {"z": d // 4, "y": d // 2 % 2, "c": d % 2, "x": lax.axis_index("tensor")}

    def shift(self, v, axis, k, swap=False):
        pairs = []
        sz = self.sizes
        for z in range(sz["z"]):
            for y in range(2):
                for c in range(2):
                    for x in range(sz["x"]):
                        src = {"z": z, "y": y, "c": c, "x": x}
                        dst = dict(src)
                        dst[axis] = src[axis] ^ k if swap else (src[axis] - k) % sz[axis]
                        flat = [((q["z"] * 2 + q["y"]) * 2 + q["c"]) * sz["x"] + q["x"] for q in (src, dst)]
                        pairs.append(tuple(flat))
        return lax.ppermute(v, ("dp", "tensor"), pairs)

    def gather(self, v, axis, dim):
        return jnp.concatenate([v] + [self.shift(v, axis, k) for k in range(1, self.sizes[axis])], axis=dim)

    def scatter(self, parts, axis, dim):
        n = self.sizes[axis]
        at = self.at[axis]

        def slot(i):
            return [lax.dynamic_index_in_dim(p, i, dim, False) for p in parts]

        arrived = []
        for k in range(1, n):
            send = added(slot((at + k) % n)).astype(jnp.bfloat16)
            arrived.append(self.shift(send, axis, n - k))
        return slot(at), arrived

    def gather_own(self, v, axis, dim):
        n = self.sizes[axis]
        at = self.at[axis]
        out = jnp.zeros(v.shape[:dim] + (n,) + v.shape[dim:], v.dtype)
        for k in range(n):
            part = v if k == 0 else self.shift(v, axis, k)
            out = lax.dynamic_update_index_in_dim(out, part, (at + k) % n, dim)
        return out

    def total(self, v, axes=("c", "x", "y", "z")):
        for axis in axes:
            bit = 1
            while bit < self.sizes[axis]:
                v = v + self.shift(v, axis, bit, True)
                bit *= 2
        return v


def rolled(net, v, dims, sign):
    for dim, axis in dims:
        v = jnp.roll(v, sign * net.at[axis], dim)
    return v


def wide_rows(net, places, mine, peer):
    if mine.shape[3] % 16 == 0:
        return places, mine, peer
    zs, kinds, cols = net.sizes["z"], mine.shape[2], mine.shape[4]
    v = rolled(net, jnp.stack([mine, peer]), ((0, "c"), (1, "y"), (2, "z")), 1)
    v = v.transpose(2, 1, 0, 4, 3, 5)
    v = v.reshape(1, 2, 2, -1, kinds, cols).transpose(2, 1, 0, 4, 3, 5)
    return places * 0, v[0], v[1]


def local(dp_size, t_size, features, lengths, span_starts, buckets, cotangent,
          qkv_w, qkv_m, qkv_v, out_w, out_m, out_v, ffn_in, ffn_in_m, ffn_in_v,
          ffn_out, ffn_out_m, ffn_out_v, small_params, small_m, small_v,
          pos_table, pos_m, pos_v, gate_proj, gate_m, gate_v, step_count):
    f32, b16 = jnp.float32, jnp.bfloat16
    net = Net(dp_size, t_size)
    zs = net.sizes["z"]
    seq = features.shape[1]
    own = ffn_out.shape[0]
    rows = qkv_w.shape[1]
    scale = HD**-0.5

    bar = lax.optimization_barrier
    places = jnp.stack([net.at["z"], net.at["y"], net.at["c"], net.at["x"]]).astype(jnp.int32)
    cols = D // GROUPS
    group_heads = H // GROUPS
    both = ("dp", "tensor")

    qkv_low = qkv_w[None, None]
    u0, u1, u2 = [qkv_low[..., g * cols : (g + 1) * cols].astype(b16) for g in range(3)]
    z0 = net.gather(u0, "z", 1)
    rev = jnp.flip(buckets)
    order = jnp.concatenate([rev[127:], jnp.full((1,), -1, jnp.int32), rev[:127]])
    onehot = (jnp.arange(NB, dtype=jnp.int32)[:, None] == order[None, :]).astype(b16)
    off3 = dot(jnp.concatenate(split3(pos_table[:NB].T), axis=0), onehot).reshape(3, H, 2 * seq)
    table = bias_tables(off3[0] + off3[1] + off3[2])
    bias_row = jnp.pad(ffn_in[D:].astype(b16), ((0, 7), (0, D - own)))
    ffn_own = jnp.concatenate([ffn_in[:D].T.astype(b16), ffn_out.astype(b16), bias_row])
    z0, u1, table, features, ffn_own, out_w, gate_proj = bar((z0, u1, table, features, ffn_own, out_w, gate_proj))

    w_all = lax.all_gather(ffn_own, both, axis=0)
    w_all_k = w_all
    if own % 16:
        w_all_k = jnp.concatenate(
            [w_all[:, k * own : (k + 1) * own].reshape(4, -1, D) for k in range(2)] + [jnp.zeros((4, 8, D), b16)], axis=1)

    y0 = net.gather(z0, "y", 0)
    z1 = net.gather(u1, "z", 1)
    positions = jnp.arange(seq, dtype=jnp.int32)
    starts = span_starts[0]
    masked = jnp.any((positions[:, None] >= starts[None, :]) & (positions[:, None] < starts[None, :] + SPAN), axis=1)[:, None]
    mask = masked.astype(f32)
    rounded = jnp.where(masked, small_params[8][None, :].astype(b16), features[0])
    ga = jnp.sum(gate_proj[:HD, :4], axis=1)
    gb = jnp.sum(gate_proj[:HD, 4:], axis=1)
    za = jnp.sum(gate_proj[HD, :4])
    zb = jnp.sum(gate_proj[HD, 4:])
    eye = jnp.eye(H, dtype=f32)[:, :, None]
    wg = jnp.concatenate([(eye * ga).reshape(H, D), (eye * gb).reshape(H, D)], axis=0)
    wg3 = split3(wg)
    z3 = dot(jnp.concatenate(wg3, axis=0), rounded, NT).reshape(3, 2 * H, seq)
    z_all = z3[0] + z3[1] + z3[2]
    gate_a = jax.nn.sigmoid(z_all[:H] + za)
    gate_b = jax.nn.sigmoid(z_all[H:] + zb)
    const = pos_table[NB][:, None]
    gates = (gate_a * (gate_b * const - 1.0) + 2.0).reshape(H, 1, seq)
    rounded_t = rounded.T
    bias3 = jnp.stack([small_params[0], jnp.zeros((D,), f32), small_params[1]])[:, None, :]
    out_parts = out_w.astype(b16).reshape(rows, 3, cols).transpose(1, 0, 2)[None, None]
    u2 = jnp.concatenate([u2, out_parts], axis=2)
    y0, z1, u2, rounded, gates, rounded_t = bar((y0, z1, u2, rounded, gates, rounded_t))

    p0 = net.shift(y0, "c", 1)

    def attend(g, mine, peer, kept):
        at, mine, peer = wide_rows(net, places, mine, peer)
        bias = bias3[:, :, g * cols : (g + 1) * cols]
        return attn_fwd(lengths, at, rounded, mine, peer, bias, table, gates, g * group_heads, group_heads, kept)

    p0, z1, u2 = bar((p0, z1, u2))
    y1 = net.gather(z1, "y", 0)
    z2 = net.gather(u2, "z", 1)
    probs0, *kept, q0, w0 = attend(0, y0, p0, ())
    y1, z2, probs0, q0, w0, *kept = bar((y1, z2, probs0, q0, w0, *kept))
    p1 = net.shift(y1, "c", 1)
    y2 = net.gather(z2, "y", 0)
    probs1, *kept, q1, w1 = attend(1, y1, p1, kept)
    y2, probs1, q1, w1, *kept = bar((y2, probs1, q1, w1, *kept))
    p2 = net.shift(y2, "c", 1)
    probs2, context, context_f, inv_sum, q2, w2 = attend(2, y2, p2, kept)
    qkv, w_qkv, probs = (q0, q1, q2), (w0, w1, w2), (probs0, probs1, probs2)

    at2, mine2, peer2 = wide_rows(net, places, y2, p2)
    bias_in = w_all[:, 2 * own, :own].reshape(1, -1).astype(f32)
    low, act, d_hidden, d_branch, layer_out, d_res1, d_attention, d_context, g_bias_in, red = middle(
        lengths, at2, context, mine2, peer2, rounded, mask, w_all_k, bias_in, cotangent[0], inv_sum, small_params)

    def attend_back(g):
        return attn_bwd(qkv[g], d_context, context_f, probs[g], table, gates, g * group_heads, group_heads)

    def by_owner(v):
        return v.reshape(zs, 2, 2, rows, v.shape[-1])

    g_ffn = ffn_grads(d_hidden, act, low, d_branch, own)
    g_ffn, d_context = bar((g_ffn, d_context))
    g_ffn = lax.psum_scatter(g_ffn.reshape(dp_size, t_size, 2 * own, D), "dp", scatter_dimension=0, tiled=False)
    d0, dg0, do0 = attend_back(0)
    m1 = by_owner(weight_grads(rounded_t, d0, context, d_attention))
    m1, d0, dg0, do0, d_context = bar((m1, d0, dg0, do0, d_context))
    stay_1, got_1 = net.scatter([m1], "c", 2)
    d1, dg1, do1 = attend_back(1)
    got_1, d1, dg1, do1, d_context = bar((got_1, d1, dg1, do1, d_context))
    stay_1, got_1 = net.scatter(stay_1 + got_1, "y", 1)
    d2, dg2, do2 = attend_back(2)
    got_1, d2, dg2, do2 = bar((got_1, d2, dg2, do2))
    m2 = by_owner(weight_grads(rounded_t, d1, d2, jnp.zeros((8, 128), f32)))
    m2, dg0, dg1, dg2, do0, do1, do2 = bar((m2, dg0, dg1, dg2, do0, do1, do2))
    stay_2, got_2 = net.scatter([m2], "c", 2)
    dgate = jnp.concatenate([dg0, dg1, dg2], axis=0).reshape(H, seq)
    d_a = dgate * (gate_b * const - 1.0) * gate_a * (1.0 - gate_a)
    d_b = dgate * gate_a * const * gate_b * (1.0 - gate_b)
    d_const = jnp.sum(dgate * gate_a * gate_b, axis=1, keepdims=True)
    dz = jnp.concatenate([d_a, d_b], axis=0)
    dz_hi = dz.astype(b16)
    dz_lo = (dz - dz_hi.astype(f32)).astype(b16)
    got_2, got_1, dz, dz_hi, dz_lo, d_const, d_res1 = bar((got_2, got_1, dz, dz_hi, dz_lo, d_const, d_res1))

    stay_2, got_2 = net.scatter(stay_2 + got_2, "y", 1)
    stay_1, got_1 = net.scatter(stay_1 + got_1, "z", 0)
    feature_grad, red0 = input_grad(
        d_res1, (d0, d1, d2), w_qkv, jnp.concatenate([dz_hi, dz_lo, dz_hi], axis=0),
        jnp.concatenate([wg3[0], wg3[0], wg3[1]], axis=0), mask)
    small_local = jnp.concatenate([red0[:2], red[:6], red0[2:3]], axis=0)
    got_2, got_1, feature_grad, small_local, do0, do1, do2, dz = bar(
        (got_2, got_1, feature_grad, small_local, do0, do1, do2, dz))
    stay_2, got_2 = net.scatter(stay_2 + got_2, "z", 0)
    m1 = added(stay_1 + got_1).astype(b16)
    m1 = tree_sum([m1.astype(f32)] + [net.shift(m1, "x", k).astype(f32) for k in range(1, t_size)])
    exact = lax.Precision.HIGHEST
    g_z2 = dot(jnp.concatenate([dz_hi, dz_lo], axis=0), rounded)
    of_head = jnp.arange(D)[None, :] // HD == jnp.arange(2 * H)[:, None] % H
    g_z = jnp.where(of_head, g_z2[: 2 * H] + g_z2[2 * H :], 0.0)
    kind = (jnp.arange(2 * H)[None, :] // H == jnp.arange(2)[:, None]).astype(f32)
    fold = (jnp.arange(D)[:, None] % HD == jnp.arange(HD)[None, :]).astype(f32)
    g_z = jnp.dot(jnp.dot(kind, g_z, precision=exact), fold, precision=exact)
    g_zb = jnp.dot(kind, jnp.sum(dz, axis=1, keepdims=True), precision=exact)
    doff = jnp.concatenate([do0, do1, do2], axis=0).reshape(H, 2 * seq)
    pos3 = dot(jnp.concatenate(split3(doff), axis=0), onehot, NT)
    pos_t = jnp.concatenate([pos3[:H] + pos3[H : 2 * H] + pos3[2 * H :], d_const], axis=1)

    wide = 384
    packed = jnp.concatenate(
        [small_local[:, :wide], small_local[:, wide:]]
        + [g_bias_in[:, k * wide : (k + 1) * wide] for k in range(FF // wide)]
        + [jnp.pad(pos_t, ((0, 0), (0, wide - NB - 1))),
           jnp.pad(jnp.concatenate([g_z, g_zb], axis=1), ((0, 0), (0, wide - HD - 1)))], axis=0)
    got_2, m1, packed, g_ffn = bar((got_2, m1, packed, g_ffn))
    m2 = added(stay_2 + got_2).astype(b16)
    m2 = tree_sum([m2.astype(f32)] + [net.shift(m2, "x", k).astype(f32) for k in range(1, t_size)])
    stay_f, got_f = net.scatter([g_ffn], "x", 0)
    g_ffn = added(stay_f + got_f)
    own_ffn = jnp.sum(jnp.square(g_ffn)) + jnp.sum(jnp.square(m1)) * (1.0 / t_size)
    g_in_t = g_ffn[:own].T
    g_outw = g_ffn[own:]
    own_sum = jnp.sum(jnp.square(m2)) * (1.0 / t_size) + own_ffn
    used = packed.shape[0]
    flat = jnp.concatenate([packed, jnp.full((48 - used, wide), own_sum)], axis=0)
    flat = net.total(flat)
    own_sum = flat[used, 0]
    flat = flat[:used]
    shared = jnp.sum(jnp.square(flat)) + 3.0 * jnp.sum(jnp.square(flat[38:40]))
    m1 = m1.reshape(rows, 2, 3, cols)
    m2 = m2.reshape(rows, 2, 3, cols)
    g_qkv = jnp.stack([m1[:, 0], m2[:, 0], m2[:, 1]], axis=2).transpose(1, 0, 2, 3).reshape(3, rows, D)
    g_out = m1[:, 1].reshape(rows, D)
    g_small = jnp.concatenate([flat[:9], flat[9:18]], axis=1)
    g_bias = flat[18:26].reshape(-1, own)
    g_pos = flat[26:38, : NB + 1].T
    g_gate = jnp.repeat(flat[38:40, : HD + 1].T, 4, axis=1)
    grad_norm = jnp.sqrt(own_sum + shared)
    clip = jnp.minimum(1.0, CLIP_NORM / (grad_norm + 1e-06))
    count = step_count[0].astype(f32)
    me = lax.axis_index("dp") * t_size + lax.axis_index("tensor")
    g_bias = lax.dynamic_slice_in_dim(g_bias.reshape(-1, own), me, 1, 0)
    g_ffn_in = jnp.concatenate([g_in_t, g_bias], axis=0)

    qkv_new, qkv_moment, qkv_second = adam_step(qkv_w, g_qkv, qkv_m, qkv_v, clip, 2.0 * D**-0.5, count)
    out_new, out_moment, out_second = adam_step(out_w, g_out, out_m, out_v, clip, 1.0, count)
    in_new, in_moment, in_second = adam_step(ffn_in, g_ffn_in, ffn_in_m, ffn_in_v, clip, 2.0 * D**-0.5, count)
    fo_new, fo_moment, fo_second = adam_step(ffn_out, g_outw, ffn_out_m, ffn_out_v, clip, 2.0 * FF**-0.5, count)
    small_new, small_moment, small_second = adam_step(small_params, g_small, small_m, small_v, clip, 0.5, count)
    pos_new, pos_moment, pos_second = adam_step(pos_table, g_pos, pos_m, pos_v, clip, 1.0, count)
    gate_new, gate_moment, gate_second = adam_step(gate_proj, g_gate, gate_m, gate_v, clip, 2.0 * HD**-0.5, count)
    return (
        layer_out[None], feature_grad[None], grad_norm.reshape(1),
        qkv_new, qkv_moment, qkv_second, qkv_new.astype(b16),
        out_new, out_moment, out_second, out_new.astype(b16),
        in_new, in_moment, in_second, in_new.astype(b16),
        fo_new, fo_moment, fo_second, fo_new.astype(b16),
        g_small, small_new, small_moment, small_second,
        pos_new, pos_moment, pos_second, gate_new, gate_moment, gate_second,
    )


def solution(mesh):
    both = ("dp", "tensor")
    three = (P(None, "dp", None),)
    row = (P("dp", None),)
    col = (P(None, both),)
    rows2 = (P(both, None),)
    utt = P(both, None, None)
    in_specs = (
        (utt, P(both), P(both, None), P(), utt) + three * 3 + row * 3 + col * 3 + rows2 * 3 + (P(),) * 10
    )
    out_specs = (utt, utt, P()) + three * 4 + row * 4 + col * 4 + rows2 * 4 + (P(),) * 10
    fn = functools.partial(local, mesh.shape["dp"], mesh.shape["tensor"])
    return jax.shard_map(fn, mesh=mesh, in_specs=in_specs, out_specs=out_specs, check_vma=False)
```

```python
import functools

import jax
import jax.numpy as jnp
from jax import lax
from jax.experimental import pallas as pl
from jax.experimental.pallas import tpu as pltpu
from jax.sharding import PartitionSpec as P

D = 768
H = 12
HD = 64
FF = 3072
NB = 320
SPAN = 10
CLIP_NORM = 1.0
BETA_ONE = 0.9
BETA_TWO = 0.98
ADAM_EPS = 1e-08
DECAY_RATE = 0.01
NORM_EPS = 1e-05
NEG_BIG = -1e30
GROUPS = 3


def adam_step(weight, grad_in, moment, second, clip_factor, rate_in, count_in):
    scaled = grad_in * clip_factor
    new_moment = BETA_ONE * moment + (1.0 - BETA_ONE) * scaled
    new_second = BETA_TWO * second + (1.0 - BETA_TWO) * scaled * scaled
    first_fix = 1.0 - BETA_ONE**count_in
    second_fix = 1.0 - BETA_TWO**count_in
    update = new_moment / first_fix / (jnp.sqrt(new_second / second_fix) + ADAM_EPS)
    return (weight - rate_in * (update + DECAY_RATE * weight), new_moment, new_second)


VMEM = 60 << 20
NT = (((1,), (1,)), ((), ()))
TN = (((0,), (0,)), ((), ()))


def dot(a, b, dims=(((1,), (0,)), ((), ()))):
    return lax.dot_general(a, b, dims, preferred_element_type=jnp.float32)


def cost(us):
    return pl.CostEstimate(flops=0, bytes_accessed=int(us * 3.0e6), transcendentals=0)


def table_kernel(off_ref, out_ref):
    heads, _, w = out_ref.shape
    for h in range(heads):
        row = jnp.broadcast_to(off_ref[h], (8, w))
        eight = pltpu.roll(row, 0, 1, stride=1, stride_axis=0)
        for r in range(0, 128, 8):
            out_ref[h, r : r + 8] = pltpu.roll(eight, r, 1) if r else eight


def bias_tables(offr, heads=4):
    n, w = offr.shape
    return pl.pallas_call(
        table_kernel,
        grid=(n // heads,),
        in_specs=[pl.BlockSpec((heads, 1, w), lambda h: (h, 0, 0))],
        out_specs=pl.BlockSpec((heads, 128, w), lambda h: (h, 0, 0)),
        out_shape=jax.ShapeDtypeStruct((n, 128, w), jnp.float32),
        compiler_params=pltpu.CompilerParams(vmem_limit_bytes=VMEM),
        cost_estimate=cost(8),
    )(offr.reshape(n, 1, w))


def fwd_kernel(len_ref, at_ref, x_ref, mine_ref, peer_ref, bias_ref, t_ref, g_ref, *rest, seq, ib, zs, rows, kept):
    p_ref, o_ref, of_ref, rl_ref, qkv_ref, w_ref, s_ref, sem = rest[kept:]
    h = pl.program_id(0)

    @pl.when(h == 0)
    def _():
        z0, y0, c0 = at_ref[0], at_ref[1], at_ref[2]
        copies = []
        for c, src in enumerate((mine_ref, peer_ref)):
            for y in range(2):
                for z in range(zs):
                    block = (lax.rem(z0 + z, zs) * 2 + lax.rem(y0 + y, 2)) * 2 + lax.rem(c0 + c, 2)
                    first = pl.multiple_of(block * rows, rows)
                    there = w_ref.at[:, pl.ds(first, rows), :]
                    copies.append(pltpu.make_async_copy(src.at[y, z, pl.ds(0, 3)], there, sem.at[len(copies)]))
        for copy in copies:
            copy.start()
        for copy in copies:
            copy.wait()
        for k in range(3):
            r = dot(x_ref[...], w_ref[k]) + bias_ref[k]
            qkv_ref[k] = (r * HD**-0.5 if k == 0 else r).astype(jnp.bfloat16)

    par = lax.rem(h, 2)
    lane = lax.broadcasted_iota(jnp.int32, (seq, 128), 1)
    rowi = lax.broadcasted_iota(jnp.int32, (seq, 128), 0)
    inh = (lane // 64) == par
    flag = lane == (64 * (1 - par))
    one = jnp.bfloat16(1.0)
    zero = jnp.bfloat16(0.0)
    pair = pl.ds(pl.multiple_of(h // 2 * 128, 128), 128)
    bias = jnp.where(rowi < len_ref[0], 0.0, NEG_BIG).astype(jnp.bfloat16)
    qm = jnp.where(flag, one, jnp.where(inh, qkv_ref[0, :, pair], zero))
    km = jnp.where(flag, bias, qkv_ref[1, :, pair])
    vm = jnp.where(flag, one, qkv_ref[2, :, pair])
    vt = vm.T
    base = seq - 128
    def scores(i0):
        gate = g_ref[0, :, i0 : i0 + ib]
        qb = qm[i0 : i0 + ib]
        m = None
        for j0 in range(0, seq, 128):
            c0 = i0 - j0 + base
            s = dot(km[j0 : j0 + 128], qb, NT) + t_ref[0, :, c0 : c0 + ib] * gate
            s_ref[i0 // ib % 2, j0 : j0 + 128, :] = s
            mm = jnp.max(s.reshape(16, 8, ib), axis=0)
            m = mm if m is None else jnp.maximum(m, mm)
        return jnp.max(m, axis=0, keepdims=True)

    m = scores(0)
    for i0 in range(0, seq, ib):
        m_next = scores(i0 + ib) if i0 + ib < seq else None
        for j0 in range(0, seq, 128):
            e = jnp.exp(s_ref[i0 // ib % 2, j0 : j0 + 128, :] - m).astype(jnp.bfloat16)
            p_ref[0, j0 : j0 + 128, i0 : i0 + ib] = e
        m = m_next
        ct = dot(vt, p_ref[0, :, i0 : i0 + ib])
        total = jnp.where(par == 0, ct[64:65], ct[0:1])
        rl = 1.0 / total
        oc = (ct * rl).T
        rc = jnp.broadcast_to(rl, (128, ib)).T
        ih = inh[i0 : i0 + ib]
        o_ref[i0 : i0 + ib, :] = jnp.where(ih, oc.astype(jnp.bfloat16), o_ref[i0 : i0 + ib, :])
        of_ref[i0 : i0 + ib, :] = jnp.where(ih, oc, of_ref[i0 : i0 + ib, :])
        rl_ref[i0 : i0 + ib, :] = jnp.where(ih, rc, rl_ref[i0 : i0 + ib, :])


def attn_fwd(length, at, x, mine, peer, bias, table, gates, head0, heads, kept, ib=256):
    seq = x.shape[0]
    _, zs, _, rows, cols = mine.shape
    w = table.shape[-1]
    f32, b16 = jnp.float32, jnp.bfloat16
    out_pair = pl.BlockSpec((seq, 128), lambda h, n, a: (0, head0 // 2 + h // 2))
    hbm = pl.BlockSpec(memory_space=pl.ANY)
    return pl.pallas_call(
        functools.partial(fwd_kernel, seq=seq, ib=ib, zs=zs, rows=rows, kept=len(kept)),
        grid_spec=pltpu.PrefetchScalarGridSpec(
            num_scalar_prefetch=2,
            grid=(heads,),
            in_specs=[
                pl.BlockSpec((seq, D), lambda h, n, a: (0, 0)),
                hbm,
                hbm,
                pl.BlockSpec((3, 1, cols), lambda h, n, a: (0, 0, 0)),
                pl.BlockSpec((1, 128, w), lambda h, n, a: (head0 + h, 0, 0)),
                pl.BlockSpec((1, 1, seq), lambda h, n, a: (head0 + h, 0, 0)),
            ] + [hbm] * len(kept),
            out_specs=[pl.BlockSpec((1, seq, seq), lambda h, n, a: (h, 0, 0)), out_pair, out_pair, out_pair,
                       pl.BlockSpec((3, seq, cols), lambda h, n, a: (0, 0, 0)),
                       pl.BlockSpec((3, D, cols), lambda h, n, a: (0, 0, 0))],
            scratch_shapes=[pltpu.VMEM((2, seq, ib), f32), pltpu.SemaphoreType.DMA((4 * zs,))],
        ),
        out_shape=[jax.ShapeDtypeStruct((heads, seq, seq), b16), jax.ShapeDtypeStruct((seq, D), b16),
                   jax.ShapeDtypeStruct((seq, D), f32), jax.ShapeDtypeStruct((seq, D), f32),
                   jax.ShapeDtypeStruct((3, seq, cols), b16), jax.ShapeDtypeStruct((3, D, cols), b16)],
        input_output_aliases={8: 1, 9: 2, 10: 3} if kept else {},
        compiler_params=pltpu.CompilerParams(vmem_limit_bytes=VMEM),
        cost_estimate=cost(2.7 * heads + 4),
    )(length, at, x, mine, peer, bias, table, gates, *kept)


def bwd_kernel(q_ref, k_ref, v_ref, dc_ref, c_ref, p_ref, t_ref, g_ref, d_ref, dg_ref, do_ref, a_ref, ds_ref, *, seq, ib):
    par = lax.rem(pl.program_id(0), 2)
    lane = lax.broadcasted_iota(jnp.int32, (seq, 128), 1)
    inh = (lane // 64) == par
    f0 = lane == (64 * (1 - par))
    f1 = lane == (64 * (1 - par) + 1)
    one = jnp.bfloat16(1.0)
    dc = dc_ref[...]
    dcf = jnp.where(inh, dc.astype(jnp.float32), 0.0)
    delta = -jnp.sum(dcf * c_ref[...], axis=1, keepdims=True)
    hi = delta.astype(jnp.bfloat16).astype(jnp.float32)
    lo = delta - hi
    dca = jnp.where(f0, hi, jnp.where(f1, lo, dcf)).astype(jnp.bfloat16)
    va = jnp.where(f0 | f1, one, v_ref[0])
    kt = k_ref[0].T
    q = q_ref[0]
    base = seq - 128
    a_ref[...] = jnp.zeros_like(a_ref)
    dv = dot(p_ref[0], dc)
    d_ref[2] = jnp.where(inh, dv.astype(jnp.bfloat16), d_ref[2])
    for i0 in range(0, seq, ib):
        gate = g_ref[0, :, i0 : i0 + ib]
        dcb = dca[i0 : i0 + ib]
        dg = jnp.zeros((8, ib), jnp.float32)
        for j0 in range(0, seq, 128):
            c0 = i0 - j0 + base
            ds = dot(va[j0 : j0 + 128], dcb, NT) * p_ref[0, j0 : j0 + 128, i0 : i0 + ib].astype(jnp.float32)
            ds_ref[j0 : j0 + 128, i0 : i0 + ib] = ds.astype(jnp.bfloat16)
            dg = dg + jnp.sum((ds * t_ref[0, :, c0 : c0 + ib]).reshape(16, 8, ib), axis=0)
            a_ref[:, c0 : c0 + ib] += ds * gate
        dg_ref[0, :, i0 : i0 + ib] = jnp.sum(dg, axis=0, keepdims=True)
        dqt = dot(kt, ds_ref[:, i0 : i0 + ib]).T * HD**-0.5
        d_ref[0, i0 : i0 + ib, :] = jnp.where(inh[i0 : i0 + ib], dqt.astype(jnp.bfloat16), d_ref[0, i0 : i0 + ib, :])
    dk = dot(ds_ref[...], q)
    d_ref[1] = jnp.where(inh, dk.astype(jnp.bfloat16), d_ref[1])
    a = a_ref[...]
    w = a.shape[1]
    r = 64
    while r >= 8:
        a = a[:r] + pltpu.roll(a[r:], w - r, 1)
        r //= 2
    acc = a[0:1]
    for r in range(1, 8):
        acc = acc + pltpu.roll(a[r : r + 1], w - r, 1)
    do_ref[0] = acc


def attn_bwd(qkv, dctx, ctx, probs, table, gates, head0, heads, ib=256):
    seq = qkv.shape[1]
    w = table.shape[-1]

    def part(k):
        return pl.BlockSpec((1, seq, 128), lambda h: (k, 0, h // 2))

    pair = pl.BlockSpec((seq, 128), lambda h: (0, head0 // 2 + h // 2))
    return pl.pallas_call(
        functools.partial(bwd_kernel, seq=seq, ib=ib),
        grid=(heads,),
        in_specs=[
            part(0),
            part(1),
            part(2),
            pair,
            pair,
            pl.BlockSpec((1, seq, seq), lambda h: (h, 0, 0)),
            pl.BlockSpec((1, 128, w), lambda h: (head0 + h, 0, 0)),
            pl.BlockSpec((1, 1, seq), lambda h: (head0 + h, 0, 0)),
        ],
        out_specs=[
            pl.BlockSpec((3, seq, 128), lambda h: (0, 0, h // 2)),
            pl.BlockSpec((1, 1, seq), lambda h: (h, 0, 0)),
            pl.BlockSpec((1, 1, w), lambda h: (h, 0, 0)),
        ],
        scratch_shapes=[pltpu.VMEM((128, w), jnp.float32), pltpu.VMEM((seq, seq), jnp.bfloat16)],
        out_shape=[
            jax.ShapeDtypeStruct((3, seq, heads * HD), jnp.bfloat16),
            jax.ShapeDtypeStruct((heads, 1, seq), jnp.float32),
            jax.ShapeDtypeStruct((heads, 1, w), jnp.float32),
        ],
        compiler_params=pltpu.CompilerParams(vmem_limit_bytes=VMEM),
        cost_estimate=cost(3.0 * heads),
    )(qkv, qkv, qkv, dctx, ctx, probs, table, gates)


def wgrad_kernel(xt_ref, d_ref, a_ref, b_ref, g_ref, *, pair):
    xt = xt_ref[...]
    for k in range(3):
        g_ref[:, k * 256 : k * 256 + 256] = dot(xt, d_ref[k]).astype(jnp.bfloat16)
    if pair:
        g_ref[:, 768:1536] = dot(a_ref[...], b_ref[...], TN).astype(jnp.bfloat16)
    else:
        for k in range(3):
            g_ref[:, 768 + k * 256 : 1024 + k * 256] = dot(xt, a_ref[k]).astype(jnp.bfloat16)


def weight_grads(xt, d3, a, b, block=256):
    seq = xt.shape[1]
    pair = a.ndim == 2
    kinds = pl.BlockSpec((3, seq, 256), lambda i: (0, 0, 0))
    a_spec = pl.BlockSpec((seq, block), lambda i: (0, i)) if pair else kinds
    b_spec = pl.BlockSpec((seq, D), lambda i: (0, 0)) if pair else pl.BlockSpec((8, 128), lambda i: (0, 0))
    return pl.pallas_call(
        functools.partial(wgrad_kernel, pair=pair),
        grid=(D // block,),
        in_specs=[pl.BlockSpec((block, seq), lambda i: (i, 0)), kinds, a_spec, b_spec],
        out_specs=pl.BlockSpec((block, 2 * D), lambda i: (i, 0)),
        out_shape=jax.ShapeDtypeStruct((D, 2 * D), jnp.bfloat16),
        compiler_params=pltpu.CompilerParams(vmem_limit_bytes=VMEM),
        cost_estimate=cost(5),
    )(xt, d3, a, b)


def ffn_grad_kernel(dh_ref, act_ref, low_ref, dlow_ref, g_ref):
    per, two, _ = g_ref.shape
    own = two // 2
    g_ref[:, :own] = dot(dh_ref[...], low_ref[...], TN).astype(jnp.bfloat16).reshape(per, own, D)
    g_ref[:, own:] = dot(act_ref[...], dlow_ref[...], TN).astype(jnp.bfloat16).reshape(per, own, D)


def ffn_grads(dh, act, low, dlow, own, cols=768):
    seq = dh.shape[0]
    if own % 16:
        parts = [dot(a, b, TN).astype(jnp.bfloat16).reshape(-1, own, D) for a, b in ((dh, low), (act, dlow))]
        return jnp.concatenate(parts, axis=1)
    hidden = pl.BlockSpec((seq, cols), lambda i: (0, i))
    wide = pl.BlockSpec((seq, D), lambda i: (0, 0))
    return pl.pallas_call(
        ffn_grad_kernel,
        grid=(FF // cols,),
        in_specs=[hidden, hidden, wide, wide],
        out_specs=pl.BlockSpec((cols // own, 2 * own, D), lambda i: (i, 0, 0)),
        out_shape=jax.ShapeDtypeStruct((FF // own, 2 * own, D), jnp.bfloat16),
        compiler_params=pltpu.CompilerParams(vmem_limit_bytes=VMEM),
        cost_estimate=cost(16),
    )(dh, act, low, dlow)


def row_norm(r):
    mean = jnp.mean(r, axis=-1, keepdims=True)
    cen = r - mean
    inv = lax.rsqrt(jnp.mean(cen * cen, axis=-1, keepdims=True) + NORM_EPS)
    return cen * inv, inv


def row_norm_back(cot, n, inv, gain):
    e = cot * gain
    return inv * (e - jnp.mean(e, axis=-1, keepdims=True) - n * jnp.mean(e * n, axis=-1, keepdims=True))


def gelu_both(x):
    cdf = 0.5 * (1.0 + lax.erf(x * 0.7071067811865476))
    dens = jnp.exp(-0.5 * x * x) * 0.3989422804014327
    return x * cdf, cdf + x * dens


def weight_copies(w_ref, wi_ref, wo_ref, sem):
    owners, own, _ = wi_ref.shape
    per = 768 // own
    copies = []
    for c in range(owners // per):
        here = pl.ds(c * per, per)
        copies.append((
            pltpu.make_async_copy(w_ref.at[here, pl.ds(0, own), :], wi_ref.at[here], sem.at[0, c]),
            pltpu.make_async_copy(w_ref.at[here, pl.ds(own, own), :], wo_ref.at[here], sem.at[1, c]),
        ))
    return per, copies


def by_step(w_ref, wi_ref, wo_ref, sem, body):
    per, copies = weight_copies(w_ref, wi_ref, wo_ref, sem)
    i = pl.program_id(0)

    @pl.when(i == 0)
    def _():
        for pair in copies:
            for copy in pair:
                copy.start()

        def wait(c):
            for copy in copies[c]:
                copy.wait()

        body(per, len(copies), wait)

    @pl.when(i > 0)
    def _():
        body(per, len(copies), lambda c: None)


def ffn_scratch(w_all, block):
    owners, rows, _ = w_all.shape
    own = (rows - 8) // 2
    return [
        pltpu.VMEM((owners, own, D), jnp.bfloat16),
        pltpu.VMEM((owners, own, D), jnp.bfloat16),
        pltpu.VMEM((block, FF), jnp.bfloat16),
        pltpu.SemaphoreType.DMA((2, owners * own // 768)),
    ]


def middle_kernel(len_ref, at_ref, c_ref, mine_ref, peer_ref, x_ref, mask_ref, w_ref, b_ref, cot_ref, rl_ref, small_ref,
                  low_ref, act_ref, dh_ref, dlow_ref, out_ref, dr1_ref, da_ref, dc_ref, gb_ref, red_ref,
                  wi_ref, wo_ref, slope_ref, sem, wa_ref, wa_sem, *, block):
    i = pl.program_id(0)
    f32, b16 = jnp.float32, jnp.bfloat16

    _, zs, _, rows, cols = mine_ref.shape

    def projection_copies():
        z0, y0, c0 = at_ref[0], at_ref[1], at_ref[2]
        copies = []
        for c, src in enumerate((mine_ref, peer_ref)):
            for y in range(2):
                for z in range(zs):
                    owner = (lax.rem(z0 + z, zs) * 2 + lax.rem(y0 + y, 2)) * 2 + lax.rem(c0 + c, 2)
                    first = pl.multiple_of(owner * rows, rows)
                    for k in range(3):
                        there = wa_ref.at[pl.ds(first, rows), pl.ds(k * cols, cols)]
                        copies.append(pltpu.make_async_copy(src.at[y, z, 3 + k], there, wa_sem.at[len(copies)]))
        return copies

    @pl.when(i == 0)
    def _():
        copies = projection_copies()
        for copy in copies:
            copy.start()
        red_ref[...] = jnp.zeros_like(red_ref)
        gb_ref[...] = jnp.zeros_like(gb_ref)
        for copy in copies:
            copy.wait()

    def body(per, chunks, wait):
        def weights(ref, c):
            return ref[c * per : c * per + per].reshape(-1, D)

        mixed = jnp.where(mask_ref[...] > 0.5, small_ref[8:9], x_ref[...].astype(f32))
        n1, inv1 = row_norm(mixed + dot(c_ref[...], wa_ref[...]) + small_ref[2:3])
        first = n1 * small_ref[3:4] + small_ref[4:5]
        low = first.astype(b16)
        low_ref[...] = low
        acc = None
        for c in range(chunks):
            wait(c)
            cols = slice(c * 768, c * 768 + 768)
            act, slo = gelu_both(dot(low, weights(wi_ref, c), NT) + b_ref[:, cols])
            act = act.astype(b16)
            act_ref[:, cols] = act
            slope_ref[:, cols] = slo.astype(b16)
            part = dot(act, weights(wo_ref, c))
            acc = part if acc is None else acc + part
        n2, inv2 = row_norm(first + (acc + small_ref[7:8]))
        out_ref[...] = n2 * small_ref[5:6] + small_ref[6:7]
        at = lax.broadcasted_iota(jnp.int32, (block, D), 0) + i * block
        cot = jnp.where(at < len_ref[0], cot_ref[...].astype(f32), 0.0)
        dres = row_norm_back(cot, n2, inv2, small_ref[5:6])
        dlow = dres.astype(b16)
        dlow_ref[...] = dlow
        for k, v in enumerate((cot * n2, cot, dlow.astype(f32))):
            red_ref[3 + k : 4 + k] += jnp.sum(v, axis=0, keepdims=True)
        acc = dres
        for c in range(chunks):
            cols = slice(c * 768, c * 768 + 768)
            dh = (dot(dlow, weights(wo_ref, c), NT) * slope_ref[:, cols].astype(f32)).astype(b16)
            dh_ref[:, cols] = dh
            gb_ref[:, cols] += jnp.sum(dh.astype(f32), axis=0, keepdims=True)
            acc = acc + dot(dh, weights(wi_ref, c))
        dr1 = row_norm_back(acc, n1, inv1, small_ref[3:4])
        da = dr1.astype(b16)
        dr1_ref[...] = dr1
        da_ref[...] = da
        dc_ref[...] = (dot(da, wa_ref[...], NT) * rl_ref[...]).astype(b16)
        for k, v in enumerate((da.astype(f32), acc * n1, acc)):
            red_ref[k : k + 1] += jnp.sum(v, axis=0, keepdims=True)

    by_step(w_ref, wi_ref, wo_ref, sem, body)


def middle(length, at, ctx, mine, peer, rounded, mask, w_all, bias, cot, rl, small, block=256):
    seq = ctx.shape[0]
    wide = pl.BlockSpec((block, D), lambda i, n, a: (i, 0))
    hidden = pl.BlockSpec((block, FF), lambda i, n, a: (i, 0))
    one = pl.BlockSpec((1, FF), lambda i, n, a: (0, 0))
    hbm = pl.BlockSpec(memory_space=pl.ANY)
    zs = mine.shape[1]
    f32, b16 = jnp.float32, jnp.bfloat16

    def shape(cols, kind, rows=seq):
        return jax.ShapeDtypeStruct((rows, cols), kind)

    return pl.pallas_call(
        functools.partial(middle_kernel, block=block),
        grid_spec=pltpu.PrefetchScalarGridSpec(
            num_scalar_prefetch=2,
            grid=(seq // block,),
            in_specs=[wide, hbm, hbm, wide, pl.BlockSpec((block, 1), lambda i, n, a: (i, 0)),
                      pl.BlockSpec(memory_space=pl.ANY), one, wide, wide, pl.BlockSpec((9, D), lambda i, n, a: (0, 0))],
            out_specs=[wide, hidden, hidden, wide, wide, wide, wide, wide, one, pl.BlockSpec((8, D), lambda i, n, a: (0, 0))],
            scratch_shapes=ffn_scratch(w_all, block)
            + [pltpu.VMEM((D, D), b16), pltpu.SemaphoreType.DMA((12 * zs,))],
        ),
        out_shape=[shape(D, b16), shape(FF, b16), shape(FF, b16), shape(D, b16), shape(D, f32), shape(D, f32),
                   shape(D, b16), shape(D, b16), shape(FF, f32, 1), shape(D, f32, 8)],
        compiler_params=pltpu.CompilerParams(vmem_limit_bytes=VMEM),
        cost_estimate=cost(40),
    )(length, at, ctx, mine, peer, rounded, mask, w_all, bias, cot, rl, small)


def input_kernel(dr_ref, d0_ref, d1_ref, d2_ref, w0_ref, w1_ref, w2_ref, z_ref, wg_ref, mask_ref,
                 fg_ref, red_ref):
    i = pl.program_id(0)
    acc = dr_ref[...] + dot(z_ref[...], wg_ref[...], TN)
    qs, vs = [], []
    for d_ref, w_ref in ((d0_ref, w0_ref), (d1_ref, w1_ref), (d2_ref, w2_ref)):
        for k in range(3):
            acc += dot(d_ref[k], w_ref[k], NT)
        qs.append(jnp.sum(d_ref[0].astype(jnp.float32), axis=0, keepdims=True))
        vs.append(jnp.sum(d_ref[2].astype(jnp.float32), axis=0, keepdims=True))
    masked = mask_ref[...] > 0.5
    fg_ref[...] = jnp.where(masked, 0.0, acc)
    dm = jnp.sum(jnp.where(masked, acc, 0.0), axis=0, keepdims=True)
    red = jnp.concatenate(
        [jnp.concatenate(qs, axis=1), jnp.concatenate(vs, axis=1), dm, jnp.zeros((5, D), jnp.float32)], axis=0
    )

    @pl.when(i == 0)
    def _():
        red_ref[...] = red

    @pl.when(i > 0)
    def _():
        red_ref[...] += red


def input_grad(dr1, ds, ws, dz, wg, mask, block=256):
    seq = dr1.shape[0]
    wide = pl.BlockSpec((block, D), lambda i: (i, 0))
    part = pl.BlockSpec((3, block, 256), lambda i: (0, i, 0))
    wpart = pl.BlockSpec((3, D, 256), lambda i: (0, 0, 0))
    return pl.pallas_call(
        input_kernel,
        grid=(seq // block,),
        in_specs=[wide, part, part, part, wpart, wpart, wpart,
                  pl.BlockSpec((dz.shape[0], block), lambda i: (0, i)),
                  pl.BlockSpec(wg.shape, lambda i: (0, 0)),
                  pl.BlockSpec((block, 1), lambda i: (i, 0))],
        out_specs=[wide, pl.BlockSpec((8, D), lambda i: (0, 0))],
        out_shape=[jax.ShapeDtypeStruct((seq, D), jnp.float32), jax.ShapeDtypeStruct((8, D), jnp.float32)],
        compiler_params=pltpu.CompilerParams(vmem_limit_bytes=VMEM),
        cost_estimate=cost(8),
    )(dr1, *ds, *ws, dz, wg, mask)


def split3(x):
    hi = x.astype(jnp.bfloat16)
    rest = x - hi.astype(jnp.float32)
    mid = rest.astype(jnp.bfloat16)
    low = (rest - mid.astype(jnp.float32)).astype(jnp.bfloat16)
    return hi, mid, low


def tree_sum(parts):
    while len(parts) > 1:
        half = len(parts) // 2
        parts = [parts[i] + parts[i + half] for i in range(half)]
    return parts[0]


def added(parts):
    return sum(p.astype(jnp.float32) for p in parts)


class Net:
    def __init__(self, dp_size, t_size):
        self.t = t_size
        self.sizes = {"z": dp_size // 4, "y": 2, "c": 2, "x": t_size}
        d = lax.axis_index("dp")
        self.at = {"z": d // 4, "y": d // 2 % 2, "c": d % 2, "x": lax.axis_index("tensor")}

    def shift(self, v, axis, k, swap=False):
        pairs = []
        sz = self.sizes
        for z in range(sz["z"]):
            for y in range(2):
                for c in range(2):
                    for x in range(sz["x"]):
                        src = {"z": z, "y": y, "c": c, "x": x}
                        dst = dict(src)
                        for one in axis:
                            dst[one] = src[one] ^ k if swap else (src[one] - k) % sz[one]
                        flat = [((q["z"] * 2 + q["y"]) * 2 + q["c"]) * sz["x"] + q["x"] for q in (src, dst)]
                        pairs.append(tuple(flat))
        return lax.ppermute(v, ("dp", "tensor"), pairs)

    def gather(self, v, axis, dim):
        return jnp.concatenate([v] + [self.shift(v, axis, k) for k in range(1, self.sizes[axis])], axis=dim)

    def scatter(self, parts, axis, dim):
        n = self.sizes[axis]
        at = self.at[axis]

        def slot(i):
            return [lax.dynamic_index_in_dim(p, i, dim, False) for p in parts]

        arrived = []
        for k in range(1, n):
            send = added(slot((at + k) % n)).astype(jnp.bfloat16)
            arrived.append(self.shift(send, axis, n - k))
        return slot(at), arrived

    def gather_own(self, v, axis, dim):
        n = self.sizes[axis]
        at = self.at[axis]
        out = jnp.zeros(v.shape[:dim] + (n,) + v.shape[dim:], v.dtype)
        for k in range(n):
            part = v if k == 0 else self.shift(v, axis, k)
            out = lax.dynamic_update_index_in_dim(out, part, (at + k) % n, dim)
        return out

    def total(self, v, axes=("c", "x", "y", "z")):
        if self.t == 2:
            v = v + self.shift(v, "c", 1, True)
            near = [self.shift(v, axis, 1, True) for axis in ("x", "y", "xy")]
            v = (v + near[0]) + (near[1] + near[2])
            axes = ("z",)
        for axis in axes:
            bit = 1
            while bit < self.sizes[axis]:
                v = v + self.shift(v, axis, bit, True)
                bit *= 2
        return v


def rolled(net, v, dims, sign):
    for dim, axis in dims:
        v = jnp.roll(v, sign * net.at[axis], dim)
    return v


def wide_rows(net, places, mine, peer):
    if mine.shape[3] % 16 == 0:
        return places, mine, peer
    zs, kinds, cols = net.sizes["z"], mine.shape[2], mine.shape[4]
    v = rolled(net, jnp.stack([mine, peer]), ((0, "c"), (1, "y"), (2, "z")), 1)
    v = v.transpose(2, 1, 0, 4, 3, 5)
    v = v.reshape(1, 2, 2, -1, kinds, cols).transpose(2, 1, 0, 4, 3, 5)
    return places * 0, v[0], v[1]


def local(dp_size, t_size, features, lengths, span_starts, buckets, cotangent,
          qkv_w, qkv_m, qkv_v, out_w, out_m, out_v, ffn_in, ffn_in_m, ffn_in_v,
          ffn_out, ffn_out_m, ffn_out_v, small_params, small_m, small_v,
          pos_table, pos_m, pos_v, gate_proj, gate_m, gate_v, step_count):
    f32, b16 = jnp.float32, jnp.bfloat16
    net = Net(dp_size, t_size)
    zs = net.sizes["z"]
    seq = features.shape[1]
    own = ffn_out.shape[0]
    rows = qkv_w.shape[1]
    scale = HD**-0.5

    bar = lax.optimization_barrier
    places = jnp.stack([net.at["z"], net.at["y"], net.at["c"], net.at["x"]]).astype(jnp.int32)
    cols = D // GROUPS
    group_heads = H // GROUPS
    both = ("dp", "tensor")

    qkv_low = qkv_w[None, None]
    u0, u1, u2 = [qkv_low[..., g * cols : (g + 1) * cols].astype(b16) for g in range(3)]
    z0 = net.gather(u0, "z", 1)
    rev = jnp.flip(buckets)
    order = jnp.concatenate([rev[127:], jnp.full((1,), -1, jnp.int32), rev[:127]])
    onehot = (jnp.arange(NB, dtype=jnp.int32)[:, None] == order[None, :]).astype(b16)
    off3 = dot(jnp.concatenate(split3(pos_table[:NB].T), axis=0), onehot).reshape(3, H, 2 * seq)
    table = bias_tables(off3[0] + off3[1] + off3[2])
    bias_row = jnp.pad(ffn_in[D:].astype(b16), ((0, 7), (0, D - own)))
    ffn_own = jnp.concatenate([ffn_in[:D].T.astype(b16), ffn_out.astype(b16), bias_row])
    z0, u1, table, features, ffn_own, out_w, gate_proj = bar((z0, u1, table, features, ffn_own, out_w, gate_proj))

    w_all = lax.all_gather(ffn_own, both, axis=0)
    w_all_k = w_all
    if own % 16:
        w_all_k = jnp.concatenate(
            [w_all[:, k * own : (k + 1) * own].reshape(4, -1, D) for k in range(2)] + [jnp.zeros((4, 8, D), b16)], axis=1)

    y0 = net.gather(z0, "y", 0)
    z1 = net.gather(u1, "z", 1)
    positions = jnp.arange(seq, dtype=jnp.int32)
    starts = span_starts[0]
    masked = jnp.any((positions[:, None] >= starts[None, :]) & (positions[:, None] < starts[None, :] + SPAN), axis=1)[:, None]
    mask = masked.astype(f32)
    rounded = jnp.where(masked, small_params[8][None, :].astype(b16), features[0])
    ga = jnp.sum(gate_proj[:HD, :4], axis=1)
    gb = jnp.sum(gate_proj[:HD, 4:], axis=1)
    za = jnp.sum(gate_proj[HD, :4])
    zb = jnp.sum(gate_proj[HD, 4:])
    eye = jnp.eye(H, dtype=f32)[:, :, None]
    wg = jnp.concatenate([(eye * ga).reshape(H, D), (eye * gb).reshape(H, D)], axis=0)
    wg3 = split3(wg)
    z3 = dot(jnp.concatenate(wg3, axis=0), rounded, NT).reshape(3, 2 * H, seq)
    z_all = z3[0] + z3[1] + z3[2]
    gate_a = jax.nn.sigmoid(z_all[:H] + za)
    gate_b = jax.nn.sigmoid(z_all[H:] + zb)
    const = pos_table[NB][:, None]
    gates = (gate_a * (gate_b * const - 1.0) + 2.0).reshape(H, 1, seq)
    rounded_t = rounded.T
    bias3 = jnp.stack([small_params[0], jnp.zeros((D,), f32), small_params[1]])[:, None, :]
    out_parts = out_w.astype(b16).reshape(rows, 3, cols).transpose(1, 0, 2)[None, None]
    u2 = jnp.concatenate([u2, out_parts], axis=2)
    y0, z1, u2, rounded, gates, rounded_t = bar((y0, z1, u2, rounded, gates, rounded_t))

    p0 = net.shift(y0, "c", 1)

    def attend(g, mine, peer, kept):
        at, mine, peer = wide_rows(net, places, mine, peer)
        bias = bias3[:, :, g * cols : (g + 1) * cols]
        return attn_fwd(lengths, at, rounded, mine, peer, bias, table, gates, g * group_heads, group_heads, kept)

    p0, z1, u2 = bar((p0, z1, u2))
    y1 = net.gather(z1, "y", 0)
    z2 = net.gather(u2, "z", 1)
    probs0, *kept, q0, w0 = attend(0, y0, p0, ())
    y1, z2, probs0, q0, w0, *kept = bar((y1, z2, probs0, q0, w0, *kept))
    p1 = net.shift(y1, "c", 1)
    y2 = net.gather(z2, "y", 0)
    probs1, *kept, q1, w1 = attend(1, y1, p1, kept)
    y2, probs1, q1, w1, *kept = bar((y2, probs1, q1, w1, *kept))
    p2 = net.shift(y2, "c", 1)
    probs2, context, context_f, inv_sum, q2, w2 = attend(2, y2, p2, kept)
    qkv, w_qkv, probs = (q0, q1, q2), (w0, w1, w2), (probs0, probs1, probs2)

    at2, mine2, peer2 = wide_rows(net, places, y2, p2)
    bias_in = w_all[:, 2 * own, :own].reshape(1, -1).astype(f32)
    low, act, d_hidden, d_branch, layer_out, d_res1, d_attention, d_context, g_bias_in, red = middle(
        lengths, at2, context, mine2, peer2, rounded, mask, w_all_k, bias_in, cotangent[0], inv_sum, small_params)

    def attend_back(g):
        return attn_bwd(qkv[g], d_context, context_f, probs[g], table, gates, g * group_heads, group_heads)

    def by_owner(v):
        return v.reshape(zs, 2, 2, rows, v.shape[-1])

    g_ffn = ffn_grads(d_hidden, act, low, d_branch, own)
    g_ffn, d_context = bar((g_ffn, d_context))
    g_ffn = lax.psum_scatter(g_ffn.reshape(dp_size, t_size, 2 * own, D), "dp", scatter_dimension=0, tiled=False)
    d0, dg0, do0 = attend_back(0)
    m1 = by_owner(weight_grads(rounded_t, d0, context, d_attention))
    m1, d0, dg0, do0, d_context = bar((m1, d0, dg0, do0, d_context))
    stay_1, got_1 = net.scatter([m1], "c", 2)
    d1, dg1, do1 = attend_back(1)
    got_1, d1, dg1, do1, d_context = bar((got_1, d1, dg1, do1, d_context))
    stay_1, got_1 = net.scatter(stay_1 + got_1, "y", 1)
    d2, dg2, do2 = attend_back(2)
    got_1, d2, dg2, do2 = bar((got_1, d2, dg2, do2))
    m2 = by_owner(weight_grads(rounded_t, d1, d2, jnp.zeros((8, 128), f32)))
    m2, dg0, dg1, dg2, do0, do1, do2 = bar((m2, dg0, dg1, dg2, do0, do1, do2))
    stay_2, got_2 = net.scatter([m2], "c", 2)
    dgate = jnp.concatenate([dg0, dg1, dg2], axis=0).reshape(H, seq)
    d_a = dgate * (gate_b * const - 1.0) * gate_a * (1.0 - gate_a)
    d_b = dgate * gate_a * const * gate_b * (1.0 - gate_b)
    d_const = jnp.sum(dgate * gate_a * gate_b, axis=1, keepdims=True)
    dz = jnp.concatenate([d_a, d_b], axis=0)
    dz_hi = dz.astype(b16)
    dz_lo = (dz - dz_hi.astype(f32)).astype(b16)
    got_2, got_1, dz, dz_hi, dz_lo, d_const, d_res1 = bar((got_2, got_1, dz, dz_hi, dz_lo, d_const, d_res1))

    stay_2, got_2 = net.scatter(stay_2 + got_2, "y", 1)
    stay_1, got_1 = net.scatter(stay_1 + got_1, "z", 0)
    feature_grad, red0 = input_grad(
        d_res1, (d0, d1, d2), w_qkv, jnp.concatenate([dz_hi, dz_lo, dz_hi], axis=0),
        jnp.concatenate([wg3[0], wg3[0], wg3[1]], axis=0), mask)
    small_local = jnp.concatenate([red0[:2], red[:6], red0[2:3]], axis=0)
    got_2, got_1, feature_grad, small_local, do0, do1, do2, dz = bar(
        (got_2, got_1, feature_grad, small_local, do0, do1, do2, dz))
    stay_2, got_2 = net.scatter(stay_2 + got_2, "z", 0)
    m1 = added(stay_1 + got_1).astype(b16)
    m1 = tree_sum([m1.astype(f32)] + [net.shift(m1, "x", k).astype(f32) for k in range(1, t_size)])
    exact = lax.Precision.HIGHEST
    g_z2 = dot(jnp.concatenate([dz_hi, dz_lo], axis=0), rounded)
    of_head = jnp.arange(D)[None, :] // HD == jnp.arange(2 * H)[:, None] % H
    g_z = jnp.where(of_head, g_z2[: 2 * H] + g_z2[2 * H :], 0.0)
    kind = (jnp.arange(2 * H)[None, :] // H == jnp.arange(2)[:, None]).astype(f32)
    fold = (jnp.arange(D)[:, None] % HD == jnp.arange(HD)[None, :]).astype(f32)
    g_z = jnp.dot(jnp.dot(kind, g_z, precision=exact), fold, precision=exact)
    g_zb = jnp.dot(kind, jnp.sum(dz, axis=1, keepdims=True), precision=exact)
    doff = jnp.concatenate([do0, do1, do2], axis=0).reshape(H, 2 * seq)
    pos3 = dot(jnp.concatenate(split3(doff), axis=0), onehot, NT)
    pos_t = jnp.concatenate([pos3[:H] + pos3[H : 2 * H] + pos3[2 * H :], d_const], axis=1)

    wide = 384
    packed = jnp.concatenate(
        [small_local[:, :wide], small_local[:, wide:]]
        + [g_bias_in[:, k * wide : (k + 1) * wide] for k in range(FF // wide)]
        + [jnp.pad(pos_t, ((0, 0), (0, wide - NB - 1))),
           jnp.pad(jnp.concatenate([g_z, g_zb], axis=1), ((0, 0), (0, wide - HD - 1)))], axis=0)
    got_2, m1, packed, g_ffn = bar((got_2, m1, packed, g_ffn))
    m2 = added(stay_2 + got_2).astype(b16)
    m2 = tree_sum([m2.astype(f32)] + [net.shift(m2, "x", k).astype(f32) for k in range(1, t_size)])
    stay_f, got_f = net.scatter([g_ffn], "x", 0)
    g_ffn = added(stay_f + got_f)
    own_ffn = jnp.sum(jnp.square(g_ffn)) + jnp.sum(jnp.square(m1)) * (1.0 / t_size)
    g_in_t = g_ffn[:own].T
    g_outw = g_ffn[own:]
    own_sum = jnp.sum(jnp.square(m2)) * (1.0 / t_size) + own_ffn
    used = packed.shape[0]
    flat = jnp.concatenate([packed, jnp.full((48 - used, wide), own_sum)], axis=0)
    flat = net.total(flat)
    own_sum = flat[used, 0]
    flat = flat[:used]
    shared = jnp.sum(jnp.square(flat)) + 3.0 * jnp.sum(jnp.square(flat[38:40]))
    m1 = m1.reshape(rows, 2, 3, cols)
    m2 = m2.reshape(rows, 2, 3, cols)
    g_qkv = jnp.stack([m1[:, 0], m2[:, 0], m2[:, 1]], axis=2).transpose(1, 0, 2, 3).reshape(3, rows, D)
    g_out = m1[:, 1].reshape(rows, D)
    g_small = jnp.concatenate([flat[:9], flat[9:18]], axis=1)
    g_bias = flat[18:26].reshape(-1, own)
    g_pos = flat[26:38, : NB + 1].T
    g_gate = jnp.repeat(flat[38:40, : HD + 1].T, 4, axis=1)
    grad_norm = jnp.sqrt(own_sum + shared)
    clip = jnp.minimum(1.0, CLIP_NORM / (grad_norm + 1e-06))
    count = step_count[0].astype(f32)
    me = lax.axis_index("dp") * t_size + lax.axis_index("tensor")
    g_bias = lax.dynamic_slice_in_dim(g_bias.reshape(-1, own), me, 1, 0)
    g_ffn_in = jnp.concatenate([g_in_t, g_bias], axis=0)

    qkv_new, qkv_moment, qkv_second = adam_step(qkv_w, g_qkv, qkv_m, qkv_v, clip, 2.0 * D**-0.5, count)
    out_new, out_moment, out_second = adam_step(out_w, g_out, out_m, out_v, clip, 1.0, count)
    in_new, in_moment, in_second = adam_step(ffn_in, g_ffn_in, ffn_in_m, ffn_in_v, clip, 2.0 * D**-0.5, count)
    fo_new, fo_moment, fo_second = adam_step(ffn_out, g_outw, ffn_out_m, ffn_out_v, clip, 2.0 * FF**-0.5, count)
    small_new, small_moment, small_second = adam_step(small_params, g_small, small_m, small_v, clip, 0.5, count)
    pos_new, pos_moment, pos_second = adam_step(pos_table, g_pos, pos_m, pos_v, clip, 1.0, count)
    gate_new, gate_moment, gate_second = adam_step(gate_proj, g_gate, gate_m, gate_v, clip, 2.0 * HD**-0.5, count)
    return (
        layer_out[None], feature_grad[None], grad_norm.reshape(1),
        qkv_new, qkv_moment, qkv_second, qkv_new.astype(b16),
        out_new, out_moment, out_second, out_new.astype(b16),
        in_new, in_moment, in_second, in_new.astype(b16),
        fo_new, fo_moment, fo_second, fo_new.astype(b16),
        g_small, small_new, small_moment, small_second,
        pos_new, pos_moment, pos_second, gate_new, gate_moment, gate_second,
    )


def solution(mesh):
    both = ("dp", "tensor")
    three = (P(None, "dp", None),)
    row = (P("dp", None),)
    col = (P(None, both),)
    rows2 = (P(both, None),)
    utt = P(both, None, None)
    in_specs = (
        (utt, P(both), P(both, None), P(), utt) + three * 3 + row * 3 + col * 3 + rows2 * 3 + (P(),) * 10
    )
    out_specs = (utt, utt, P()) + three * 4 + row * 4 + col * 4 + rows2 * 4 + (P(),) * 10
    fn = functools.partial(local, mesh.shape["dp"], mesh.shape["tensor"])
    return jax.shard_map(fn, mesh=mesh, in_specs=in_specs, out_specs=out_specs, check_vma=False)
```
